32 devices in a mesh: section: 2 (over y), dp: 4 (over x, core), tensor: 4 (over z).
Axes of the slice: x: 2, y: 2, z: 4, core: 2. Of those that a mesh axis runs over, the one named last changes fastest.
Arguments:
- inputs: bfloat16 [2, 4, 4096, 1024], P('section', None, ('dp', 'tensor')), may hold values from -6 to 6
- lengths: int32 [2, 4, 4], P(None, None, 'dp'), may hold values from 1 to 1024, 2560 in all within a row
- cotangent: bfloat16 [4, 4096, 1024], P(None, ('dp', 'tensor')), may hold values from -6 to 6
- qkv_weight: bfloat16 [2, 1024, 3072], P('section', None, 'tensor'), may hold values from -0.25 to 0.25
- attn_out_weight: bfloat16 [2, 1024, 1024], P('section', 'tensor'), may hold values from -1.5 to 1.5
- cross_weight: bfloat16 [2, 1024, 2048], P('section', None, 'tensor'), may hold values from -1.5 to 1.5
- ffn_in_weight: bfloat16 [2, 1024, 4096], P('section', None, 'tensor'), may hold values from -0.1875 to 0.1875
- ffn_in_bias: bfloat16 [2, 4096], P('section', 'tensor'), may hold values from -3 to 3
- ffn_out_weight: bfloat16 [2, 4096, 1024], P('section', 'tensor'), may hold values from -0.375 to 0.375
- ffn_out_bias: bfloat16 [2, 1024], P('section'), may hold values from -3 to 3
- norm_gain: bfloat16 [2, 3, 1024], P('section'), may hold values from 0.5 to 1.5
- norm_bias: bfloat16 [2, 3, 1024], P('section'), may hold values from -2 to 2
Outputs:
- outputs: bfloat16 [2, 4, 4096, 1024], P('section', None, ('dp', 'tensor'))
- input_grad: float32 [2, 4, 4096, 1024], P('section', None, ('dp', 'tensor'))
- qkv_grad: float32 [2, 1024, 3072], P('section', None, 'tensor')
- attn_out_grad: float32 [2, 1024, 1024], P('section', 'tensor')
- cross_grad: float32 [2, 1024, 2048], P('section', None, 'tensor')
- ffn_in_grad: float32 [2, 1024, 4096], P('section', None, 'tensor')
- ffn_in_bias_grad: float32 [2, 4096], P('section', 'tensor')
- ffn_out_grad: float32 [2, 4096, 1024], P('section', 'tensor')
- ffn_out_bias_grad: float32 [2, 1024], P('section')
- norm_gain_grad: float32 [2, 3, 1024], P('section')
- norm_bias_grad: float32 [2, 3, 1024], P('section')
The draws below stay inside these ranges and needn't reach their ends.
Inputs may be any that keep to these rules, and one draw needn't show every extreme that they name: In each micro-batch and for each index of the first dimension the 4 lengths add up to 2560, and the longest is 1024.
All inputs are finite; a program needn't handle non-finite values. No bound on the sum of `lengths` on one device may be relied on, other than what follows from the above.
Results may differ from the reference program's by a relative error of at most 0.03.
Values may be sent and summed in bfloat16 or wider, within the bound.
A program may use at most 640 MiB of HBM per device.

```python
import math
import jax
import jax.numpy as jnp
import numpy as np
from jax import lax

D = 1024
HEADS = 16
HS = 64
FF = 4096
SLOT = 1024
MB = 4
SEQS_MB = 4
TOKENS_MB = 4096


def draw_cross_weight(key, part):
    normal_draw = jnp.clip(jax.random.normal(key, (2, D, 2 * D), jnp.float32), -6.0, 6.0)
    column_index = lax.broadcasted_iota(jnp.int32, (2, D, 2 * D), 2)
    layer_index = lax.broadcasted_iota(jnp.int32, (2, D, 2 * D), 0)
    output_part = (column_index // HS % 2 == 1) & (layer_index == 1)
    col_scale = jnp.where(output_part, 0.25, (2.0 / D) ** 0.5)
    return (normal_draw * col_scale).astype(jnp.bfloat16)


def block_scale(stream_key, dims, cuts, low, high):
    loudness, own = 1.0, jax.random.fold_in(stream_key, 6)
    for position, shards_of in cuts:
        heights = jnp.exp(jax.random.uniform(jax.random.fold_in(own, position), (shards_of,), jnp.float32, low / len(cuts), high / len(cuts)))
        loudness = loudness * jnp.repeat(heights, dims[position] // shards_of).reshape([-1 if axis == position else 1 for axis in range(len(dims))])
    return loudness


def split_up(number_of, total, bound, slope):
    loads = [(1 << 20) // math.isqrt(rank ** slope) + 1 for rank in range(2, number_of + 1)]
    surplus, counts = total - bound - (number_of - 1), [1] * (number_of - 1)
    while surplus > 0:
        movable = [i for i in range(number_of - 1) if counts[i] < bound]
        mass, left = sum([loads[i] for i in movable]), surplus
        for i in movable:
            extra = min(bound - counts[i], max(1, left * loads[i] // mass), surplus)
            counts[i] = counts[i] + extra
            surplus = surplus - extra
    return np.array([bound] + counts)


def uneven(rng, amount, total, bound, skew):
    if amount == 2:
        one = jax.random.randint(rng, (), max(1, total - bound), min(bound, total - 1) + 1)
        return jnp.stack([one, total - one])
    sizes = jnp.asarray(split_up(amount, total, bound, skew), jnp.int32)
    twos = (amount - 1) // 2
    donor, receiver = sizes[1:1 + 2 * twos:2], sizes[2:2 + 2 * twos:2]
    room = jnp.minimum(donor - 1, bound - receiver)
    passed = jax.random.randint(jax.random.fold_in(rng, 1), (twos,), 0, 1 << 20) % (room + 1)
    sizes = sizes.at[1:1 + 2 * twos:2].set(donor - passed).at[2:2 + 2 * twos:2].set(receiver + passed)
    return sizes[jax.random.permutation(jax.random.fold_in(rng, 2), amount)]


def gaussian(own_key, dims, width, most, cuts=(), held_as=jnp.bfloat16):
    gain = block_scale(own_key, dims, cuts, -0.22, 0.18) if cuts else 1.0
    result = jax.random.normal(own_key, dims, jnp.float32) * width * gain
    return jnp.minimum(jnp.maximum(result, -most), most).astype(held_as)


def setup_inputs(seed: int = 0) -> dict:
    arg_keys = jax.random.split(jax.random.key(seed), 13)
    return {
        "inputs": gaussian(arg_keys[0], (2, MB, TOKENS_MB, D), 1.0, 6.0, ((0, 2), (2, 16))),
        "lengths": jax.vmap(lambda own: uneven(own, SEQS_MB, 5 * SEQS_MB * SLOT // 8, SLOT, 2))(jax.random.split(arg_keys[1], 2 * MB)).reshape((2, MB, SEQS_MB)).astype(jnp.int32),
        "cotangent": gaussian(arg_keys[2], (MB, TOKENS_MB, D), 1.0, 6.0, ((1, 16),)),
        "qkv_weight": gaussian(arg_keys[3], (2, D, 3 * D), (D // 2) ** -0.5, 0.25, ((0, 2), (2, 4))),
        "attn_out_weight": gaussian(arg_keys[4], (2, D, D), 16 ** -0.5, 1.5, ((0, 2), (1, 4))),
        "cross_weight": draw_cross_weight(jax.random.fold_in(arg_keys[12], 71), 0),
        "ffn_in_weight": gaussian(arg_keys[6], (2, D, FF), D ** -0.5, 0.1875, ((0, 2), (2, 4))),
        "ffn_in_bias": gaussian(arg_keys[7], (2, FF), 0.5, 3.0, ((0, 2), (1, 4))),
        "ffn_out_weight": gaussian(arg_keys[8], (2, FF, D), (FF // 16) ** -0.5, 0.375, ((0, 2), (1, 4))),
        "ffn_out_bias": gaussian(arg_keys[9], (2, D), 0.5, 3.0, ((0, 2),)),
        "norm_gain": jnp.clip(1.0 + 0.1 * jax.random.normal(arg_keys[10], (2, 3, D), jnp.float32), 0.5, 1.5).astype(jnp.bfloat16),
        "norm_bias": gaussian(arg_keys[11], (2, 3, D), 0.3, 2.0, ((0, 2),)),
    }


ALPHA_ENC = 0.81 * (100.0 ** 5) ** (1.0 / 16.0)
ALPHA_DEC = (3.0 * 100.0) ** 0.25
EPS = 1e-05
NEG = -1e+30
HIGH = lax.Precision.HIGHEST

@jax.custom_vjp
def low(v):
    return lax.optimization_barrier(v.astype(jnp.bfloat16)).astype(jnp.float32)

@jax.custom_vjp
def low_back(v):
    return v

def low_keep(v):
    return (low(v), None)

def low_pass(kept, grad):
    return (grad,)

def back_keep(v):
    return (v, None)

def back_low(kept, grad):
    return (low(grad),)
low.defvjp(low_keep, low_pass)
low_back.defvjp(back_keep, back_low)

def matmul(left, right):
    return jnp.dot(left, right, precision=HIGH)

def layer_norm(values, gain_row, shift_row):
    centered = values - lax.optimization_barrier(jnp.mean(values, axis=-1, keepdims=True))
    return centered * lax.rsqrt(lax.optimization_barrier(jnp.mean(centered * centered, axis=-1, keepdims=True)) + EPS) * gain_row + shift_row

def attention(queries, keys_in, values, allowed):
    scaled = low_back(jnp.einsum('qhe,khe->hqk', queries, keys_in, precision=HIGH)) * HS ** (-0.5)
    scores = jnp.where(allowed[None], scaled, NEG)
    row_max = lax.optimization_barrier(jnp.max(scores, axis=-1, keepdims=True))
    expo_vals = jnp.exp(scores - row_max)
    probs = expo_vals / lax.optimization_barrier(jnp.sum(expo_vals, axis=-1, keepdims=True))
    mixed = jnp.einsum('hqk,khe->qhe', low(probs), values, precision=HIGH)
    return low(low_back(mixed)).reshape(SLOT, D)

def self_block(rows, qkv_mat, out_mat, allowed, alpha, gain_row, shift_row):
    qkv = low(low_back(matmul(rows, qkv_mat))).reshape(SLOT, HEADS, 3, HS)
    mixed = attention(qkv[:, :, 0], qkv[:, :, 1], qkv[:, :, 2], allowed)
    return layer_norm(alpha * rows + low_back(matmul(mixed, out_mat)), gain_row, shift_row)

def feed_block(rows, in_mat, in_shift, down_mat, down_shift, alpha, gain_row, shift_row):
    pre_act = low_back(matmul(low(rows), in_mat) + in_shift)
    hidden = low(jax.nn.gelu(pre_act))
    return layer_norm(alpha * rows + low_back(matmul(hidden, down_mat)) + down_shift, gain_row, shift_row)

def seq_pair(source_rows, target_rows, source_len, target_len, params):
    qkv_w, out_w, cross_w, in_w, in_b, down_w, down_b, gains, shifts = params
    key_pos = lax.broadcasted_iota(jnp.int32, (SLOT, SLOT), 1)
    query_pos = lax.broadcasted_iota(jnp.int32, (SLOT, SLOT), 0)
    source_ok = key_pos < source_len
    target_ok = (key_pos < target_len) & (key_pos <= query_pos)
    enc_a = self_block(source_rows, qkv_w[0], out_w[0], source_ok, ALPHA_ENC, gains[0, 0], shifts[0, 0])
    memory = feed_block(enc_a, in_w[0], in_b[0], down_w[0], down_b[0], ALPHA_ENC, gains[0, 2], shifts[0, 2])
    key_value = low(low_back(matmul(low(memory), cross_w[0]))).reshape(SLOT, HEADS, 2, HS)
    dec_a = self_block(target_rows, qkv_w[1], out_w[1], target_ok, ALPHA_DEC, gains[1, 0], shifts[1, 0])
    cross_dec = cross_w[1].reshape(D, HEADS, 2, HS)
    query_mat = cross_dec[:, :, 0].reshape(D, D)
    outer_mat = cross_dec[:, :, 1].reshape(D, D)
    queries = low(low_back(matmul(low(dec_a), query_mat))).reshape(SLOT, HEADS, HS)
    cross_mix = attention(queries, key_value[:, :, 0], key_value[:, :, 1], source_ok)
    crossed = low_back(matmul(cross_mix, outer_mat.T))
    dec_c = layer_norm(ALPHA_DEC * dec_a + crossed, gains[1, 1], shifts[1, 1])
    decoded = feed_block(dec_c, in_w[1], in_b[1], down_w[1], down_b[1], ALPHA_DEC, gains[1, 2], shifts[1, 2])
    return (memory, decoded)

def reference(inputs, lengths, cotangent, qkv_weight, attn_out_weight, cross_weight, ffn_in_weight, ffn_in_bias, ffn_out_weight, ffn_out_bias, norm_gain, norm_bias):
    seq_total = MB * SEQS_MB
    params = tuple((array.astype(jnp.float32) for array in (qkv_weight, attn_out_weight, cross_weight, ffn_in_weight, ffn_in_bias, ffn_out_weight, ffn_out_bias, norm_gain, norm_bias)))
    source = inputs[0].astype(jnp.float32).reshape(seq_total, SLOT, D)
    target = inputs[1].astype(jnp.float32).reshape(seq_total, SLOT, D)
    source_len = lengths[0].reshape(seq_total).astype(jnp.int32)
    target_len = lengths[1].reshape(seq_total).astype(jnp.int32)

    def forward(source_rows, target_rows, weights):

        def advance(state_carry, seq_item):
            return (state_carry, jax.checkpoint(seq_pair)(seq_item[0], seq_item[1], seq_item[2], seq_item[3], weights))
        return lax.scan(advance, jnp.zeros((), jnp.float32), (source_rows, target_rows, source_len, target_len))[1]
    (memory, decoded), pullback = jax.vjp(forward, source, target, params)
    slot_pos = lax.broadcasted_iota(jnp.int32, (seq_total, SLOT, 1), 1)
    grad_top = jnp.where(slot_pos < target_len[:, None, None], cotangent.astype(jnp.float32).reshape(seq_total, SLOT, D), 0.0)
    grad_source, grad_target, grad_params = pullback((jnp.zeros_like(memory), grad_top))
    outputs = jnp.stack([memory.reshape(MB, TOKENS_MB, D), decoded.reshape(MB, TOKENS_MB, D)]).astype(jnp.bfloat16)
    input_grad = jnp.stack([grad_source.reshape(MB, TOKENS_MB, D), grad_target.reshape(MB, TOKENS_MB, D)])
    return (outputs, input_grad, grad_params[0], grad_params[1], grad_params[2], grad_params[3], grad_params[4], grad_params[5], grad_params[6], grad_params[7], grad_params[8])
```

```python
import jax
import jax.numpy as jnp
from jax import lax
from jax.experimental import pallas as pl
from jax.experimental.pallas import tpu as pltpu
from jax.sharding import PartitionSpec as P

HS = 64
QBLOCK = 512


ALPHA_ENC = 0.81 * (100.0**5) ** (1.0 / 16.0)
ALPHA_DEC = (3.0 * 100.0) ** 0.25
EPS = 1e-05
NEG = -1e30
ROW_DIMS = (((0,), (0,)), ((), ()))
COL_DIMS = (((1,), (1,)), ((), ()))
LANES = 2 * HS
ROWS = 256
SCALE = HS ** (-0.5)
GELU_C = (2.0 / 3.141592653589793) ** 0.5


def from_behind(block, axis, distance):
    devices = range(lax.axis_size(axis))
    route = [(i - distance, i) for i in devices if i - distance in devices]
    return lax.ppermute(block, axis, route)


def layer_norm(values, gain_row, shift_row):
    centered = values - jnp.mean(values, axis=-1, keepdims=True)
    factor = lax.rsqrt(jnp.mean(centered * centered, axis=-1, keepdims=True) + EPS)
    normed = centered * factor
    return (normed * gain_row + shift_row, normed, factor)


def norm_back(gradient, normed, factor, gain_row):
    scaled = gradient * gain_row
    centred = (
        scaled
        - jnp.mean(scaled, axis=-1, keepdims=True)
        - normed * jnp.mean(scaled * normed, axis=-1, keepdims=True)
    )
    return (centred * factor, jnp.sum(gradient * normed, axis=0), jnp.sum(gradient, axis=0))


def visible(first_row, row_count, key_count, seq_lengths, causal):
    key_pos = lax.broadcasted_iota(jnp.int32, (1, row_count, key_count), 2)
    query_pos = first_row + lax.broadcasted_iota(jnp.int32, (1, row_count, key_count), 1)
    inside = key_pos < seq_lengths[:, None, None]
    return inside & ((key_pos <= query_pos) | jnp.logical_not(causal))


def attend(queries, keys_in, values, seq_lengths, causal):
    key_count = queries.shape[1]
    score_scale = queries.shape[3] ** (-0.5)
    row_block = min(QBLOCK, key_count)
    mixed_parts, lse_parts = ([], [])
    for first_row in range(0, key_count, row_block):
        allowed = visible(first_row, row_block, key_count, seq_lengths, causal)
        raw_scores = jnp.einsum(
            "bqhe,bkhe->bhqk",
            queries[:, first_row : first_row + row_block],
            keys_in,
            preferred_element_type=jnp.float32,
        )
        scores = jnp.where(allowed[:, None], raw_scores * score_scale, NEG)
        row_max = jnp.max(scores, axis=-1, keepdims=True)
        expo_vals = jnp.exp(scores - row_max)
        row_total = jnp.sum(expo_vals, axis=-1, keepdims=True)
        weights = (expo_vals / row_total).astype(jnp.bfloat16)
        mixed_block = jnp.einsum(
            "bhqk,bkhe->bqhe", weights, values, preferred_element_type=jnp.float32
        )
        mixed_parts.append(mixed_block.astype(jnp.bfloat16))
        lse_parts.append(row_max + jnp.log(row_total))
    return (jnp.concatenate(mixed_parts, axis=1), jnp.concatenate(lse_parts, axis=2))


def attend_back(grad_mixed, queries, keys_in, values, log_totals, seq_lengths, causal):
    key_count = queries.shape[1]
    score_scale = queries.shape[3] ** (-0.5)
    row_block = min(QBLOCK, key_count)
    query_parts = []
    grad_keys = jnp.zeros(keys_in.shape, jnp.float32)
    grad_values = jnp.zeros(values.shape, jnp.float32)
    for first_row in range(0, key_count, row_block):
        query_part = queries[:, first_row : first_row + row_block]
        grad_part = grad_mixed[:, first_row : first_row + row_block]
        allowed = visible(first_row, row_block, key_count, seq_lengths, causal)
        raw_scores = jnp.einsum(
            "bqhe,bkhe->bhqk", query_part, keys_in, preferred_element_type=jnp.float32
        )
        scores = jnp.where(allowed[:, None], raw_scores * score_scale, NEG)
        probs = jnp.exp(scores - log_totals[:, :, first_row : first_row + row_block])
        grad_probs = jnp.einsum(
            "bqhe,bkhe->bhqk", grad_part, values, preferred_element_type=jnp.float32
        )
        grad_scores = probs * (grad_probs - jnp.sum(probs * grad_probs, axis=-1, keepdims=True))
        grad_raw = (grad_scores * score_scale).astype(jnp.bfloat16)
        query_parts.append(
            jnp.einsum("bhqk,bkhe->bqhe", grad_raw, keys_in, preferred_element_type=jnp.float32)
        )
        grad_keys = grad_keys + jnp.einsum(
            "bhqk,bqhe->bkhe", grad_raw, query_part, preferred_element_type=jnp.float32
        )
        grad_values = grad_values + jnp.einsum(
            "bhqk,bqhe->bkhe",
            probs.astype(jnp.bfloat16),
            grad_part,
            preferred_element_type=jnp.float32,
        )
    return (jnp.concatenate(query_parts, axis=1), grad_keys, grad_values)


def ffn_forward(rows_in, in_proj, in_shift, down_proj):
    pre_act = jnp.dot(rows_in, in_proj, preferred_element_type=jnp.float32) + in_shift
    hidden = jax.nn.gelu(pre_act).astype(jnp.bfloat16)
    return (pre_act, jnp.dot(hidden, down_proj, preferred_element_type=jnp.float32))


def ffn_backward(grad_in, rows_in, pre_act, in_proj, down_proj):
    activated, slope_back = jax.vjp(jax.nn.gelu, pre_act)
    hidden = activated.astype(jnp.bfloat16)
    grad_down = lax.dot_general(hidden, grad_in, ROW_DIMS, preferred_element_type=jnp.float32)
    grad_hidden = lax.dot_general(grad_in, down_proj, COL_DIMS, preferred_element_type=jnp.float32)
    grad_pre = slope_back(grad_hidden)[0].astype(jnp.bfloat16)
    grad_shift = jnp.sum(grad_pre.astype(jnp.float32), axis=0)
    grad_inner = lax.dot_general(rows_in, grad_pre, ROW_DIMS, preferred_element_type=jnp.float32)
    grad_rows_out = lax.dot_general(grad_pre, in_proj, COL_DIMS, preferred_element_type=jnp.float32)
    return (grad_rows_out, grad_inner, grad_shift, grad_down)


def gather_rows(shard):
    return lax.all_gather(shard, "tensor", axis=0, tiled=True)


def sum_rows(partial_value):
    return lax.psum_scatter(partial_value, "tensor", scatter_dimension=0, tiled=True)


def ffn_input_rows(shard):
    return lax.all_gather(shard, "tensor", axis=0, tiled=True)


def ffn_sum_rows(partial_value):
    return lax.psum_scatter(
        partial_value.astype(jnp.bfloat16), "tensor", scatter_dimension=0, tiled=True
    ).astype(jnp.float32)


def grad_rows(shard):
    return lax.all_gather(shard, "tensor", axis=0, tiled=True)


def grad_sums(partial_value):
    return lax.psum_scatter(
        partial_value.astype(jnp.bfloat16), "tensor", scatter_dimension=0, tiled=True
    ).astype(jnp.float32)


def ffn_grad_rows(shard):
    return lax.all_gather(shard, "tensor", axis=0, tiled=True)


def ffn_grad_sums(partial_value):
    return lax.psum_scatter(
        partial_value.astype(jnp.bfloat16), "tensor", scatter_dimension=0, tiled=True
    ).astype(jnp.float32)


def body(
    inputs,
    lengths,
    cotangent,
    qkv_weight,
    attn_out_weight,
    cross_weight,
    ffn_in_weight,
    ffn_in_bias,
    ffn_out_weight,
    ffn_out_bias,
    norm_gain,
    norm_bias,
):
    tensor_count = lax.axis_size("tensor")
    section = lax.axis_index("section")
    tensor_index = lax.axis_index("tensor")
    decoder = section == 1
    alpha = jnp.where(decoder, ALPHA_DEC, ALPHA_ENC).astype(jnp.float32)
    batches, shard_rows, width = (inputs.shape[1], inputs.shape[2], inputs.shape[3])
    seq_count = lengths.shape[2]
    full_rows = shard_rows * tensor_count
    slots = full_rows // seq_count
    qkv_proj = qkv_weight[0]
    head_local = qkv_proj.shape[1] // (3 * HS)
    head_cols = head_local * HS
    out_proj = attn_out_weight[0]
    cross_proj = cross_weight[0]
    cross_split = cross_proj.reshape(width, head_local, 2, HS)
    first_cols = cross_split[:, :, 0].reshape(width, head_cols)
    second_cols = cross_split[:, :, 1].reshape(width, head_cols)
    in_proj = ffn_in_weight[0]
    in_shift = ffn_in_bias[0].astype(jnp.float32)
    down_proj = ffn_out_weight[0]
    hidden_width = in_proj.shape[1]
    down_shift = ffn_out_bias[0].astype(jnp.float32)
    gains = norm_gain[0].astype(jnp.float32)
    shifts = norm_bias[0].astype(jnp.float32)
    own_lengths = lax.dynamic_index_in_dim(lengths, section, 0, keepdims=False)
    source_lengths = lengths[0]
    row_index = tensor_index * shard_rows + lax.iota(jnp.int32, shard_rows)
    row_seq = row_index // slots
    row_pos = row_index % slots
    seq_ids = lax.iota(jnp.int32, seq_count)
    lse_shape = (seq_count, head_local, slots, 1)

    def zeros_float(shape):
        return jnp.zeros(shape, jnp.float32)

    def zeros_low(shape):
        return jnp.zeros(shape, jnp.bfloat16)

    def to_heads(flat_rows):
        return flat_rows.reshape(seq_count, slots, flat_rows.shape[1] // HS, HS)

    def to_rows(split_rows):
        return split_rows.reshape(full_rows, -1)

    def cross_forward(query_rows, kv_source, source_len):
        kv_split = kv_source.reshape(seq_count, slots, head_local, 2, HS)
        query_c = jnp.dot(query_rows, first_cols, preferred_element_type=jnp.float32).astype(
            jnp.bfloat16
        )
        mixed_c, lse_cross = attend(
            to_heads(query_c), kv_split[:, :, :, 0], kv_split[:, :, :, 1], source_len, False
        )
        mixed_c = to_rows(mixed_c)
        partial_value = lax.dot_general(
            mixed_c, second_cols, COL_DIMS, preferred_element_type=jnp.float32
        )
        return (query_c, mixed_c, lse_cross, partial_value)

    kv_held = zeros_low((full_rows, 2 * head_cols))
    kv_ticks, kept_ticks, out_ticks = ([], [], [])
    for tick_index in range(batches + 1):
        batch = jnp.clip(tick_index - section, 0, batches - 1)
        x_shard = lax.dynamic_index_in_dim(inputs[0], batch, 0, keepdims=False)
        own_len = lax.dynamic_index_in_dim(own_lengths, batch, 0, keepdims=False)
        source_len = lax.dynamic_index_in_dim(source_lengths, batch, 0, keepdims=False)
        x_full = gather_rows(x_shard)
        qkv = jnp.dot(x_full, qkv_proj, preferred_element_type=jnp.float32).astype(jnp.bfloat16)
        qkv_split = qkv.reshape(seq_count, slots, head_local, 3, HS)
        mixed, lse_self = attend(
            qkv_split[:, :, :, 0], qkv_split[:, :, :, 1], qkv_split[:, :, :, 2], own_len, decoder
        )
        mixed = to_rows(mixed)
        attn_sum = sum_rows(jnp.dot(mixed, out_proj, preferred_element_type=jnp.float32))
        resid_a, norm_a, factor_a = layer_norm(
            alpha * x_shard.astype(jnp.float32) + attn_sum, gains[0], shifts[0]
        )
        a_shard = resid_a.astype(jnp.bfloat16)
        a_full = gather_rows(a_shard)

        def enc_second():
            hidden_made, partial_value = ffn_forward(a_full, in_proj, in_shift, down_proj)
            return (
                hidden_made,
                zeros_low((full_rows, head_cols)),
                zeros_low((full_rows, head_cols)),
                zeros_float(lse_shape),
                partial_value,
            )

        def dec_second():
            query_c, mixed_c, lse_cross, partial_value = cross_forward(a_full, kv_held, source_len)
            return (
                zeros_float((full_rows, hidden_width)),
                query_c,
                mixed_c,
                lse_cross,
                partial_value,
            )

        hidden_enc, query_c, mixed_c, lse_cross, partial_value = lax.cond(
            decoder, dec_second, enc_second
        )
        second_sum = sum_rows(partial_value)
        resid_ye, norm_ye, factor_ye = layer_norm(
            alpha * resid_a + second_sum + down_shift, gains[2], shifts[2]
        )
        resid_c, norm_c, factor_c = layer_norm(alpha * resid_a + second_sum, gains[1], shifts[1])
        wide_rows = ffn_input_rows(jnp.where(decoder, resid_c, resid_ye).astype(jnp.bfloat16))

        def enc_third():
            kv_made = jnp.dot(wide_rows, cross_proj, preferred_element_type=jnp.float32).astype(
                jnp.bfloat16
            )
            return (
                kv_made,
                zeros_float((full_rows, hidden_width)),
                zeros_float((full_rows, width)),
            )

        def dec_third():
            hidden_made, partial_made = ffn_forward(wide_rows, in_proj, in_shift, down_proj)
            return (zeros_low((full_rows, 2 * head_cols)), hidden_made, partial_made)

        kv_out, hidden_dec, partial_third = lax.cond(decoder, dec_third, enc_third)
        third_sum = ffn_sum_rows(partial_third)
        resid_yd, norm_yd, factor_yd = layer_norm(
            alpha * resid_c + third_sum + down_shift, gains[2], shifts[2]
        )
        resid_y = jnp.where(decoder, resid_yd, resid_ye)
        norm_y = jnp.where(decoder, norm_yd, norm_ye)
        factor_y = jnp.where(decoder, factor_yd, factor_ye)
        hidden = jnp.where(decoder, hidden_dec, hidden_enc)
        ffn_rows = jnp.where(decoder, wide_rows, a_full)
        y_shard = resid_y.astype(jnp.bfloat16)
        kv_held = from_behind(kv_out, "section", 1)
        kv_ticks.append(kv_held)
        out_ticks.append(y_shard)
        kept_ticks.append(
            dict(
                x_rows=x_full,
                qkv=qkv,
                mixed=mixed,
                lse_self=lse_self,
                a_rows=a_full,
                kv_rows=wide_rows,
                ffn_rows=ffn_rows,
                hidden=hidden,
                query_c=query_c,
                mixed_c=mixed_c,
                lse_cross=lse_cross,
                norm_a=norm_a,
                factor_a=factor_a,
                norm_c=norm_c,
                factor_c=factor_c,
                norm_y=norm_y,
                factor_y=factor_y,
            )
        )
    kept_all = jax.tree.map(lambda *leaves: jnp.stack(leaves), *kept_ticks)
    kv_stack = jnp.stack(kv_ticks)
    outputs = lax.dynamic_slice_in_dim(jnp.stack(out_ticks), section, batches, 0)
    totals = dict(
        qkv=zeros_float(qkv_proj.shape),
        outer=zeros_float(out_proj.shape),
        cross=zeros_float(cross_proj.shape),
        inner=zeros_float(in_proj.shape),
        inner_shift=zeros_float(in_shift.shape),
        down=zeros_float(down_proj.shape),
        down_shift=zeros_float(down_shift.shape),
        gain=zeros_float(gains.shape),
        shift=zeros_float(shifts.shape),
    )
    zero_ffn = (
        zeros_float(in_proj.shape),
        zeros_float(in_shift.shape),
        zeros_float(down_proj.shape),
    )
    zero_cross = zeros_float((width, 2 * head_cols))
    dkv_held = zeros_low((full_rows, 2 * head_cols))
    grad_ticks = []
    for tick_index in range(batches + 1):
        batch_raw = batches - tick_index - section
        live = (batch_raw >= 0) & (batch_raw < batches)
        batch = jnp.clip(batch_raw, 0, batches - 1)
        kept = jax.tree.map(
            lambda leaf_value: lax.dynamic_index_in_dim(
                leaf_value, batch + section, 0, keepdims=False
            ),
            kept_all,
        )
        own_len = lax.dynamic_index_in_dim(own_lengths, batch, 0, keepdims=False)
        source_len = lax.dynamic_index_in_dim(source_lengths, batch, 0, keepdims=False)
        kv_now = lax.dynamic_index_in_dim(kv_stack, batch, 0, keepdims=False)
        kv_split = kv_now.reshape(seq_count, slots, head_local, 2, HS)
        own_rows = jnp.sum(
            jnp.where(row_seq[:, None] == seq_ids[None, :], own_len[None, :], 0), axis=1
        )
        grad_top = lax.dynamic_index_in_dim(cotangent, batch, 0, keepdims=False).astype(jnp.float32)
        grad_top = jnp.where((row_pos < own_rows)[:, None], grad_top, 0.0)
        grad_r3d, gain_yd, shift_yd = norm_back(
            grad_top, kept["norm_y"], kept["factor_y"], gains[2]
        )
        dkv_now = dkv_held

        def kv_back():
            partial_value = lax.dot_general(
                dkv_now, cross_proj, COL_DIMS, preferred_element_type=jnp.float32
            )
            grad_cross_enc = lax.dot_general(
                kept["kv_rows"], dkv_now, ROW_DIMS, preferred_element_type=jnp.float32
            )
            return (partial_value, grad_cross_enc)

        def cross_back(grad_full):
            grad_mixed_c = jnp.dot(
                grad_full, second_cols, preferred_element_type=jnp.float32
            ).astype(jnp.bfloat16)
            grad_second = lax.dot_general(
                grad_full, kept["mixed_c"], ROW_DIMS, preferred_element_type=jnp.float32
            )
            grad_qc, grad_kc, grad_vc = attend_back(
                to_heads(grad_mixed_c),
                to_heads(kept["query_c"]),
                kv_split[:, :, :, 0],
                kv_split[:, :, :, 1],
                kept["lse_cross"],
                source_len,
                False,
            )
            grad_qc = to_rows(grad_qc).astype(jnp.bfloat16)
            grad_first = lax.dot_general(
                kept["a_rows"], grad_qc, ROW_DIMS, preferred_element_type=jnp.float32
            )
            partial_value = lax.dot_general(
                grad_qc, first_cols, COL_DIMS, preferred_element_type=jnp.float32
            )
            grad_kv = (
                jnp.stack([grad_kc, grad_vc], axis=3)
                .astype(jnp.bfloat16)
                .reshape(full_rows, 2 * head_cols)
            )
            grad_cross_dec = jnp.stack(
                [
                    grad_first.reshape(width, head_local, HS),
                    grad_second.reshape(width, head_local, HS),
                ],
                axis=2,
            ).reshape(width, 2 * head_cols)
            return (partial_value, grad_cross_dec, grad_kv)

        first_full = grad_rows(jnp.where(decoder, grad_r3d, 0.0).astype(jnp.bfloat16))

        def enc_first():
            partial_value, grad_cross_enc = kv_back()
            return (partial_value, grad_cross_enc) + zero_ffn

        def dec_first():
            partial_value, inner_made, shift_made, down_made = ffn_backward(
                first_full, kept["ffn_rows"], kept["hidden"], in_proj, down_proj
            )
            return (partial_value, zero_cross, inner_made, shift_made, down_made)

        partial_one, cross_enc, inner_one, inner_shift_one, down_one = lax.cond(
            decoder, dec_first, enc_first
        )
        first_sum = grad_sums(partial_one)
        grad_r3e, gain_ye, shift_ye = norm_back(
            first_sum, kept["norm_y"], kept["factor_y"], gains[2]
        )
        grad_r2, gain_c, shift_c = norm_back(
            alpha * grad_r3d + first_sum, kept["norm_c"], kept["factor_c"], gains[1]
        )
        grad_r3 = jnp.where(decoder, grad_r3d, grad_r3e)
        gain_y = jnp.where(decoder, gain_yd, gain_ye)
        shift_y = jnp.where(decoder, shift_yd, shift_ye)
        middle_grad = jnp.where(decoder, grad_r2, grad_r3e)
        second_full = ffn_grad_rows(middle_grad.astype(jnp.bfloat16))

        def enc_second():
            partial_value, inner_made, shift_made, down_made = ffn_backward(
                second_full, kept["ffn_rows"], kept["hidden"], in_proj, down_proj
            )
            return (
                partial_value,
                inner_made,
                shift_made,
                down_made,
                zero_cross,
                zeros_low((full_rows, 2 * head_cols)),
            )

        def dec_second():
            partial_value, grad_cross_dec, grad_kv_made = cross_back(second_full)
            return (partial_value,) + zero_ffn + (grad_cross_dec, grad_kv_made)

        partial_two, inner_two, inner_shift_two, down_two, cross_dec, grad_kv = lax.cond(
            decoder, dec_second, enc_second
        )
        grad_a = alpha * middle_grad + ffn_grad_sums(partial_two)
        dkv_held = from_behind(grad_kv, "section", -1)
        grad_r1, gain_a, shift_a = norm_back(grad_a, kept["norm_a"], kept["factor_a"], gains[0])
        attn_full = grad_rows(grad_r1.astype(jnp.bfloat16))
        grad_mixed = lax.dot_general(
            attn_full, out_proj, COL_DIMS, preferred_element_type=jnp.float32
        ).astype(jnp.bfloat16)
        grad_outer = lax.dot_general(
            kept["mixed"], attn_full, ROW_DIMS, preferred_element_type=jnp.float32
        )
        qkv_split = kept["qkv"].reshape(seq_count, slots, head_local, 3, HS)
        grad_q, grad_k, grad_v = attend_back(
            to_heads(grad_mixed),
            qkv_split[:, :, :, 0],
            qkv_split[:, :, :, 1],
            qkv_split[:, :, :, 2],
            kept["lse_self"],
            own_len,
            decoder,
        )
        grad_qkv = (
            jnp.stack([grad_q, grad_k, grad_v], axis=3)
            .astype(jnp.bfloat16)
            .reshape(full_rows, 3 * head_cols)
        )
        grad_qkv_proj = lax.dot_general(
            kept["x_rows"], grad_qkv, ROW_DIMS, preferred_element_type=jnp.float32
        )
        grad_x = alpha * grad_r1 + grad_sums(
            lax.dot_general(grad_qkv, qkv_proj, COL_DIMS, preferred_element_type=jnp.float32)
        )
        grad_ticks.append(grad_x)
        gain_step = jnp.stack([gain_a, jnp.where(decoder, gain_c, 0.0), gain_y])
        shift_step = jnp.stack([shift_a, jnp.where(decoder, shift_c, 0.0), shift_y])
        steps = dict(
            qkv=grad_qkv_proj,
            outer=grad_outer,
            cross=cross_enc + cross_dec,
            inner=inner_one + inner_two,
            inner_shift=inner_shift_one + inner_shift_two,
            down=down_one + down_two,
            down_shift=jnp.sum(grad_r3, axis=0),
            gain=gain_step,
            shift=shift_step,
        )
        totals = {name: totals[name] + jnp.where(live, steps[name], 0.0) for name in totals}
    input_grad = lax.dynamic_slice_in_dim(jnp.stack(grad_ticks[::-1]), section, batches, 0)
    inner_total, inner_shift_total, down_total = (
        totals["inner"],
        totals["inner_shift"],
        totals["down"],
    )
    summed = (
        lax.psum(totals["qkv"].astype(jnp.bfloat16), "dp").astype(jnp.float32),
        lax.psum(totals["outer"].astype(jnp.bfloat16), "dp").astype(jnp.float32),
        lax.psum(totals["cross"].astype(jnp.bfloat16), "dp").astype(jnp.float32),
        lax.psum(inner_total.astype(jnp.bfloat16), "dp").astype(jnp.float32),
        lax.psum(inner_shift_total.astype(jnp.bfloat16), "dp").astype(jnp.float32),
        lax.psum(down_total.astype(jnp.bfloat16), "dp").astype(jnp.float32),
    )
    vectors = lax.psum((totals["gain"], totals["shift"], totals["down_shift"]), ("dp", "tensor"))
    return (
        outputs[None],
        input_grad[None],
        summed[0][None],
        summed[1][None],
        summed[2][None],
        summed[3][None],
        summed[4][None],
        summed[5][None],
        vectors[2][None],
        vectors[0][None],
        vectors[1][None],
    )


def split_lanes(rows):
    return lax.broadcasted_iota(jnp.int32, (rows, 2 * HS), 1) < HS


def swap_halves(tile):
    return jnp.concatenate([tile[:, HS:], tile[:, :HS]], axis=1)


def pair_of(packed, left):
    first, second, third = (packed[:, :LANES], packed[:, LANES : 2 * LANES], packed[:, 2 * LANES :])
    queries = jnp.where(left, first, second)
    keys_in = jnp.where(left, swap_halves(first), swap_halves(third))
    values = jnp.where(left, second, third)
    return (queries, keys_in, values)


def key_limit(position, length, causal):
    return jnp.minimum(length, jnp.where(causal != 0, position + 1, position.dtype.type(1 << 20)))


def attend_pair(scalars, queries_at, keys_in, values, mixed_ref, lse_ref, slots, left):
    length, causal = (scalars[0], scalars[1])
    zero = jnp.zeros((), keys_in.dtype)
    key_halves = (jnp.where(left, keys_in, zero), jnp.where(left, zero, keys_in))
    value_halves = (jnp.where(left, values, zero), jnp.where(left, zero, values))
    left_block = split_lanes(ROWS)
    key_pos = lax.broadcasted_iota(jnp.int32, (ROWS, slots), 1)

    def block(index, carry):
        first_row = pl.multiple_of(index * ROWS, ROWS)
        queries = queries_at(first_row)
        position = first_row + lax.broadcasted_iota(jnp.int32, (ROWS, 1), 0)
        allowed = key_pos < key_limit(position, length, causal)
        total, tops, sums = (None, [], [])
        for half in range(2):
            raw = lax.dot_general(
                queries, key_halves[half], COL_DIMS, preferred_element_type=jnp.float32
            )
            scores = jnp.where(allowed, raw * SCALE, NEG)
            top = jnp.max(scores, axis=1, keepdims=True)
            expo = jnp.exp(scores - top)
            tops.append(top)
            sums.append(jnp.sum(expo, axis=1, keepdims=True))
            part = jnp.dot(
                expo.astype(jnp.bfloat16), value_halves[half], preferred_element_type=jnp.float32
            )
            total = part if half == 0 else total + part
        norm = jnp.where(left_block, sums[0], sums[1])
        mixed_ref[pl.ds(first_row, ROWS), :] = (total / norm).astype(jnp.bfloat16)
        logs = jnp.where(left_block, tops[0] + jnp.log(sums[0]), tops[1] + jnp.log(sums[1]))
        lse_ref[0, :, pl.ds(first_row, ROWS)] = jnp.transpose(logs)[HS - 4 : HS + 4]
        return carry

    lax.fori_loop(0, slots // ROWS, block, 0)


def self_forward_kernel(scalars, packed_ref, mixed_ref, lse_ref, queries_ref):
    slots = packed_ref.shape[0]
    left = split_lanes(slots)
    queries, keys_in, values = pair_of(packed_ref[...], left)
    queries_ref[...] = queries
    attend_pair(
        scalars,
        lambda row: queries_ref[pl.ds(row, ROWS), :],
        keys_in,
        values,
        mixed_ref,
        lse_ref,
        slots,
        left,
    )


def cross_forward_kernel(scalars, query_ref, key_ref, value_ref, mixed_ref, lse_ref):
    slots = query_ref.shape[0]
    attend_pair(
        scalars,
        lambda row: query_ref[pl.ds(row, ROWS), :],
        key_ref[...],
        value_ref[...],
        mixed_ref,
        lse_ref,
        slots,
        split_lanes(slots),
    )


def attend_pair_back(
    scalars, queries_at, keys_in, values, mixed_ref, grad_ref, lse_ref, put_query, key_acc, value_acc
):
    length, causal = (scalars[0], scalars[1])
    slots = keys_in.shape[0]
    left = split_lanes(slots)
    left_block = split_lanes(ROWS)
    zero = jnp.zeros((), keys_in.dtype)
    key_halves = (jnp.where(left, keys_in, zero), jnp.where(left, zero, keys_in))
    value_halves = (jnp.where(left, values, zero), jnp.where(left, zero, values))
    key_pos = lax.broadcasted_iota(jnp.int32, (slots, ROWS), 0)
    key_acc[...] = jnp.zeros_like(key_acc)
    value_acc[...] = jnp.zeros_like(value_acc)

    def block(index, carry):
        first_row = pl.multiple_of(index * ROWS, ROWS)
        queries = queries_at(first_row)
        grads = grad_ref[pl.ds(first_row, ROWS), :]
        mixed = mixed_ref[pl.ds(first_row, ROWS), :]
        product = jnp.transpose(grads.astype(jnp.float32) * mixed.astype(jnp.float32))
        position = first_row + lax.broadcasted_iota(jnp.int32, (1, ROWS), 1)
        allowed = key_pos < key_limit(position, length, causal)
        logs = lse_ref[0, :, pl.ds(first_row, ROWS)]
        query_total = None
        for half in range(2):
            mine = left_block if half == 0 else jnp.logical_not(left_block)
            query_half = jnp.where(mine, queries, zero)
            grad_half = jnp.where(mine, grads, zero)
            raw = lax.dot_general(
                key_halves[half], queries, COL_DIMS, preferred_element_type=jnp.float32
            )
            scores = jnp.where(allowed, raw * SCALE, NEG)
            probs = jnp.exp(scores - logs[3 + half : 4 + half])
            grad_probs = lax.dot_general(
                value_halves[half], grads, COL_DIMS, preferred_element_type=jnp.float32
            )
            delta = jnp.sum(product[half * HS : half * HS + HS], axis=0, keepdims=True)
            grad_raw = (probs * (grad_probs - delta) * SCALE).astype(jnp.bfloat16)
            value_acc[...] += jnp.dot(
                probs.astype(jnp.bfloat16), grad_half, preferred_element_type=jnp.float32
            )
            key_acc[...] += jnp.dot(grad_raw, query_half, preferred_element_type=jnp.float32)
            part = lax.dot_general(
                grad_raw, key_halves[half], ROW_DIMS, preferred_element_type=jnp.float32
            )
            query_total = part if half == 0 else query_total + part
        put_query(first_row, query_total.astype(jnp.bfloat16))
        return carry

    lax.fori_loop(0, slots // ROWS, block, 0)


def self_backward_kernel(
    scalars, packed_ref, mixed_ref, grad_ref, lse_ref, out_ref, queries_ref, dq_ref, key_acc, value_acc
):
    slots = packed_ref.shape[0]
    left = split_lanes(slots)
    queries, keys_in, values = pair_of(packed_ref[...], left)
    queries_ref[...] = queries

    def put_query(row, block):
        dq_ref[pl.ds(row, ROWS), :] = block

    attend_pair_back(
        scalars,
        lambda row: queries_ref[pl.ds(row, ROWS), :],
        keys_in,
        values,
        mixed_ref,
        grad_ref,
        lse_ref,
        put_query,
        key_acc,
        value_acc,
    )
    grad_query = dq_ref[...]
    grad_key = swap_halves(key_acc[...].astype(jnp.bfloat16))
    grad_value = value_acc[...].astype(jnp.bfloat16)
    out_ref[:, :LANES] = jnp.where(left, grad_query, grad_key)
    out_ref[:, LANES : 2 * LANES] = jnp.where(left, grad_value, grad_query)
    out_ref[:, 2 * LANES :] = jnp.where(left, grad_key, grad_value)


def cross_backward_kernel(
    scalars,
    query_ref,
    key_ref,
    value_ref,
    mixed_ref,
    grad_ref,
    lse_ref,
    dq_ref,
    dk_ref,
    dv_ref,
    key_acc,
    value_acc,
):
    def put_query(row, block):
        dq_ref[pl.ds(row, ROWS), :] = block

    attend_pair_back(
        scalars,
        lambda row: query_ref[pl.ds(row, ROWS), :],
        key_ref[...],
        value_ref[...],
        mixed_ref,
        grad_ref,
        lse_ref,
        put_query,
        key_acc,
        value_acc,
    )
    dk_ref[...] = key_acc[...].astype(jnp.bfloat16)
    dv_ref[...] = value_acc[...].astype(jnp.bfloat16)


def head_call(kernel, scalars, arrays, widths, out_widths, scratch, lse_in, lse_out):
    slots = arrays[0].shape[0]
    pairs = arrays[0].shape[1] // widths[0]

    def spec(width):
        return pl.BlockSpec((slots, width), lambda pair, *_: (0, pair))

    lse_spec = pl.BlockSpec((1, 8, slots), lambda pair, *_: (pair, 0, 0))
    in_specs = [spec(width) for width in widths]
    operands = list(arrays)
    if lse_in is not None:
        in_specs.append(lse_spec)
        operands.append(lse_in)
    out_specs = [spec(width) for width in out_widths]
    out_shape = [
        jax.ShapeDtypeStruct((slots, pairs * width), jnp.bfloat16) for width in out_widths
    ]
    if lse_out:
        out_specs.append(lse_spec)
        out_shape.append(jax.ShapeDtypeStruct((pairs, 8, slots), jnp.float32))
    products = 7 if lse_in is None else 17
    return pl.pallas_call(
        kernel,
        grid_spec=pltpu.PrefetchScalarGridSpec(
            num_scalar_prefetch=1,
            grid=(pairs,),
            in_specs=in_specs,
            out_specs=out_specs,
            scratch_shapes=scratch,
        ),
        out_shape=out_shape,
        compiler_params=pltpu.CompilerParams(
            dimension_semantics=("arbitrary",), vmem_limit_bytes=48 * 1024 * 1024
        ),
        cost_estimate=pl.CostEstimate(
            flops=products * pairs * slots * slots * LANES * 8,
            bytes_accessed=sum(a.size * 2 for a in arrays) * 2,
            transcendentals=2 * pairs * slots * slots,
        ),
    )(scalars, *operands)


def self_attention(scalars, packed):
    slots = packed.shape[0]
    return head_call(
        self_forward_kernel,
        scalars,
        [packed],
        [3 * LANES],
        [LANES],
        [pltpu.VMEM((slots, LANES), jnp.bfloat16)],
        None,
        True,
    )


def cross_attention(scalars, queries, keys_in, values):
    return head_call(
        cross_forward_kernel, scalars, [queries, keys_in, values], [LANES] * 3, [LANES], [], None, True
    )


def self_attention_back(scalars, packed, mixed, grads, lse):
    slots = packed.shape[0]
    return head_call(
        self_backward_kernel,
        scalars,
        [packed, mixed, grads],
        [3 * LANES, LANES, LANES],
        [3 * LANES],
        [
            pltpu.VMEM((slots, LANES), jnp.bfloat16),
            pltpu.VMEM((slots, LANES), jnp.bfloat16),
            pltpu.VMEM((slots, LANES), jnp.float32),
            pltpu.VMEM((slots, LANES), jnp.float32),
        ],
        lse,
        False,
    )[0]


def cross_attention_back(scalars, queries, keys_in, values, mixed, grads, lse):
    slots = queries.shape[0]
    return head_call(
        cross_backward_kernel,
        scalars,
        [queries, keys_in, values, mixed, grads],
        [LANES] * 5,
        [LANES] * 3,
        [pltpu.VMEM((slots, LANES), jnp.float32), pltpu.VMEM((slots, LANES), jnp.float32)],
        lse,
        False,
    )


def rows_nt(rows, weight_rows):
    return lax.dot_general(rows, weight_rows, COL_DIMS, preferred_element_type=jnp.float32)


def rows_nn(rows, weight_rows):
    return jnp.dot(rows, weight_rows, preferred_element_type=jnp.float32)


def rows_tn(left_rows, right_rows):
    return lax.dot_general(left_rows, right_rows, ROW_DIMS, preferred_element_type=jnp.float32)


def gelu_slope(values):
    inner = GELU_C * (values + 0.044715 * values * values * values)
    bend = jnp.tanh(inner)
    rise = GELU_C * (1.0 + 3 * 0.044715 * values * values)
    return 0.5 * (1.0 + bend) + 0.5 * values * (1.0 - bend * bend) * rise


def low(values):
    return values.astype(jnp.bfloat16)


def sequence_body(
    inputs,
    lengths,
    cotangent,
    qkv_weight,
    attn_out_weight,
    cross_weight,
    ffn_in_weight,
    ffn_in_bias,
    ffn_out_weight,
    ffn_out_bias,
    norm_gain,
    norm_bias,
):
    section = lax.axis_index("section")
    tensor_index = lax.axis_index("tensor")
    unit = lax.axis_index("dp")
    units = lax.axis_size("dp")
    decoder = section == 1
    alpha = jnp.where(decoder, ALPHA_DEC, ALPHA_ENC).astype(jnp.float32)
    batches, shard_rows, width = (inputs.shape[1], inputs.shape[2], inputs.shape[3])
    slots = batches * shard_rows
    gains = norm_gain[0].astype(jnp.float32)
    shifts = norm_bias[0].astype(jnp.float32)
    down_shift = ffn_out_bias[0].astype(jnp.float32)
    everyone = ("dp", "tensor")

    def own_unit(array, axis):
        size = array.shape[axis] // units
        return lax.dynamic_slice_in_dim(array, unit * size, size, axis)

    def gathered(rows):
        return lax.all_gather(rows, everyone, axis=0, tiled=True)

    def to_sequence(shards):
        return lax.all_to_all(shards, "tensor", 0, 0, tiled=True).reshape(slots, width)

    def to_shards(rows):
        return lax.all_to_all(
            rows.reshape(batches, shard_rows, width), "tensor", 0, 0, tiled=True
        )

    x = to_sequence(inputs[0])
    head_units = cross_weight.shape[2] // (2 * HS) // units
    qkv_rows = gathered(own_unit(qkv_weight[0], 1).T)
    out_rows = gathered(own_unit(attn_out_weight[0], 0))
    cross_unit = own_unit(cross_weight[0], 1).T.reshape(head_units, 2, HS, width)
    cross_first = gathered(cross_unit[:, 0].reshape(head_units * HS, width))
    cross_second = gathered(cross_unit[:, 1].reshape(head_units * HS, width))
    in_rows = gathered(own_unit(ffn_in_weight[0], 1).T)
    down_rows = gathered(own_unit(ffn_out_weight[0], 0))
    in_shift = gathered(own_unit(ffn_in_bias[0], 0)[None]).reshape(-1).astype(jnp.float32)

    source_len = lax.dynamic_index_in_dim(lengths[0, :, 0], tensor_index, 0, keepdims=False)
    target_len = lax.dynamic_index_in_dim(lengths[1, :, 0], tensor_index, 0, keepdims=False)
    own_len = jnp.where(decoder, target_len, source_len)
    self_scalars = jnp.stack([own_len, decoder.astype(jnp.int32)])
    cross_scalars = jnp.stack([source_len, jnp.zeros_like(source_len)])

    qkv = low(rows_nt(x, qkv_rows))
    mixed, lse_self = self_attention(self_scalars, qkv)
    resid_a, norm_a, factor_a = layer_norm(
        alpha * x.astype(jnp.float32) + rows_nn(mixed, out_rows), gains[0], shifts[0]
    )
    a_low = low(resid_a)

    wide = jnp.bfloat16
    square = jnp.zeros((slots, width), wide)

    query_sent = lax.cond(decoder, lambda: low(rows_nt(a_low, cross_first)), lambda: square)
    query_held = lax.ppermute(query_sent, "section", [(1, 0)])

    def feed(rows_low, rows_wide, gain_row, shift_row):
        pre_act = rows_nt(rows_low, in_rows) + in_shift
        hidden = low(jax.nn.gelu(pre_act))
        made = layer_norm(
            alpha * rows_wide + rows_nn(hidden, down_rows) + down_shift, gain_row, shift_row
        )
        return (pre_act, hidden) + made

    def feed_back(grad_sum, pre_act):
        grad_low = low(grad_sum)
        grad_pre = low(rows_nt(grad_low, down_rows) * gelu_slope(pre_act))
        return (grad_low, grad_pre, alpha * grad_sum + rows_nn(grad_pre, in_rows))

    def enc_feed():
        pre_act, hidden, memory, norm_y, factor_y = feed(a_low, resid_a, gains[2], shifts[2])
        memory_low = low(memory)
        keys_in = low(rows_nt(memory_low, cross_first))
        values = low(rows_nt(memory_low, cross_second))
        mixed_c, lse_c = cross_attention(cross_scalars, query_held, keys_in, values)
        return (pre_act, hidden, memory_low, norm_y, factor_y, keys_in, values, mixed_c, lse_c)

    def no_feed():
        shapes = jax.eval_shape(enc_feed)
        return jax.tree.map(lambda leaf: jnp.zeros(leaf.shape, leaf.dtype), shapes)

    pre_e, hidden_e, memory_low, norm_e, factor_e, keys_in, values, mixed_c, lse_c = lax.cond(
        decoder, no_feed, enc_feed
    )
    mixed_held = lax.ppermute(mixed_c, "section", [(0, 1)])

    own_pos = lax.broadcasted_iota(jnp.int32, (slots, 1), 0)
    cotangent_rows = to_sequence(cotangent)

    def dec_middle():
        resid_c, norm_c, factor_c = layer_norm(
            alpha * resid_a + rows_nn(mixed_held, cross_second), gains[1], shifts[1]
        )
        c_low = low(resid_c)
        pre_act, hidden, decoded, norm_y, factor_y = feed(c_low, resid_c, gains[2], shifts[2])
        grad_top = jnp.where(own_pos < target_len, cotangent_rows.astype(jnp.float32), 0.0)
        grad_y, gain_y, shift_y = norm_back(grad_top, norm_y, factor_y, gains[2])
        grad_low, grad_pre, grad_c = feed_back(grad_y, pre_act)
        grad_mid, gain_c, shift_c = norm_back(grad_c, norm_c, factor_c, gains[1])
        mid_low = low(grad_mid)
        grad_mixed_c = low(rows_nt(mid_low, cross_second))
        return (
            low(decoded),
            hidden,
            c_low,
            grad_low,
            grad_pre,
            grad_mid,
            mid_low,
            grad_mixed_c,
            (gain_c, gain_y),
            (shift_c, shift_y),
            jnp.sum(grad_y, axis=0),
        )

    def no_middle():
        shapes = jax.eval_shape(dec_middle)
        return jax.tree.map(lambda leaf: jnp.zeros(leaf.shape, leaf.dtype), shapes)

    (
        decoded_low,
        hidden_d,
        c_low,
        grad_low_d,
        grad_pre_d,
        grad_mid,
        mid_low,
        grad_mixed_c,
        gains_d,
        shifts_d,
        down_shift_d,
    ) = lax.cond(decoder, dec_middle, no_middle)
    grad_mixed_held = lax.ppermute(grad_mixed_c, "section", [(1, 0)])
    outputs = to_shards(jnp.where(decoder, decoded_low, memory_low))

    def enc_cross():
        return tuple(
            cross_attention_back(
                cross_scalars, query_held, keys_in, values, mixed_c, grad_mixed_held, lse_c
            )
        )

    def no_cross():
        return (square, square, square)

    grad_query, grad_key, grad_value = lax.cond(decoder, no_cross, enc_cross)
    grad_query_held = lax.ppermute(grad_query, "section", [(0, 1)])

    def enc_back():
        grad_memory = rows_nn(grad_key, cross_first) + rows_nn(grad_value, cross_second)
        grad_y, gain_y, shift_y = norm_back(grad_memory, norm_e, factor_e, gains[2])
        grad_low, grad_pre, grad_a = feed_back(grad_y, pre_e)
        zero_row = jnp.zeros_like(gain_y)
        return (
            grad_low,
            grad_pre,
            hidden_e,
            a_low,
            grad_a,
            (zero_row, gain_y),
            (zero_row, shift_y),
            jnp.sum(grad_y, axis=0),
            grad_key,
            memory_low,
            grad_value,
            memory_low,
        )

    def dec_back():
        grad_a = alpha * grad_mid + rows_nn(grad_query_held, cross_first)
        return (
            grad_low_d,
            grad_pre_d,
            hidden_d,
            c_low,
            grad_a,
            gains_d,
            shifts_d,
            down_shift_d,
            grad_query_held,
            a_low,
            mixed_held,
            mid_low,
        )

    (
        grad_low,
        grad_pre,
        hidden,
        feed_rows,
        grad_a,
        gain_cy,
        shift_cy,
        down_shift_step,
        first_left,
        first_right,
        second_left,
        second_right,
    ) = lax.cond(decoder, dec_back, enc_back)

    def summed(grad_rows_all, block):
        scattered = lax.psum_scatter(
            low(grad_rows_all), everyone, scatter_dimension=0, tiled=True
        )
        return lax.all_gather(scattered, "dp", axis=0, tiled=True).astype(jnp.float32)

    first_grad = summed(rows_tn(first_left, first_right), HS)
    second_grad = summed(rows_tn(second_left, second_right), HS)
    down_grad = summed(rows_tn(hidden, grad_low), 0)
    in_grad = summed(rows_tn(grad_pre, feed_rows), 0)
    in_shift_grad = lax.psum_scatter(
        jnp.sum(grad_pre.astype(jnp.float32), axis=0), everyone, scatter_dimension=0, tiled=True
    )
    in_shift_grad = lax.all_gather(in_shift_grad, "dp", axis=0, tiled=True)

    grad_r, gain_a, shift_a = norm_back(grad_a, norm_a, factor_a, gains[0])
    r_low = low(grad_r)
    grad_mixed = low(rows_nt(r_low, out_rows))
    out_grad = summed(rows_tn(mixed, r_low), 0)
    grad_qkv = self_attention_back(self_scalars, qkv, mixed, grad_mixed, lse_self)
    grad_x = alpha * grad_r + rows_nn(grad_qkv, qkv_rows)
    input_grad = to_shards(low(grad_x)).astype(jnp.float32)
    qkv_grad = summed(rows_tn(grad_qkv, x), 0)

    vectors = lax.psum(
        (
            jnp.stack([gain_a, gain_cy[0], gain_cy[1]]),
            jnp.stack([shift_a, shift_cy[0], shift_cy[1]]),
            down_shift_step,
        ),
        everyone,
    )
    cross_grad = (
        jnp.stack([first_grad.reshape(-1, HS, width), second_grad.reshape(-1, HS, width)], axis=1)
        .reshape(-1, width)
        .T
    )
    return (
        outputs[None],
        input_grad[None],
        qkv_grad.T[None],
        out_grad[None],
        cross_grad[None],
        in_grad.T[None],
        in_shift_grad[None],
        down_grad[None],
        vectors[2][None],
        vectors[0][None],
        vectors[1][None],
    )


def solution(mesh):
    placed = (
        P("section", None, ("dp", "tensor"), None),
        P(None, None, "dp"),
        P(None, ("dp", "tensor"), None),
        P("section", None, "tensor"),
        P("section", "tensor", None),
        P("section", None, "tensor"),
        P("section", None, "tensor"),
        P("section", "tensor"),
        P("section", "tensor", None),
        P("section", None),
        P("section", None, None),
        P("section", None, None),
    )
    returned = (
        P("section", None, ("dp", "tensor"), None),
        P("section", None, ("dp", "tensor"), None),
        P("section", None, "tensor"),
        P("section", "tensor", None),
        P("section", None, "tensor"),
        P("section", None, "tensor"),
        P("section", "tensor"),
        P("section", "tensor", None),
        P("section", None),
        P("section", None, None),
        P("section", None, None),
    )
    sizes = dict(mesh.shape)

    def whole(*arrays):
        batches, sequences = arrays[1].shape[1:]
        heads = arrays[3].shape[2] // (3 * HS)
        group = sizes["dp"] * sizes["tensor"]
        one_each = batches == sizes["tensor"] and sequences == sizes["dp"] and heads % group == 0
        chosen = sequence_body if one_each else body
        return jax.shard_map(
            chosen, mesh=mesh, in_specs=placed, out_specs=returned, check_vma=False
        )(*arrays)

    return whole
```

```python
import functools

import jax
import jax.numpy as jnp
from jax import lax
from jax.experimental import pallas as pl
from jax.experimental.pallas import tpu as pltpu
from jax.sharding import PartitionSpec as P

HS = 64
QBLOCK = 512


ALPHA_ENC = 0.81 * (100.0**5) ** (1.0 / 16.0)
ALPHA_DEC = (3.0 * 100.0) ** 0.25
EPS = 1e-05
NEG = -1e30
ROW_DIMS = (((0,), (0,)), ((), ()))
COL_DIMS = (((1,), (1,)), ((), ()))
LANES = 2 * HS
ROWS = 256
CHUNK = 32
MESH = pl.DeviceIdType.MESH
SCALE = HS ** (-0.5)
GELU_C = (2.0 / 3.141592653589793) ** 0.5


def from_behind(block, axis, distance):
    devices = range(lax.axis_size(axis))
    route = [(i - distance, i) for i in devices if i - distance in devices]
    return lax.ppermute(block, axis, route)


def layer_norm(values, gain_row, shift_row):
    centered = values - jnp.mean(values, axis=-1, keepdims=True)
    factor = lax.rsqrt(jnp.mean(centered * centered, axis=-1, keepdims=True) + EPS)
    normed = centered * factor
    return (normed * gain_row + shift_row, normed, factor)


def norm_back(gradient, normed, factor, gain_row):
    scaled = gradient * gain_row
    centred = (
        scaled
        - jnp.mean(scaled, axis=-1, keepdims=True)
        - normed * jnp.mean(scaled * normed, axis=-1, keepdims=True)
    )
    return (centred * factor, jnp.sum(gradient * normed, axis=0), jnp.sum(gradient, axis=0))


def visible(first_row, row_count, key_count, seq_lengths, causal):
    key_pos = lax.broadcasted_iota(jnp.int32, (1, row_count, key_count), 2)
    query_pos = first_row + lax.broadcasted_iota(jnp.int32, (1, row_count, key_count), 1)
    inside = key_pos < seq_lengths[:, None, None]
    return inside & ((key_pos <= query_pos) | jnp.logical_not(causal))


def attend(queries, keys_in, values, seq_lengths, causal):
    key_count = queries.shape[1]
    score_scale = queries.shape[3] ** (-0.5)
    row_block = min(QBLOCK, key_count)
    mixed_parts, lse_parts = ([], [])
    for first_row in range(0, key_count, row_block):
        allowed = visible(first_row, row_block, key_count, seq_lengths, causal)
        raw_scores = jnp.einsum(
            "bqhe,bkhe->bhqk",
            queries[:, first_row : first_row + row_block],
            keys_in,
            preferred_element_type=jnp.float32,
        )
        scores = jnp.where(allowed[:, None], raw_scores * score_scale, NEG)
        row_max = jnp.max(scores, axis=-1, keepdims=True)
        expo_vals = jnp.exp(scores - row_max)
        row_total = jnp.sum(expo_vals, axis=-1, keepdims=True)
        weights = (expo_vals / row_total).astype(jnp.bfloat16)
        mixed_block = jnp.einsum(
            "bhqk,bkhe->bqhe", weights, values, preferred_element_type=jnp.float32
        )
        mixed_parts.append(mixed_block.astype(jnp.bfloat16))
        lse_parts.append(row_max + jnp.log(row_total))
    return (jnp.concatenate(mixed_parts, axis=1), jnp.concatenate(lse_parts, axis=2))


def attend_back(grad_mixed, queries, keys_in, values, log_totals, seq_lengths, causal):
    key_count = queries.shape[1]
    score_scale = queries.shape[3] ** (-0.5)
    row_block = min(QBLOCK, key_count)
    query_parts = []
    grad_keys = jnp.zeros(keys_in.shape, jnp.float32)
    grad_values = jnp.zeros(values.shape, jnp.float32)
    for first_row in range(0, key_count, row_block):
        query_part = queries[:, first_row : first_row + row_block]
        grad_part = grad_mixed[:, first_row : first_row + row_block]
        allowed = visible(first_row, row_block, key_count, seq_lengths, causal)
        raw_scores = jnp.einsum(
            "bqhe,bkhe->bhqk", query_part, keys_in, preferred_element_type=jnp.float32
        )
        scores = jnp.where(allowed[:, None], raw_scores * score_scale, NEG)
        probs = jnp.exp(scores - log_totals[:, :, first_row : first_row + row_block])
        grad_probs = jnp.einsum(
            "bqhe,bkhe->bhqk", grad_part, values, preferred_element_type=jnp.float32
        )
        grad_scores = probs * (grad_probs - jnp.sum(probs * grad_probs, axis=-1, keepdims=True))
        grad_raw = (grad_scores * score_scale).astype(jnp.bfloat16)
        query_parts.append(
            jnp.einsum("bhqk,bkhe->bqhe", grad_raw, keys_in, preferred_element_type=jnp.float32)
        )
        grad_keys = grad_keys + jnp.einsum(
            "bhqk,bqhe->bkhe", grad_raw, query_part, preferred_element_type=jnp.float32
        )
        grad_values = grad_values + jnp.einsum(
            "bhqk,bqhe->bkhe",
            probs.astype(jnp.bfloat16),
            grad_part,
            preferred_element_type=jnp.float32,
        )
    return (jnp.concatenate(query_parts, axis=1), grad_keys, grad_values)


def ffn_forward(rows_in, in_proj, in_shift, down_proj):
    pre_act = jnp.dot(rows_in, in_proj, preferred_element_type=jnp.float32) + in_shift
    hidden = jax.nn.gelu(pre_act).astype(jnp.bfloat16)
    return (pre_act, jnp.dot(hidden, down_proj, preferred_element_type=jnp.float32))


def ffn_backward(grad_in, rows_in, pre_act, in_proj, down_proj):
    activated, slope_back = jax.vjp(jax.nn.gelu, pre_act)
    hidden = activated.astype(jnp.bfloat16)
    grad_down = lax.dot_general(hidden, grad_in, ROW_DIMS, preferred_element_type=jnp.float32)
    grad_hidden = lax.dot_general(grad_in, down_proj, COL_DIMS, preferred_element_type=jnp.float32)
    grad_pre = slope_back(grad_hidden)[0].astype(jnp.bfloat16)
    grad_shift = jnp.sum(grad_pre.astype(jnp.float32), axis=0)
    grad_inner = lax.dot_general(rows_in, grad_pre, ROW_DIMS, preferred_element_type=jnp.float32)
    grad_rows_out = lax.dot_general(grad_pre, in_proj, COL_DIMS, preferred_element_type=jnp.float32)
    return (grad_rows_out, grad_inner, grad_shift, grad_down)


def gather_rows(shard):
    return lax.all_gather(shard, "tensor", axis=0, tiled=True)


def sum_rows(partial_value):
    return lax.psum_scatter(partial_value, "tensor", scatter_dimension=0, tiled=True)


def ffn_input_rows(shard):
    return lax.all_gather(shard, "tensor", axis=0, tiled=True)


def ffn_sum_rows(partial_value):
    return lax.psum_scatter(
        partial_value.astype(jnp.bfloat16), "tensor", scatter_dimension=0, tiled=True
    ).astype(jnp.float32)


def grad_rows(shard):
    return lax.all_gather(shard, "tensor", axis=0, tiled=True)


def grad_sums(partial_value):
    return lax.psum_scatter(
        partial_value.astype(jnp.bfloat16), "tensor", scatter_dimension=0, tiled=True
    ).astype(jnp.float32)


def ffn_grad_rows(shard):
    return lax.all_gather(shard, "tensor", axis=0, tiled=True)


def ffn_grad_sums(partial_value):
    return lax.psum_scatter(
        partial_value.astype(jnp.bfloat16), "tensor", scatter_dimension=0, tiled=True
    ).astype(jnp.float32)


def body(
    inputs,
    lengths,
    cotangent,
    qkv_weight,
    attn_out_weight,
    cross_weight,
    ffn_in_weight,
    ffn_in_bias,
    ffn_out_weight,
    ffn_out_bias,
    norm_gain,
    norm_bias,
):
    tensor_count = lax.axis_size("tensor")
    section = lax.axis_index("section")
    tensor_index = lax.axis_index("tensor")
    decoder = section == 1
    alpha = jnp.where(decoder, ALPHA_DEC, ALPHA_ENC).astype(jnp.float32)
    batches, shard_rows, width = (inputs.shape[1], inputs.shape[2], inputs.shape[3])
    seq_count = lengths.shape[2]
    full_rows = shard_rows * tensor_count
    slots = full_rows // seq_count
    qkv_proj = qkv_weight[0]
    head_local = qkv_proj.shape[1] // (3 * HS)
    head_cols = head_local * HS
    out_proj = attn_out_weight[0]
    cross_proj = cross_weight[0]
    cross_split = cross_proj.reshape(width, head_local, 2, HS)
    first_cols = cross_split[:, :, 0].reshape(width, head_cols)
    second_cols = cross_split[:, :, 1].reshape(width, head_cols)
    in_proj = ffn_in_weight[0]
    in_shift = ffn_in_bias[0].astype(jnp.float32)
    down_proj = ffn_out_weight[0]
    hidden_width = in_proj.shape[1]
    down_shift = ffn_out_bias[0].astype(jnp.float32)
    gains = norm_gain[0].astype(jnp.float32)
    shifts = norm_bias[0].astype(jnp.float32)
    own_lengths = lax.dynamic_index_in_dim(lengths, section, 0, keepdims=False)
    source_lengths = lengths[0]
    row_index = tensor_index * shard_rows + lax.iota(jnp.int32, shard_rows)
    row_seq = row_index // slots
    row_pos = row_index % slots
    seq_ids = lax.iota(jnp.int32, seq_count)
    lse_shape = (seq_count, head_local, slots, 1)

    def zeros_float(shape):
        return jnp.zeros(shape, jnp.float32)

    def zeros_low(shape):
        return jnp.zeros(shape, jnp.bfloat16)

    def to_heads(flat_rows):
        return flat_rows.reshape(seq_count, slots, flat_rows.shape[1] // HS, HS)

    def to_rows(split_rows):
        return split_rows.reshape(full_rows, -1)

    def cross_forward(query_rows, kv_source, source_len):
        kv_split = kv_source.reshape(seq_count, slots, head_local, 2, HS)
        query_c = jnp.dot(query_rows, first_cols, preferred_element_type=jnp.float32).astype(
            jnp.bfloat16
        )
        mixed_c, lse_cross = attend(
            to_heads(query_c), kv_split[:, :, :, 0], kv_split[:, :, :, 1], source_len, False
        )
        mixed_c = to_rows(mixed_c)
        partial_value = lax.dot_general(
            mixed_c, second_cols, COL_DIMS, preferred_element_type=jnp.float32
        )
        return (query_c, mixed_c, lse_cross, partial_value)

    kv_held = zeros_low((full_rows, 2 * head_cols))
    kv_ticks, kept_ticks, out_ticks = ([], [], [])
    for tick_index in range(batches + 1):
        batch = jnp.clip(tick_index - section, 0, batches - 1)
        x_shard = lax.dynamic_index_in_dim(inputs[0], batch, 0, keepdims=False)
        own_len = lax.dynamic_index_in_dim(own_lengths, batch, 0, keepdims=False)
        source_len = lax.dynamic_index_in_dim(source_lengths, batch, 0, keepdims=False)
        x_full = gather_rows(x_shard)
        qkv = jnp.dot(x_full, qkv_proj, preferred_element_type=jnp.float32).astype(jnp.bfloat16)
        qkv_split = qkv.reshape(seq_count, slots, head_local, 3, HS)
        mixed, lse_self = attend(
            qkv_split[:, :, :, 0], qkv_split[:, :, :, 1], qkv_split[:, :, :, 2], own_len, decoder
        )
        mixed = to_rows(mixed)
        attn_sum = sum_rows(jnp.dot(mixed, out_proj, preferred_element_type=jnp.float32))
        resid_a, norm_a, factor_a = layer_norm(
            alpha * x_shard.astype(jnp.float32) + attn_sum, gains[0], shifts[0]
        )
        a_shard = resid_a.astype(jnp.bfloat16)
        a_full = gather_rows(a_shard)

        def enc_second():
            hidden_made, partial_value = ffn_forward(a_full, in_proj, in_shift, down_proj)
            return (
                hidden_made,
                zeros_low((full_rows, head_cols)),
                zeros_low((full_rows, head_cols)),
                zeros_float(lse_shape),
                partial_value,
            )

        def dec_second():
            query_c, mixed_c, lse_cross, partial_value = cross_forward(a_full, kv_held, source_len)
            return (
                zeros_float((full_rows, hidden_width)),
                query_c,
                mixed_c,
                lse_cross,
                partial_value,
            )

        hidden_enc, query_c, mixed_c, lse_cross, partial_value = lax.cond(
            decoder, dec_second, enc_second
        )
        second_sum = sum_rows(partial_value)
        resid_ye, norm_ye, factor_ye = layer_norm(
            alpha * resid_a + second_sum + down_shift, gains[2], shifts[2]
        )
        resid_c, norm_c, factor_c = layer_norm(alpha * resid_a + second_sum, gains[1], shifts[1])
        wide_rows = ffn_input_rows(jnp.where(decoder, resid_c, resid_ye).astype(jnp.bfloat16))

        def enc_third():
            kv_made = jnp.dot(wide_rows, cross_proj, preferred_element_type=jnp.float32).astype(
                jnp.bfloat16
            )
            return (
                kv_made,
                zeros_float((full_rows, hidden_width)),
                zeros_float((full_rows, width)),
            )

        def dec_third():
            hidden_made, partial_made = ffn_forward(wide_rows, in_proj, in_shift, down_proj)
            return (zeros_low((full_rows, 2 * head_cols)), hidden_made, partial_made)

        kv_out, hidden_dec, partial_third = lax.cond(decoder, dec_third, enc_third)
        third_sum = ffn_sum_rows(partial_third)
        resid_yd, norm_yd, factor_yd = layer_norm(
            alpha * resid_c + third_sum + down_shift, gains[2], shifts[2]
        )
        resid_y = jnp.where(decoder, resid_yd, resid_ye)
        norm_y = jnp.where(decoder, norm_yd, norm_ye)
        factor_y = jnp.where(decoder, factor_yd, factor_ye)
        hidden = jnp.where(decoder, hidden_dec, hidden_enc)
        ffn_rows = jnp.where(decoder, wide_rows, a_full)
        y_shard = resid_y.astype(jnp.bfloat16)
        kv_held = from_behind(kv_out, "section", 1)
        kv_ticks.append(kv_held)
        out_ticks.append(y_shard)
        kept_ticks.append(
            dict(
                x_rows=x_full,
                qkv=qkv,
                mixed=mixed,
                lse_self=lse_self,
                a_rows=a_full,
                kv_rows=wide_rows,
                ffn_rows=ffn_rows,
                hidden=hidden,
                query_c=query_c,
                mixed_c=mixed_c,
                lse_cross=lse_cross,
                norm_a=norm_a,
                factor_a=factor_a,
                norm_c=norm_c,
                factor_c=factor_c,
                norm_y=norm_y,
                factor_y=factor_y,
            )
        )
    kept_all = jax.tree.map(lambda *leaves: jnp.stack(leaves), *kept_ticks)
    kv_stack = jnp.stack(kv_ticks)
    outputs = lax.dynamic_slice_in_dim(jnp.stack(out_ticks), section, batches, 0)
    totals = dict(
        qkv=zeros_float(qkv_proj.shape),
        outer=zeros_float(out_proj.shape),
        cross=zeros_float(cross_proj.shape),
        inner=zeros_float(in_proj.shape),
        inner_shift=zeros_float(in_shift.shape),
        down=zeros_float(down_proj.shape),
        down_shift=zeros_float(down_shift.shape),
        gain=zeros_float(gains.shape),
        shift=zeros_float(shifts.shape),
    )
    zero_ffn = (
        zeros_float(in_proj.shape),
        zeros_float(in_shift.shape),
        zeros_float(down_proj.shape),
    )
    zero_cross = zeros_float((width, 2 * head_cols))
    dkv_held = zeros_low((full_rows, 2 * head_cols))
    grad_ticks = []
    for tick_index in range(batches + 1):
        batch_raw = batches - tick_index - section
        live = (batch_raw >= 0) & (batch_raw < batches)
        batch = jnp.clip(batch_raw, 0, batches - 1)
        kept = jax.tree.map(
            lambda leaf_value: lax.dynamic_index_in_dim(
                leaf_value, batch + section, 0, keepdims=False
            ),
            kept_all,
        )
        own_len = lax.dynamic_index_in_dim(own_lengths, batch, 0, keepdims=False)
        source_len = lax.dynamic_index_in_dim(source_lengths, batch, 0, keepdims=False)
        kv_now = lax.dynamic_index_in_dim(kv_stack, batch, 0, keepdims=False)
        kv_split = kv_now.reshape(seq_count, slots, head_local, 2, HS)
        own_rows = jnp.sum(
            jnp.where(row_seq[:, None] == seq_ids[None, :], own_len[None, :], 0), axis=1
        )
        grad_top = lax.dynamic_index_in_dim(cotangent, batch, 0, keepdims=False).astype(jnp.float32)
        grad_top = jnp.where((row_pos < own_rows)[:, None], grad_top, 0.0)
        grad_r3d, gain_yd, shift_yd = norm_back(
            grad_top, kept["norm_y"], kept["factor_y"], gains[2]
        )
        dkv_now = dkv_held

        def kv_back():
            partial_value = lax.dot_general(
                dkv_now, cross_proj, COL_DIMS, preferred_element_type=jnp.float32
            )
            grad_cross_enc = lax.dot_general(
                kept["kv_rows"], dkv_now, ROW_DIMS, preferred_element_type=jnp.float32
            )
            return (partial_value, grad_cross_enc)

        def cross_back(grad_full):
            grad_mixed_c = jnp.dot(
                grad_full, second_cols, preferred_element_type=jnp.float32
            ).astype(jnp.bfloat16)
            grad_second = lax.dot_general(
                grad_full, kept["mixed_c"], ROW_DIMS, preferred_element_type=jnp.float32
            )
            grad_qc, grad_kc, grad_vc = attend_back(
                to_heads(grad_mixed_c),
                to_heads(kept["query_c"]),
                kv_split[:, :, :, 0],
                kv_split[:, :, :, 1],
                kept["lse_cross"],
                source_len,
                False,
            )
            grad_qc = to_rows(grad_qc).astype(jnp.bfloat16)
            grad_first = lax.dot_general(
                kept["a_rows"], grad_qc, ROW_DIMS, preferred_element_type=jnp.float32
            )
            partial_value = lax.dot_general(
                grad_qc, first_cols, COL_DIMS, preferred_element_type=jnp.float32
            )
            grad_kv = (
                jnp.stack([grad_kc, grad_vc], axis=3)
                .astype(jnp.bfloat16)
                .reshape(full_rows, 2 * head_cols)
            )
            grad_cross_dec = jnp.stack(
                [
                    grad_first.reshape(width, head_local, HS),
                    grad_second.reshape(width, head_local, HS),
                ],
                axis=2,
            ).reshape(width, 2 * head_cols)
            return (partial_value, grad_cross_dec, grad_kv)

        first_full = grad_rows(jnp.where(decoder, grad_r3d, 0.0).astype(jnp.bfloat16))

        def enc_first():
            partial_value, grad_cross_enc = kv_back()
            return (partial_value, grad_cross_enc) + zero_ffn

        def dec_first():
            partial_value, inner_made, shift_made, down_made = ffn_backward(
                first_full, kept["ffn_rows"], kept["hidden"], in_proj, down_proj
            )
            return (partial_value, zero_cross, inner_made, shift_made, down_made)

        partial_one, cross_enc, inner_one, inner_shift_one, down_one = lax.cond(
            decoder, dec_first, enc_first
        )
        first_sum = grad_sums(partial_one)
        grad_r3e, gain_ye, shift_ye = norm_back(
            first_sum, kept["norm_y"], kept["factor_y"], gains[2]
        )
        grad_r2, gain_c, shift_c = norm_back(
            alpha * grad_r3d + first_sum, kept["norm_c"], kept["factor_c"], gains[1]
        )
        grad_r3 = jnp.where(decoder, grad_r3d, grad_r3e)
        gain_y = jnp.where(decoder, gain_yd, gain_ye)
        shift_y = jnp.where(decoder, shift_yd, shift_ye)
        middle_grad = jnp.where(decoder, grad_r2, grad_r3e)
        second_full = ffn_grad_rows(middle_grad.astype(jnp.bfloat16))

        def enc_second():
            partial_value, inner_made, shift_made, down_made = ffn_backward(
                second_full, kept["ffn_rows"], kept["hidden"], in_proj, down_proj
            )
            return (
                partial_value,
                inner_made,
                shift_made,
                down_made,
                zero_cross,
                zeros_low((full_rows, 2 * head_cols)),
            )

        def dec_second():
            partial_value, grad_cross_dec, grad_kv_made = cross_back(second_full)
            return (partial_value,) + zero_ffn + (grad_cross_dec, grad_kv_made)

        partial_two, inner_two, inner_shift_two, down_two, cross_dec, grad_kv = lax.cond(
            decoder, dec_second, enc_second
        )
        grad_a = alpha * middle_grad + ffn_grad_sums(partial_two)
        dkv_held = from_behind(grad_kv, "section", -1)
        grad_r1, gain_a, shift_a = norm_back(grad_a, kept["norm_a"], kept["factor_a"], gains[0])
        attn_full = grad_rows(grad_r1.astype(jnp.bfloat16))
        grad_mixed = lax.dot_general(
            attn_full, out_proj, COL_DIMS, preferred_element_type=jnp.float32
        ).astype(jnp.bfloat16)
        grad_outer = lax.dot_general(
            kept["mixed"], attn_full, ROW_DIMS, preferred_element_type=jnp.float32
        )
        qkv_split = kept["qkv"].reshape(seq_count, slots, head_local, 3, HS)
        grad_q, grad_k, grad_v = attend_back(
            to_heads(grad_mixed),
            qkv_split[:, :, :, 0],
            qkv_split[:, :, :, 1],
            qkv_split[:, :, :, 2],
            kept["lse_self"],
            own_len,
            decoder,
        )
        grad_qkv = (
            jnp.stack([grad_q, grad_k, grad_v], axis=3)
            .astype(jnp.bfloat16)
            .reshape(full_rows, 3 * head_cols)
        )
        grad_qkv_proj = lax.dot_general(
            kept["x_rows"], grad_qkv, ROW_DIMS, preferred_element_type=jnp.float32
        )
        grad_x = alpha * grad_r1 + grad_sums(
            lax.dot_general(grad_qkv, qkv_proj, COL_DIMS, preferred_element_type=jnp.float32)
        )
        grad_ticks.append(grad_x)
        gain_step = jnp.stack([gain_a, jnp.where(decoder, gain_c, 0.0), gain_y])
        shift_step = jnp.stack([shift_a, jnp.where(decoder, shift_c, 0.0), shift_y])
        steps = dict(
            qkv=grad_qkv_proj,
            outer=grad_outer,
            cross=cross_enc + cross_dec,
            inner=inner_one + inner_two,
            inner_shift=inner_shift_one + inner_shift_two,
            down=down_one + down_two,
            down_shift=jnp.sum(grad_r3, axis=0),
            gain=gain_step,
            shift=shift_step,
        )
        totals = {name: totals[name] + jnp.where(live, steps[name], 0.0) for name in totals}
    input_grad = lax.dynamic_slice_in_dim(jnp.stack(grad_ticks[::-1]), section, batches, 0)
    inner_total, inner_shift_total, down_total = (
        totals["inner"],
        totals["inner_shift"],
        totals["down"],
    )
    summed = (
        lax.psum(totals["qkv"].astype(jnp.bfloat16), "dp").astype(jnp.float32),
        lax.psum(totals["outer"].astype(jnp.bfloat16), "dp").astype(jnp.float32),
        lax.psum(totals["cross"].astype(jnp.bfloat16), "dp").astype(jnp.float32),
        lax.psum(inner_total.astype(jnp.bfloat16), "dp").astype(jnp.float32),
        lax.psum(inner_shift_total.astype(jnp.bfloat16), "dp").astype(jnp.float32),
        lax.psum(down_total.astype(jnp.bfloat16), "dp").astype(jnp.float32),
    )
    vectors = lax.psum((totals["gain"], totals["shift"], totals["down_shift"]), ("dp", "tensor"))
    return (
        outputs[None],
        input_grad[None],
        summed[0][None],
        summed[1][None],
        summed[2][None],
        summed[3][None],
        summed[4][None],
        summed[5][None],
        vectors[2][None],
        vectors[0][None],
        vectors[1][None],
    )


def split_lanes(rows):
    return lax.broadcasted_iota(jnp.int32, (rows, 2 * HS), 1) < HS


def swap_halves(tile):
    return jnp.concatenate([tile[:, HS:], tile[:, :HS]], axis=1)


def pair_of(packed, left):
    first, second, third = (packed[:, :LANES], packed[:, LANES : 2 * LANES], packed[:, 2 * LANES :])
    queries = jnp.where(left, first, second)
    keys_in = jnp.where(left, swap_halves(first), swap_halves(third))
    values = jnp.where(left, second, third)
    return (queries, keys_in, values)


def key_limit(position, length, causal):
    return jnp.minimum(length, jnp.where(causal != 0, position + 1, position.dtype.type(1 << 20)))


def attend_pair(scalars, queries_at, keys_in, values, mixed_ref, lse_ref, slots, left):
    length, causal = (scalars[0], scalars[1])
    zero = jnp.zeros((), keys_in.dtype)
    key_halves = (jnp.where(left, keys_in, zero), jnp.where(left, zero, keys_in))
    value_halves = (jnp.where(left, values, zero), jnp.where(left, zero, values))
    left_block = split_lanes(ROWS)
    key_pos = lax.broadcasted_iota(jnp.int32, (ROWS, slots), 1)

    def block(index, carry):
        first_row = pl.multiple_of(index * ROWS, ROWS)
        queries = queries_at(first_row)
        position = first_row + lax.broadcasted_iota(jnp.int32, (ROWS, 1), 0)
        allowed = key_pos < key_limit(position, length, causal)
        total, tops, sums = (None, [], [])
        for half in range(2):
            raw = lax.dot_general(
                queries, key_halves[half], COL_DIMS, preferred_element_type=jnp.float32
            )
            scores = jnp.where(allowed, raw * SCALE, NEG)
            top = jnp.max(scores, axis=1, keepdims=True)
            expo = jnp.exp(scores - top)
            tops.append(top)
            sums.append(jnp.sum(expo, axis=1, keepdims=True))
            part = jnp.dot(
                expo.astype(jnp.bfloat16), value_halves[half], preferred_element_type=jnp.float32
            )
            total = part if half == 0 else total + part
        norm = jnp.where(left_block, sums[0], sums[1])
        mixed_ref[pl.ds(first_row, ROWS), :] = (total / norm).astype(jnp.bfloat16)
        logs = jnp.where(left_block, tops[0] + jnp.log(sums[0]), tops[1] + jnp.log(sums[1]))
        lse_ref[0, :, pl.ds(first_row, ROWS)] = jnp.transpose(logs)[HS - 4 : HS + 4]
        return carry

    lax.fori_loop(0, slots // ROWS, block, 0)


def self_forward_kernel(scalars, packed_ref, mixed_ref, lse_ref, queries_ref):
    slots = packed_ref.shape[0]
    left = split_lanes(slots)
    queries, keys_in, values = pair_of(packed_ref[...], left)
    queries_ref[...] = queries
    attend_pair(
        scalars,
        lambda row: queries_ref[pl.ds(row, ROWS), :],
        keys_in,
        values,
        mixed_ref,
        lse_ref,
        slots,
        left,
    )


def cross_forward_kernel(scalars, query_ref, key_ref, value_ref, mixed_ref, lse_ref):
    slots = query_ref.shape[0]
    attend_pair(
        scalars,
        lambda row: query_ref[pl.ds(row, ROWS), :],
        key_ref[...],
        value_ref[...],
        mixed_ref,
        lse_ref,
        slots,
        split_lanes(slots),
    )


def attend_pair_back(
    scalars, queries_at, keys_in, values, mixed_ref, grad_ref, lse_ref, put_query, key_acc, value_acc
):
    length, causal = (scalars[0], scalars[1])
    slots = keys_in.shape[0]
    left = split_lanes(slots)
    left_block = split_lanes(ROWS)
    zero = jnp.zeros((), keys_in.dtype)
    key_halves = (jnp.where(left, keys_in, zero), jnp.where(left, zero, keys_in))
    value_halves = (jnp.where(left, values, zero), jnp.where(left, zero, values))
    key_pos = lax.broadcasted_iota(jnp.int32, (slots, ROWS), 0)
    key_acc[...] = jnp.zeros_like(key_acc)
    value_acc[...] = jnp.zeros_like(value_acc)

    def block(index, carry):
        first_row = pl.multiple_of(index * ROWS, ROWS)
        queries = queries_at(first_row)
        grads = grad_ref[pl.ds(first_row, ROWS), :]
        mixed = mixed_ref[pl.ds(first_row, ROWS), :]
        product = jnp.transpose(grads.astype(jnp.float32) * mixed.astype(jnp.float32))
        position = first_row + lax.broadcasted_iota(jnp.int32, (1, ROWS), 1)
        allowed = key_pos < key_limit(position, length, causal)
        logs = lse_ref[0, :, pl.ds(first_row, ROWS)]
        query_total = None
        for half in range(2):
            mine = left_block if half == 0 else jnp.logical_not(left_block)
            query_half = jnp.where(mine, queries, zero)
            grad_half = jnp.where(mine, grads, zero)
            raw = lax.dot_general(
                key_halves[half], queries, COL_DIMS, preferred_element_type=jnp.float32
            )
            scores = jnp.where(allowed, raw * SCALE, NEG)
            probs = jnp.exp(scores - logs[3 + half : 4 + half])
            grad_probs = lax.dot_general(
                value_halves[half], grads, COL_DIMS, preferred_element_type=jnp.float32
            )
            delta = jnp.sum(product[half * HS : half * HS + HS], axis=0, keepdims=True)
            grad_raw = (probs * (grad_probs - delta) * SCALE).astype(jnp.bfloat16)
            value_acc[...] += jnp.dot(
                probs.astype(jnp.bfloat16), grad_half, preferred_element_type=jnp.float32
            )
            key_acc[...] += jnp.dot(grad_raw, query_half, preferred_element_type=jnp.float32)
            part = lax.dot_general(
                grad_raw, key_halves[half], ROW_DIMS, preferred_element_type=jnp.float32
            )
            query_total = part if half == 0 else query_total + part
        put_query(first_row, query_total.astype(jnp.bfloat16))
        return carry

    lax.fori_loop(0, slots // ROWS, block, 0)


def self_backward_kernel(
    scalars, packed_ref, mixed_ref, grad_ref, lse_ref, out_ref, queries_ref, dq_ref, key_acc, value_acc
):
    slots = packed_ref.shape[0]
    left = split_lanes(slots)
    queries, keys_in, values = pair_of(packed_ref[...], left)
    queries_ref[...] = queries

    def put_query(row, block):
        dq_ref[pl.ds(row, ROWS), :] = block

    attend_pair_back(
        scalars,
        lambda row: queries_ref[pl.ds(row, ROWS), :],
        keys_in,
        values,
        mixed_ref,
        grad_ref,
        lse_ref,
        put_query,
        key_acc,
        value_acc,
    )
    grad_query = dq_ref[...]
    grad_key = swap_halves(key_acc[...].astype(jnp.bfloat16))
    grad_value = value_acc[...].astype(jnp.bfloat16)
    out_ref[:, :LANES] = jnp.where(left, grad_query, grad_key)
    out_ref[:, LANES : 2 * LANES] = jnp.where(left, grad_value, grad_query)
    out_ref[:, 2 * LANES :] = jnp.where(left, grad_key, grad_value)


def cross_backward_kernel(
    scalars,
    query_ref,
    key_ref,
    value_ref,
    mixed_ref,
    grad_ref,
    lse_ref,
    dq_ref,
    dkv_ref,
    key_acc,
    value_acc,
):
    def put_query(row, block):
        dq_ref[pl.ds(row, ROWS), :] = block

    attend_pair_back(
        scalars,
        lambda row: query_ref[pl.ds(row, ROWS), :],
        key_ref[...],
        value_ref[...],
        mixed_ref,
        grad_ref,
        lse_ref,
        put_query,
        key_acc,
        value_acc,
    )
    dkv_ref[0] = key_acc[...].astype(jnp.bfloat16)
    dkv_ref[1] = value_acc[...].astype(jnp.bfloat16)


def head_call(kernel, scalars, pairs, blocks, outs, scratch, lse_in, lse_out):
    slots = blocks[0][0].shape[0]

    def spec(width, shift):
        return pl.BlockSpec((slots, width), lambda pair, *_: (0, pair + shift))

    lse_spec = pl.BlockSpec((1, 8, slots), lambda pair, *_: (pair, 0, 0))
    in_specs = [spec(width, shift) for _, width, shift in blocks]
    operands = [array for array, _, _ in blocks]
    if lse_in is not None:
        in_specs.append(lse_spec)
        operands.append(lse_in)
    out_specs, out_shape = ([], [])
    for stacked, width in outs:
        if stacked:
            out_specs.append(pl.BlockSpec((2, slots, width), lambda pair, *_: (0, 0, pair)))
            out_shape.append(jax.ShapeDtypeStruct((2, slots, pairs * width), jnp.bfloat16))
        else:
            out_specs.append(spec(width, 0))
            out_shape.append(jax.ShapeDtypeStruct((slots, pairs * width), jnp.bfloat16))
    if lse_out:
        out_specs.append(lse_spec)
        out_shape.append(jax.ShapeDtypeStruct((pairs, 8, slots), jnp.float32))
    products = 2 if lse_in is None else 5
    return pl.pallas_call(
        kernel,
        grid_spec=pltpu.PrefetchScalarGridSpec(
            num_scalar_prefetch=1,
            grid=(pairs,),
            in_specs=in_specs,
            out_specs=out_specs,
            scratch_shapes=scratch,
        ),
        out_shape=out_shape,
        compiler_params=pltpu.CompilerParams(
            dimension_semantics=("arbitrary",), vmem_limit_bytes=48 * 1024 * 1024
        ),
        cost_estimate=pl.CostEstimate(
            flops=products * pairs * slots * slots * LANES * 16,
            bytes_accessed=2 * sum(array.size for array in operands),
            transcendentals=2 * pairs * slots * slots,
        ),
    )(scalars, *operands)


def self_attention(scalars, packed):
    slots = packed.shape[0]
    return head_call(
        self_forward_kernel,
        scalars,
        packed.shape[1] // (3 * LANES),
        [(packed, 3 * LANES, 0)],
        [(False, LANES)],
        [pltpu.VMEM((slots, LANES), jnp.bfloat16)],
        None,
        True,
    )


def cross_attention(scalars, queries, key_values):
    pairs = queries.shape[1] // LANES
    return head_call(
        cross_forward_kernel,
        scalars,
        pairs,
        [(queries, LANES, 0), (key_values, LANES, 0), (key_values, LANES, pairs)],
        [(False, LANES)],
        [],
        None,
        True,
    )


def self_attention_back(scalars, packed, mixed, grads, lse):
    slots = packed.shape[0]
    return head_call(
        self_backward_kernel,
        scalars,
        packed.shape[1] // (3 * LANES),
        [(packed, 3 * LANES, 0), (mixed, LANES, 0), (grads, LANES, 0)],
        [(False, 3 * LANES)],
        [
            pltpu.VMEM((slots, LANES), jnp.bfloat16),
            pltpu.VMEM((slots, LANES), jnp.bfloat16),
            pltpu.VMEM((slots, LANES), jnp.float32),
            pltpu.VMEM((slots, LANES), jnp.float32),
        ],
        lse,
        False,
    )[0]


def cross_attention_back(scalars, queries, key_values, mixed, grads, lse):
    slots = queries.shape[0]
    pairs = queries.shape[1] // LANES
    return head_call(
        cross_backward_kernel,
        scalars,
        pairs,
        [
            (queries, LANES, 0),
            (key_values, LANES, 0),
            (key_values, LANES, pairs),
            (mixed, LANES, 0),
            (grads, LANES, 0),
        ],
        [(False, LANES), (True, LANES)],
        [pltpu.VMEM((slots, LANES), jnp.float32), pltpu.VMEM((slots, LANES), jnp.float32)],
        lse,
        False,
    )


def rows_nt(rows, weight_rows):
    return lax.dot_general(rows, weight_rows, COL_DIMS, preferred_element_type=jnp.float32)


def rows_nn(rows, weight_rows):
    return jnp.dot(rows, weight_rows, preferred_element_type=jnp.float32)


def rows_tn(left_rows, right_rows):
    return lax.dot_general(left_rows, right_rows, ROW_DIMS, preferred_element_type=jnp.float32)


def low(values):
    return values.astype(jnp.bfloat16)


def gelu_and_slope(values):
    square = values * values
    bend = jnp.tanh(GELU_C * values * (1.0 + 0.044715 * square))
    rise = GELU_C * (1.0 + 3 * 0.044715 * square)
    gate = 0.5 * (1.0 + bend)
    return (values * gate, gate + 0.5 * values * (1.0 - bend * bend) * rise)


def after(value, *earlier):
    return lax.optimization_barrier((value, earlier))[0]


def around(value, distance):
    count = lax.axis_size("tensor")
    return lax.ppermute(value, "tensor", [(i, (i + distance) % count) for i in range(count)])


def partner(value, bit):
    return lax.ppermute(value, "dp", [(i, i ^ bit) for i in range(lax.axis_size("dp"))])


def exchange(blocks, store_type):
    count = lax.axis_size("tensor")
    place = lax.axis_index("tensor")
    arrived = [lax.dynamic_index_in_dim(blocks, place, 0)]
    for distance in range(1, count):
        sent = lax.dynamic_index_in_dim(blocks, (place + distance) % count, 0)
        arrived.append(around(sent, distance))
    placed = jnp.zeros(blocks.shape, store_type)
    for distance in range(count):
        block = arrived[distance].astype(store_type)
        placed = lax.dynamic_update_slice_in_dim(placed, block, (place - distance) % count, 0)
    return placed


def mesh_place():
    return (
        lax.axis_index("dp"),
        lax.axis_index("tensor"),
        lax.axis_size("tensor"),
    )


def greet(unit, place, count):
    partners = [{"tensor": lax.rem(place + d, count)} for d in range(1, count)]
    partners.append({"dp": lax.rem(unit + 2, 4)})
    partners.append({"dp": unit + 1 - 2 * lax.rem(unit, 2)})
    barrier = pltpu.get_barrier_semaphore()
    for partner_id in partners:
        pl.semaphore_signal(barrier, inc=1, device_id=partner_id, device_id_type=MESH)
    pl.semaphore_wait(barrier, len(partners))
    return partners


def remote(source, target, send_sem, recv_sem, device_id):
    return pltpu.make_async_remote_copy(
        src_ref=source,
        dst_ref=target,
        send_sem=send_sem,
        recv_sem=recv_sem,
        device_id=device_id,
        device_id_type=MESH,
    )


def at_slot(ref, axis, slot):
    return ref.at[slot] if axis == 0 else ref.at[:, slot]


def gather_kernel(axes, *refs):
    groups = len(axes)
    blocks, own, across = (refs[0], refs[1 : 1 + groups], refs[1 + groups : 1 + 2 * groups])
    rest = refs[1 + 2 * groups :]
    rows, near, far = (rest[0], rest[1 : 1 + groups], rest[1 + groups : 1 + 2 * groups])
    local_sem, block_send, block_recv, ring_send, ring_recv = rest[1 + 2 * groups : 6 + 2 * groups]
    side_send, side_recv, core_send, core_recv = rest[6 + 2 * groups :]
    unit, place, count = mesh_place()
    partners = greet(unit, place, count)
    right, side, core = (partners[0], partners[-2], partners[-1])
    started = []

    def begin(copy):
        copy.start()
        started.append(copy)
        return copy

    local = []

    def begin_local(source, target, index):
        copy = pltpu.make_async_copy(source, target, local_sem.at[index])
        copy.start()
        local.append(copy)

    def slot(refs_of, group, index):
        return at_slot(refs_of[group], axes[group], index)

    def hop(group, step):
        source = own[group] if step == 1 else slot(near, group, step - 1)
        return begin(
            remote(
                source,
                slot(near, group, step),
                ring_send.at[group, step - 1],
                ring_recv.at[group, step - 1],
                right,
            )
        )

    def to_side(group, step):
        return begin(
            remote(
                slot(near, group, step),
                slot(near, group, count + step),
                side_send.at[group, step - 1],
                side_recv.at[group, step - 1],
                side,
            )
        )

    def to_core(group, index, source):
        return begin(
            remote(
                source,
                slot(far, group, index),
                core_send.at[group, index],
                core_recv.at[group, index],
                core,
            )
        )

    hops = {(0, 1): hop(0, 1)}
    block_copies = []
    for distance in range(1, count):
        block_copies.append(
            begin(
                remote(
                    blocks.at[lax.rem(place + distance, count)],
                    rows.at[place],
                    block_send.at[distance - 1],
                    block_recv.at[distance - 1],
                    partners[distance - 1],
                )
            )
        )
    for group in range(1, groups):
        hops[group, 1] = hop(group, 1)
    begin_local(blocks.at[place], rows.at[place], 0)
    cores, sides = ([], {})
    for group in range(groups):
        begin_local(own[group], slot(near, group, 0), 1 + 2 * group)
        begin_local(across[group], slot(near, group, count), 2 + 2 * group)
        cores.append(to_core(group, 0, own[group]))
        cores.append(to_core(group, count, across[group]))
    for step in range(1, count):
        for group in range(groups):
            hops[group, step].wait_recv()
            if step + 1 < count:
                hops[group, step + 1] = hop(group, step + 1)
            sides[group, step] = to_side(group, step)
            cores.append(to_core(group, step, slot(near, group, step)))
            earlier = (group, step - 1)
            if step > 1:
                sides[earlier].wait_recv()
                cores.append(to_core(group, count + step - 1, slot(near, group, count + step - 1)))
    for group in range(groups):
        last = count - 1
        sides[group, last].wait_recv()
        cores.append(to_core(group, count + last, slot(near, group, count + last)))
    for copy in block_copies:
        copy.wait_recv()
    for copy in cores:
        copy.wait_recv()
    for copy in local:
        copy.wait()
    for copy in started:
        copy.wait_send()


def gather_all(blocks, own, across, axes):
    count = lax.axis_size("tensor")
    groups = len(axes)
    anywhere = pl.BlockSpec(memory_space=pl.ANY)

    def spread_shape(array, axis):
        shape = list(array.shape)
        shape.insert(axis, 2 * count)
        return jax.ShapeDtypeStruct(tuple(shape), array.dtype)

    halves = [spread_shape(array, axis) for array, axis in zip(own, axes)]
    dma = pltpu.SemaphoreType.DMA
    made = pl.pallas_call(
        functools.partial(gather_kernel, axes),
        in_specs=[anywhere] * (1 + 2 * groups),
        out_specs=[anywhere] * (1 + 2 * groups),
        out_shape=[jax.ShapeDtypeStruct(blocks.shape, blocks.dtype)] + halves + halves,
        scratch_shapes=[
            dma((1 + 2 * groups,)),
            dma((count - 1,)),
            dma((count - 1,)),
            dma((groups, count - 1)),
            dma((groups, count - 1)),
            dma((groups, count - 1)),
            dma((groups, count - 1)),
            dma((groups, 2 * count)),
            dma((groups, 2 * count)),
        ],
        compiler_params=pltpu.CompilerParams(collective_id=0, has_side_effects=True),
    )(blocks, *own, *across)
    return (made[0], made[1 : 1 + groups], made[1 + groups :])


def reduce_kernel(axes, depths, *refs):
    groups = len(axes)
    blocks, small = refs[:2]
    near, far = (refs[2 : 2 + groups], refs[2 + groups : 2 + 2 * groups])
    rest = refs[2 + 2 * groups :]
    rows, small_out, out = (rest[0], rest[1], rest[2 : 2 + groups])
    (
        near_buf,
        sums,
        side_in,
        ring_in,
        pair,
        other,
        small_core,
        small_side,
        small_far,
        near_sem,
        core_send,
        core_recv,
        side_send,
        side_recv,
        ring_send,
        ring_recv,
        pair_send,
        pair_recv,
        last_send,
        last_recv,
        out_sem,
        block_sem,
        block_send,
        block_recv,
        tiny_send,
        tiny_recv,
    ) = rest[2 + groups :]
    unit, place, count = mesh_place()
    partners = greet(unit, place, count)
    side, core = (partners[-2], partners[-1])
    units = (
        unit,
        lax.rem(unit + 2, 4),
        unit + 1 - 2 * lax.rem(unit, 2),
        lax.rem(unit + 3 - 2 * lax.rem(unit, 2), 4),
    )
    sends = []

    def begin(copy):
        copy.start()
        sends.append(copy)
        return copy

    chunks = []
    for group in range(groups):
        if axes[group] == 0:
            for first in range(0, depths[group], CHUNK):
                chunks.append((group, (pl.ds(first, CHUNK),)))
        else:
            for part in range(2):
                for first in range(0, depths[group], CHUNK):
                    chunks.append((group, (part, pl.ds(first, CHUNK))))

    def rows_of(ref, chunk, slots):
        group, place_in = chunk
        if axes[group] == 0:
            return ref[group].at[slots, place_in[0]]
        return ref[group].at[place_in[0], slots, place_in[1]]

    everything = slice(None)
    block_copies = []
    for distance in range(1, count):
        block_copies.append(
            begin(
                remote(
                    blocks.at[lax.rem(place + distance, count)],
                    rows.at[place],
                    block_send.at[distance - 1],
                    block_recv.at[distance - 1],
                    partners[distance - 1],
                )
            )
        )
    own_block = pltpu.make_async_copy(blocks.at[place], rows.at[place], block_sem.at[0])
    own_block.start()
    tiny = begin(remote(small, small_core, tiny_send.at[0], tiny_recv.at[0], core))
    state = {}
    outs = []

    def wide(value):
        return value.astype(jnp.float32)

    def enter(index):
        chunk = chunks[index]
        copy = pltpu.make_async_copy(
            rows_of(near, chunk, everything), near_buf.at[index % 3], near_sem.at[index]
        )
        copy.start()
        state["near", index] = copy
        state["core", index] = begin(
            remote(
                rows_of(far, chunk, everything),
                sums.at[index],
                core_send.at[index],
                core_recv.at[index],
                core,
            )
        )

    def first_sum(index):
        state["near", index].wait()
        state["core", index].wait_recv()
        upper = pl.ds(count, count)
        total = wide(near_buf[index % 3, upper]) + wide(sums[index, upper])
        sums[index, upper] = total.astype(jnp.bfloat16)
        state["side", index] = begin(
            remote(
                sums.at[index, upper],
                side_in.at[index],
                side_send.at[index],
                side_recv.at[index],
                side,
            )
        )

    def second_sum(index):
        state["side", index].wait_recv()
        lower = pl.ds(0, count)
        total = wide(near_buf[index % 3, lower]) + wide(sums[index, lower]) + wide(side_in[index])
        sums[index, lower] = total.astype(jnp.bfloat16)
        for distance in range(1, count):
            state["ring", index, distance] = begin(
                remote(
                    sums.at[index, distance],
                    ring_in.at[index, distance - 1],
                    ring_send.at[index, distance - 1],
                    ring_recv.at[index, distance - 1],
                    partners[count - distance - 1],
                )
            )

    def third_sum(index):
        total = wide(sums[index, 0])
        for distance in range(1, count):
            state["ring", index, distance].wait_recv()
            total = total + wide(ring_in[index, distance - 1])
        pair[index, 0] = total.astype(jnp.bfloat16)
        state["pair", index] = begin(
            remote(
                pair.at[index, 0],
                pair.at[index, 1],
                pair_send.at[index],
                pair_recv.at[index],
                side,
            )
        )

    def spread_pair(index):
        state["pair", index].wait_recv()
        state["last", index] = begin(
            remote(pair.at[index], other.at[index], last_send.at[index], last_recv.at[index], core)
        )

    def leave(index):
        state["last", index].wait_recv()
        chunk = chunks[index]
        found = (pair.at[index, 0], pair.at[index, 1], other.at[index, 0], other.at[index, 1])
        for bits in range(4):
            copy = pltpu.make_async_copy(
                found[bits], rows_of(out, chunk, units[bits]), out_sem.at[index, bits]
            )
            copy.start()
            outs.append(copy)

    stages = (enter, first_sum, second_sum, third_sum, spread_pair, leave)
    for tick in range(len(chunks) + len(stages) - 1):
        for number, stage in enumerate(stages):
            if 0 <= tick - number < len(chunks):
                stage(tick - number)
        if tick == 2:
            tiny.wait_recv()
            small_core[...] += small[...]
            tiny = begin(remote(small_core, small_side, tiny_send.at[1], tiny_recv.at[1], side))
        if tick == 4:
            tiny.wait_recv()
            small_side[...] += small_core[...]
            tiny = [
                begin(
                    remote(
                        small_side,
                        small_far.at[distance - 1],
                        tiny_send.at[1 + distance],
                        tiny_recv.at[1 + distance],
                        partners[distance - 1],
                    )
                )
                for distance in range(1, count)
            ]
        if tick == 6:
            total = small_side[...]
            for distance in range(1, count):
                tiny[distance - 1].wait_recv()
                total = total + small_far[distance - 1]
            small_out[...] = total
    for copy in block_copies:
        copy.wait_recv()
    own_block.wait()
    for copy in outs:
        copy.wait()
    for copy in sends:
        copy.wait_send()


def reduce_all(blocks, small, near, far, axes):
    count = lax.axis_size("tensor")
    units = lax.axis_size("dp")
    groups = len(axes)
    anywhere = pl.BlockSpec(memory_space=pl.ANY)
    vmem = pl.BlockSpec(memory_space=pltpu.VMEM)
    width = blocks.shape[-1]
    depths = [array.shape[axis + 1] for array, axis in zip(near, axes)]
    total = sum(depth * (1 + axis) for depth, axis in zip(depths, axes)) // CHUNK

    def own_shape(array, axis):
        shape = list(array.shape)
        shape[axis] = units
        return jax.ShapeDtypeStruct(tuple(shape), array.dtype)

    dma = pltpu.SemaphoreType.DMA
    bf16 = jnp.bfloat16
    made = pl.pallas_call(
        functools.partial(reduce_kernel, axes, depths),
        in_specs=[anywhere, vmem] + [anywhere] * (2 * groups),
        out_specs=[anywhere, vmem] + [anywhere] * groups,
        out_shape=[
            jax.ShapeDtypeStruct(blocks.shape, blocks.dtype),
            jax.ShapeDtypeStruct(small.shape, small.dtype),
        ]
        + [own_shape(array, axis) for array, axis in zip(near, axes)],
        scratch_shapes=[
            pltpu.VMEM((3, 2 * count, CHUNK, width), bf16),
            pltpu.VMEM((total, 2 * count, CHUNK, width), bf16),
            pltpu.VMEM((total, count, CHUNK, width), bf16),
            pltpu.VMEM((total, count - 1, CHUNK, width), bf16),
            pltpu.VMEM((total, 2, CHUNK, width), bf16),
            pltpu.VMEM((total, 2, CHUNK, width), bf16),
            pltpu.VMEM(small.shape, small.dtype),
            pltpu.VMEM(small.shape, small.dtype),
            pltpu.VMEM((count - 1,) + small.shape, small.dtype),
            dma((total,)),
            dma((total,)),
            dma((total,)),
            dma((total,)),
            dma((total,)),
            dma((total, count - 1)),
            dma((total, count - 1)),
            dma((total,)),
            dma((total,)),
            dma((total,)),
            dma((total,)),
            dma((total, 4)),
            dma((1,)),
            dma((count - 1,)),
            dma((count - 1,)),
            dma((count + 1,)),
            dma((count + 1,)),
        ],
        compiler_params=pltpu.CompilerParams(
            collective_id=1, has_side_effects=True, vmem_limit_bytes=56 * 1024 * 1024
        ),
    )(blocks, small, *near, *far)
    return (made[0], made[1], made[2:])


def sequence_body(
    inputs,
    lengths,
    cotangent,
    qkv_weight,
    attn_out_weight,
    cross_weight,
    ffn_in_weight,
    ffn_in_bias,
    ffn_out_weight,
    ffn_out_bias,
    norm_gain,
    norm_bias,
):
    section = lax.axis_index("section")
    tensor_index = lax.axis_index("tensor")
    tensor_count = lax.axis_size("tensor")
    unit = lax.axis_index("dp")
    units = lax.axis_size("dp")
    decoder = section == 1
    alpha = jnp.where(decoder, ALPHA_DEC, ALPHA_ENC).astype(jnp.float32)
    batches, shard_rows, width = (inputs.shape[1], inputs.shape[2], inputs.shape[3])
    slots = batches * shard_rows
    gains = norm_gain[0].astype(jnp.float32)
    shifts = norm_bias[0].astype(jnp.float32)
    down_shift = ffn_out_bias[0].astype(jnp.float32)

    def unit_of(array, axis, bits):
        size = array.shape[axis] // units
        piece = lax.dynamic_slice_in_dim(array, (unit ^ bits) * size, size, axis)
        return piece.T if axis == 1 else piece

    def units_of(bits):
        return (
            unit_of(qkv_weight[0], 1, bits),
            unit_of(attn_out_weight[0], 0, bits),
            unit_of(ffn_in_weight[0], 1, bits),
            unit_of(ffn_out_weight[0], 0, bits),
            unit_of(cross_weight[0], 1, bits).reshape(2, HS, width),
            jnp.broadcast_to(unit_of(ffn_in_bias[0], 0, bits)[None], (16, bias_size)),
        )

    bias_size = ffn_in_bias.shape[1] // units
    x, near, far = gather_all(inputs[0], units_of(0), units_of(2), (0, 0, 0, 0, 1, 0))
    x = x.reshape(slots, width)
    qkv_rows, out_rows, in_rows, down_rows = [
        tuple(array.reshape(-1, width) for array in halves)
        for halves in zip(near[:4], far[:4])
    ]
    cross_rows = tuple(array.reshape(2, -1, width) for array in (near[4], far[4]))
    in_shift = tuple(
        array[:, 0].reshape(-1).astype(jnp.float32) for array in (near[5], far[5])
    )

    source_len = lax.dynamic_index_in_dim(lengths[0, :, 0], tensor_index, 0, keepdims=False)
    target_len = lax.dynamic_index_in_dim(lengths[1, :, 0], tensor_index, 0, keepdims=False)
    own_len = jnp.where(decoder, target_len, source_len)
    self_scalars = jnp.stack([own_len, decoder.astype(jnp.int32)])
    cross_scalars = jnp.stack([source_len, jnp.zeros_like(source_len)])
    sides = (0, 1)

    qkv = [low(rows_nt(x, qkv_rows[side])) for side in sides]
    mixed, lse_self = zip(*[self_attention(self_scalars, qkv[side]) for side in sides])
    attn_sum = rows_nn(mixed[0], out_rows[0]) + rows_nn(mixed[1], out_rows[1])
    resid_a, norm_a, factor_a = layer_norm(
        alpha * x.astype(jnp.float32) + attn_sum, gains[0], shifts[0]
    )
    a_low = low(resid_a)
    half_width = width // 2
    half_zero = jnp.zeros((slots, half_width), jnp.bfloat16)

    def zeros_like_of(branch):
        shapes = jax.eval_shape(branch)
        return lambda: jax.tree.map(lambda leaf: jnp.zeros(leaf.shape, leaf.dtype), shapes)

    def dec_query():
        return tuple(low(rows_nt(a_low, cross_rows[side][0])) for side in sides)

    query_sent = lax.cond(decoder, dec_query, zeros_like_of(dec_query))
    query_held = [lax.ppermute(piece, "section", [(1, 0)]) for piece in query_sent]

    def feed(rows_low, rows_wide, gain_row, shift_row):
        hidden, slopes, total = ([], [], alpha * rows_wide + down_shift)
        for side in sides:
            made, slope = gelu_and_slope(rows_nt(rows_low, in_rows[side]) + in_shift[side])
            hidden.append(low(made))
            slopes.append(low(slope))
        for side in sides:
            total = total + rows_nn(hidden[side], down_rows[side])
        return (tuple(hidden), tuple(slopes)) + layer_norm(total, gain_row, shift_row)

    def feed_back(grad_sum, slopes):
        grad_low = low(grad_sum)
        grad_pre = tuple(
            low(rows_nt(grad_low, down_rows[side]) * slopes[side].astype(jnp.float32))
            for side in sides
        )
        total = alpha * grad_sum
        for side in sides:
            total = total + rows_nn(grad_pre[side], in_rows[side])
        return (grad_low, grad_pre, total)

    def enc_feed():
        hidden, slopes, memory, norm_y, factor_y = feed(a_low, resid_a, gains[2], shifts[2])
        memory_low = low(memory)
        key_values = tuple(
            low(rows_nt(memory_low, cross_rows[side].reshape(-1, width))) for side in sides
        )
        return (hidden, slopes, memory_low, norm_y, factor_y, key_values)

    hidden_e, slopes_e, memory_low, norm_e, factor_e, key_values = lax.cond(
        decoder, zeros_like_of(enc_feed), enc_feed
    )

    mixed_c, lse_c, mixed_held = ([], [], [])
    for side in sides:

        def enc_mix():
            return tuple(cross_attention(cross_scalars, query_held[side], key_values[side]))

        mix_made, lse_made = lax.cond(decoder, zeros_like_of(enc_mix), enc_mix)
        mixed_c.append(mix_made)
        lse_c.append(lse_made)
        mixed_held.append(lax.ppermute(mix_made, "section", [(0, 1)]))

    own_pos = lax.broadcasted_iota(jnp.int32, (slots, 1), 0)
    cotangent_rows = exchange(after(cotangent, qkv[0]), jnp.bfloat16).reshape(slots, width)

    def dec_middle():
        crossed = rows_nn(mixed_held[0], cross_rows[0][1]) + rows_nn(
            mixed_held[1], cross_rows[1][1]
        )
        resid_c, norm_c, factor_c = layer_norm(alpha * resid_a + crossed, gains[1], shifts[1])
        c_low = low(resid_c)
        hidden, slopes, decoded, norm_y, factor_y = feed(c_low, resid_c, gains[2], shifts[2])
        grad_top = jnp.where(own_pos < target_len, cotangent_rows.astype(jnp.float32), 0.0)
        grad_y, gain_y, shift_y = norm_back(grad_top, norm_y, factor_y, gains[2])
        grad_low, grad_pre, grad_c = feed_back(grad_y, slopes)
        grad_mid, gain_c, shift_c = norm_back(grad_c, norm_c, factor_c, gains[1])
        mid_low = low(grad_mid)
        grad_mixed_c = tuple(low(rows_nt(mid_low, cross_rows[side][1])) for side in sides)
        return (
            low(decoded),
            hidden,
            c_low,
            grad_low,
            grad_pre,
            grad_mid,
            mid_low,
            grad_mixed_c,
            jnp.stack([gain_c, gain_y, shift_c, shift_y, jnp.sum(grad_y, axis=0)]),
        )

    (
        decoded_low,
        hidden_d,
        c_low,
        grad_low_d,
        grad_pre_d,
        grad_mid,
        mid_low,
        grad_mixed_c,
        vectors_d,
    ) = lax.cond(decoder, dec_middle, zeros_like_of(dec_middle))
    grad_mixed_held = [lax.ppermute(piece, "section", [(1, 0)]) for piece in grad_mixed_c]
    grad_query_held, grad_kv = ([], [])
    for side in sides:

        def enc_cross():
            return tuple(
                cross_attention_back(
                    cross_scalars,
                    query_held[side],
                    key_values[side],
                    mixed_c[side],
                    grad_mixed_held[side],
                    lse_c[side],
                )
            )

        query_made, kv_made = lax.cond(decoder, zeros_like_of(enc_cross), enc_cross)
        grad_kv.append(kv_made)
        grad_query_held.append(lax.ppermute(query_made, "section", [(0, 1)]))

    def enc_back():
        grad_memory = None
        for side in sides:
            for part in range(2):
                term = rows_nn(grad_kv[side][part], cross_rows[side][part])
                grad_memory = term if grad_memory is None else grad_memory + term
        grad_y, gain_y, shift_y = norm_back(grad_memory, norm_e, factor_e, gains[2])
        grad_low, grad_pre, grad_a = feed_back(grad_y, slopes_e)
        zero_row = jnp.zeros_like(gain_y)
        rows = jnp.stack([zero_row, gain_y, zero_row, shift_y, jnp.sum(grad_y, axis=0)])
        return (grad_low, grad_pre, grad_a, rows)

    def dec_back():
        grad_a = alpha * grad_mid
        for side in sides:
            grad_a = grad_a + rows_nn(grad_query_held[side], cross_rows[side][0])
        return (grad_low_d, grad_pre_d, grad_a, vectors_d)

    grad_low, grad_pre, grad_a, vectors = lax.cond(decoder, dec_back, enc_back)

    outputs = exchange(
        after(jnp.where(decoder, decoded_low, memory_low), grad_a).reshape(
            batches, shard_rows, width
        ),
        jnp.bfloat16,
    )

    def cross_grads(side):
        def enc():
            return jnp.stack([low(rows_tn(grad_kv[side][part], memory_low)) for part in range(2)])

        def dec():
            return jnp.stack(
                [
                    low(rows_tn(grad_query_held[side], a_low)),
                    low(rows_tn(mixed_held[side], mid_low)),
                ]
            )

        return lax.cond(decoder, dec, enc)

    def down_grads(side):
        return lax.cond(
            decoder,
            lambda: low(rows_tn(hidden_d[side], grad_low)),
            lambda: low(rows_tn(hidden_e[side], grad_low)),
        )

    def in_grads(side):
        return lax.cond(
            decoder,
            lambda: low(rows_tn(grad_pre[side], c_low)),
            lambda: low(rows_tn(grad_pre[side], a_low)),
        )

    def total_of(made):
        far = made(1)
        return (made(0), far)

    down_made, in_made, cross_made = (
        total_of(down_grads),
        total_of(in_grads),
        total_of(cross_grads),
    )

    grad_r, gain_a, shift_a = norm_back(grad_a, norm_a, factor_a, gains[0])
    r_low = low(grad_r)
    grad_mixed = [low(rows_nt(r_low, out_rows[side])) for side in sides]
    out_made = total_of(lambda side: low(rows_tn(mixed[side], r_low)))
    grad_qkv = [
        self_attention_back(self_scalars, qkv[side], mixed[side], grad_mixed[side], lse_self[side])
        for side in sides
    ]
    grad_x = alpha * grad_r
    for side in sides:
        grad_x = grad_x + rows_nn(grad_qkv[side], qkv_rows[side])
    qkv_made = total_of(lambda side: low(rows_tn(grad_qkv[side], x)))

    slot_bits = jnp.asarray([0, 2, 1, 3], jnp.int32)[:, None]
    slot_unit = unit ^ slot_bits
    slot_tensor = (tensor_index - lax.iota(jnp.int32, tensor_count)[None]) % tensor_count
    slot_index = (slot_tensor * units + slot_unit).reshape(-1)
    hot = (slot_index[None, :] == lax.iota(jnp.int32, slot_index.shape[0])[:, None]).astype(
        jnp.float32
    )
    shift_rel = jnp.concatenate(
        [jnp.sum(grad_pre[side].astype(jnp.float32), axis=0) for side in sides]
    ).reshape(-1, bias_size)
    shift_abs = jnp.dot(hot, shift_rel, precision=lax.Precision.HIGHEST).reshape(-1, width)
    small = jnp.concatenate([jnp.stack([gain_a, shift_a]), vectors, shift_abs])
    small = jnp.pad(small, ((0, -small.shape[0] % 8), (0, 0)))
    made = (qkv_made, out_made, in_made, down_made, cross_made)
    axes = (0, 0, 0, 0, 1)

    def by_slot(array, axis):
        shape = list(array.shape)
        shape[axis : axis + 1] = [2 * tensor_count, shape[axis] // (2 * tensor_count)]
        return array.reshape(shape)

    input_rows, small, grads = reduce_all(
        low(grad_x).reshape(batches, shard_rows, width),
        small,
        [by_slot(halves[0], axis) for halves, axis in zip(made, axes)],
        [by_slot(halves[1], axis) for halves, axis in zip(made, axes)],
        axes,
    )
    input_grad = input_rows.astype(jnp.float32)
    qkv_grad, out_grad, in_grad, down_grad, cross_grad = [
        array.astype(jnp.float32) for array in grads
    ]
    cross_grad = jnp.swapaxes(cross_grad, 0, 1)
    in_shift_grad = lax.dynamic_index_in_dim(
        small[7:11].reshape(tensor_count, -1), tensor_index, 0, keepdims=False
    )

    def columns(ordered):
        return ordered.reshape(-1, width).T[None]

    return (
        outputs[None],
        input_grad[None],
        columns(qkv_grad),
        out_grad.reshape(1, -1, width),
        columns(cross_grad),
        columns(in_grad),
        in_shift_grad[None],
        down_grad.reshape(1, -1, width),
        small[6][None],
        small[jnp.asarray([0, 2, 3])][None],
        small[jnp.asarray([1, 4, 5])][None],
    )


def solution(mesh):
    placed = (
        P("section", None, ("dp", "tensor"), None),
        P(None, None, "dp"),
        P(None, ("dp", "tensor"), None),
        P("section", None, "tensor"),
        P("section", "tensor", None),
        P("section", None, "tensor"),
        P("section", None, "tensor"),
        P("section", "tensor"),
        P("section", "tensor", None),
        P("section", None),
        P("section", None, None),
        P("section", None, None),
    )
    returned = (
        P("section", None, ("dp", "tensor"), None),
        P("section", None, ("dp", "tensor"), None),
        P("section", None, "tensor"),
        P("section", "tensor", None),
        P("section", None, "tensor"),
        P("section", None, "tensor"),
        P("section", "tensor"),
        P("section", "tensor", None),
        P("section", None),
        P("section", None, None),
        P("section", None, None),
    )
    sizes = dict(mesh.shape)

    def whole(*arrays):
        batches, sequences = arrays[1].shape[1:]
        heads = arrays[3].shape[2] // (3 * HS)
        group = sizes["dp"] * sizes["tensor"]
        one_each = batches == sizes["tensor"] and sizes["dp"] == 4 and sequences == sizes["dp"] and heads % group == 0
        chosen = sequence_body if one_each else body
        return jax.shard_map(
            chosen, mesh=mesh, in_specs=placed, out_specs=returned, check_vma=False
        )(*arrays)

    return whole
```

```python
import functools

import jax
import jax.numpy as jnp
from jax import lax
from jax.experimental import pallas as pl
from jax.experimental.pallas import tpu as pltpu
from jax.sharding import PartitionSpec as P

HS = 64
QBLOCK = 512


ALPHA_ENC = 0.81 * (100.0**5) ** (1.0 / 16.0)
ALPHA_DEC = (3.0 * 100.0) ** 0.25
EPS = 1e-05
NEG = -1e30
ROW_DIMS = (((0,), (0,)), ((), ()))
COL_DIMS = (((1,), (1,)), ((), ()))
LANES = 2 * HS
ROWS = 256
CHUNK = 32
BLOCK = 512
MESH = pl.DeviceIdType.MESH
SCALE = HS ** (-0.5)
GELU_C = (2.0 / 3.141592653589793) ** 0.5


def from_behind(block, axis, distance):
    devices = range(lax.axis_size(axis))
    route = [(i - distance, i) for i in devices if i - distance in devices]
    return lax.ppermute(block, axis, route)


def layer_norm(values, gain_row, shift_row):
    centered = values - jnp.mean(values, axis=-1, keepdims=True)
    factor = lax.rsqrt(jnp.mean(centered * centered, axis=-1, keepdims=True) + EPS)
    normed = centered * factor
    return (normed * gain_row + shift_row, normed, factor)


def norm_back(gradient, normed, factor, gain_row):
    scaled = gradient * gain_row
    centred = (
        scaled
        - jnp.mean(scaled, axis=-1, keepdims=True)
        - normed * jnp.mean(scaled * normed, axis=-1, keepdims=True)
    )
    return (centred * factor, jnp.sum(gradient * normed, axis=0), jnp.sum(gradient, axis=0))


def visible(first_row, row_count, key_count, seq_lengths, causal):
    key_pos = lax.broadcasted_iota(jnp.int32, (1, row_count, key_count), 2)
    query_pos = first_row + lax.broadcasted_iota(jnp.int32, (1, row_count, key_count), 1)
    inside = key_pos < seq_lengths[:, None, None]
    return inside & ((key_pos <= query_pos) | jnp.logical_not(causal))


def attend(queries, keys_in, values, seq_lengths, causal):
    key_count = queries.shape[1]
    score_scale = queries.shape[3] ** (-0.5)
    row_block = min(QBLOCK, key_count)
    mixed_parts, lse_parts = ([], [])
    for first_row in range(0, key_count, row_block):
        allowed = visible(first_row, row_block, key_count, seq_lengths, causal)
        raw_scores = jnp.einsum(
            "bqhe,bkhe->bhqk",
            queries[:, first_row : first_row + row_block],
            keys_in,
            preferred_element_type=jnp.float32,
        )
        scores = jnp.where(allowed[:, None], raw_scores * score_scale, NEG)
        row_max = jnp.max(scores, axis=-1, keepdims=True)
        expo_vals = jnp.exp(scores - row_max)
        row_total = jnp.sum(expo_vals, axis=-1, keepdims=True)
        weights = (expo_vals / row_total).astype(jnp.bfloat16)
        mixed_block = jnp.einsum(
            "bhqk,bkhe->bqhe", weights, values, preferred_element_type=jnp.float32
        )
        mixed_parts.append(mixed_block.astype(jnp.bfloat16))
        lse_parts.append(row_max + jnp.log(row_total))
    return (jnp.concatenate(mixed_parts, axis=1), jnp.concatenate(lse_parts, axis=2))


def attend_back(grad_mixed, queries, keys_in, values, log_totals, seq_lengths, causal):
    key_count = queries.shape[1]
    score_scale = queries.shape[3] ** (-0.5)
    row_block = min(QBLOCK, key_count)
    query_parts = []
    grad_keys = jnp.zeros(keys_in.shape, jnp.float32)
    grad_values = jnp.zeros(values.shape, jnp.float32)
    for first_row in range(0, key_count, row_block):
        query_part = queries[:, first_row : first_row + row_block]
        grad_part = grad_mixed[:, first_row : first_row + row_block]
        allowed = visible(first_row, row_block, key_count, seq_lengths, causal)
        raw_scores = jnp.einsum(
            "bqhe,bkhe->bhqk", query_part, keys_in, preferred_element_type=jnp.float32
        )
        scores = jnp.where(allowed[:, None], raw_scores * score_scale, NEG)
        probs = jnp.exp(scores - log_totals[:, :, first_row : first_row + row_block])
        grad_probs = jnp.einsum(
            "bqhe,bkhe->bhqk", grad_part, values, preferred_element_type=jnp.float32
        )
        grad_scores = probs * (grad_probs - jnp.sum(probs * grad_probs, axis=-1, keepdims=True))
        grad_raw = (grad_scores * score_scale).astype(jnp.bfloat16)
        query_parts.append(
            jnp.einsum("bhqk,bkhe->bqhe", grad_raw, keys_in, preferred_element_type=jnp.float32)
        )
        grad_keys = grad_keys + jnp.einsum(
            "bhqk,bqhe->bkhe", grad_raw, query_part, preferred_element_type=jnp.float32
        )
        grad_values = grad_values + jnp.einsum(
            "bhqk,bqhe->bkhe",
            probs.astype(jnp.bfloat16),
            grad_part,
            preferred_element_type=jnp.float32,
        )
    return (jnp.concatenate(query_parts, axis=1), grad_keys, grad_values)


def ffn_forward(rows_in, in_proj, in_shift, down_proj):
    pre_act = jnp.dot(rows_in, in_proj, preferred_element_type=jnp.float32) + in_shift
    hidden = jax.nn.gelu(pre_act).astype(jnp.bfloat16)
    return (pre_act, jnp.dot(hidden, down_proj, preferred_element_type=jnp.float32))


def ffn_backward(grad_in, rows_in, pre_act, in_proj, down_proj):
    activated, slope_back = jax.vjp(jax.nn.gelu, pre_act)
    hidden = activated.astype(jnp.bfloat16)
    grad_down = lax.dot_general(hidden, grad_in, ROW_DIMS, preferred_element_type=jnp.float32)
    grad_hidden = lax.dot_general(grad_in, down_proj, COL_DIMS, preferred_element_type=jnp.float32)
    grad_pre = slope_back(grad_hidden)[0].astype(jnp.bfloat16)
    grad_shift = jnp.sum(grad_pre.astype(jnp.float32), axis=0)
    grad_inner = lax.dot_general(rows_in, grad_pre, ROW_DIMS, preferred_element_type=jnp.float32)
    grad_rows_out = lax.dot_general(grad_pre, in_proj, COL_DIMS, preferred_element_type=jnp.float32)
    return (grad_rows_out, grad_inner, grad_shift, grad_down)


def gather_rows(shard):
    return lax.all_gather(shard, "tensor", axis=0, tiled=True)


def sum_rows(partial_value):
    return lax.psum_scatter(partial_value, "tensor", scatter_dimension=0, tiled=True)


def ffn_input_rows(shard):
    return lax.all_gather(shard, "tensor", axis=0, tiled=True)


def ffn_sum_rows(partial_value):
    return lax.psum_scatter(
        partial_value.astype(jnp.bfloat16), "tensor", scatter_dimension=0, tiled=True
    ).astype(jnp.float32)


def grad_rows(shard):
    return lax.all_gather(shard, "tensor", axis=0, tiled=True)


def grad_sums(partial_value):
    return lax.psum_scatter(
        partial_value.astype(jnp.bfloat16), "tensor", scatter_dimension=0, tiled=True
    ).astype(jnp.float32)


def ffn_grad_rows(shard):
    return lax.all_gather(shard, "tensor", axis=0, tiled=True)


def ffn_grad_sums(partial_value):
    return lax.psum_scatter(
        partial_value.astype(jnp.bfloat16), "tensor", scatter_dimension=0, tiled=True
    ).astype(jnp.float32)


def body(
    inputs,
    lengths,
    cotangent,
    qkv_weight,
    attn_out_weight,
    cross_weight,
    ffn_in_weight,
    ffn_in_bias,
    ffn_out_weight,
    ffn_out_bias,
    norm_gain,
    norm_bias,
):
    tensor_count = lax.axis_size("tensor")
    section = lax.axis_index("section")
    tensor_index = lax.axis_index("tensor")
    decoder = section == 1
    alpha = jnp.where(decoder, ALPHA_DEC, ALPHA_ENC).astype(jnp.float32)
    batches, shard_rows, width = (inputs.shape[1], inputs.shape[2], inputs.shape[3])
    seq_count = lengths.shape[2]
    full_rows = shard_rows * tensor_count
    slots = full_rows // seq_count
    qkv_proj = qkv_weight[0]
    head_local = qkv_proj.shape[1] // (3 * HS)
    head_cols = head_local * HS
    out_proj = attn_out_weight[0]
    cross_proj = cross_weight[0]
    cross_split = cross_proj.reshape(width, head_local, 2, HS)
    first_cols = cross_split[:, :, 0].reshape(width, head_cols)
    second_cols = cross_split[:, :, 1].reshape(width, head_cols)
    in_proj = ffn_in_weight[0]
    in_shift = ffn_in_bias[0].astype(jnp.float32)
    down_proj = ffn_out_weight[0]
    hidden_width = in_proj.shape[1]
    down_shift = ffn_out_bias[0].astype(jnp.float32)
    gains = norm_gain[0].astype(jnp.float32)
    shifts = norm_bias[0].astype(jnp.float32)
    own_lengths = lax.dynamic_index_in_dim(lengths, section, 0, keepdims=False)
    source_lengths = lengths[0]
    row_index = tensor_index * shard_rows + lax.iota(jnp.int32, shard_rows)
    row_seq = row_index // slots
    row_pos = row_index % slots
    seq_ids = lax.iota(jnp.int32, seq_count)
    lse_shape = (seq_count, head_local, slots, 1)

    def zeros_float(shape):
        return jnp.zeros(shape, jnp.float32)

    def zeros_low(shape):
        return jnp.zeros(shape, jnp.bfloat16)

    def to_heads(flat_rows):
        return flat_rows.reshape(seq_count, slots, flat_rows.shape[1] // HS, HS)

    def to_rows(split_rows):
        return split_rows.reshape(full_rows, -1)

    def cross_forward(query_rows, kv_source, source_len):
        kv_split = kv_source.reshape(seq_count, slots, head_local, 2, HS)
        query_c = jnp.dot(query_rows, first_cols, preferred_element_type=jnp.float32).astype(
            jnp.bfloat16
        )
        mixed_c, lse_cross = attend(
            to_heads(query_c), kv_split[:, :, :, 0], kv_split[:, :, :, 1], source_len, False
        )
        mixed_c = to_rows(mixed_c)
        partial_value = lax.dot_general(
            mixed_c, second_cols, COL_DIMS, preferred_element_type=jnp.float32
        )
        return (query_c, mixed_c, lse_cross, partial_value)

    kv_held = zeros_low((full_rows, 2 * head_cols))
    kv_ticks, kept_ticks, out_ticks = ([], [], [])
    for tick_index in range(batches + 1):
        batch = jnp.clip(tick_index - section, 0, batches - 1)
        x_shard = lax.dynamic_index_in_dim(inputs[0], batch, 0, keepdims=False)
        own_len = lax.dynamic_index_in_dim(own_lengths, batch, 0, keepdims=False)
        source_len = lax.dynamic_index_in_dim(source_lengths, batch, 0, keepdims=False)
        x_full = gather_rows(x_shard)
        qkv = jnp.dot(x_full, qkv_proj, preferred_element_type=jnp.float32).astype(jnp.bfloat16)
        qkv_split = qkv.reshape(seq_count, slots, head_local, 3, HS)
        mixed, lse_self = attend(
            qkv_split[:, :, :, 0], qkv_split[:, :, :, 1], qkv_split[:, :, :, 2], own_len, decoder
        )
        mixed = to_rows(mixed)
        attn_sum = sum_rows(jnp.dot(mixed, out_proj, preferred_element_type=jnp.float32))
        resid_a, norm_a, factor_a = layer_norm(
            alpha * x_shard.astype(jnp.float32) + attn_sum, gains[0], shifts[0]
        )
        a_shard = resid_a.astype(jnp.bfloat16)
        a_full = gather_rows(a_shard)

        def enc_second():
            hidden_made, partial_value = ffn_forward(a_full, in_proj, in_shift, down_proj)
            return (
                hidden_made,
                zeros_low((full_rows, head_cols)),
                zeros_low((full_rows, head_cols)),
                zeros_float(lse_shape),
                partial_value,
            )

        def dec_second():
            query_c, mixed_c, lse_cross, partial_value = cross_forward(a_full, kv_held, source_len)
            return (
                zeros_float((full_rows, hidden_width)),
                query_c,
                mixed_c,
                lse_cross,
                partial_value,
            )

        hidden_enc, query_c, mixed_c, lse_cross, partial_value = lax.cond(
            decoder, dec_second, enc_second
        )
        second_sum = sum_rows(partial_value)
        resid_ye, norm_ye, factor_ye = layer_norm(
            alpha * resid_a + second_sum + down_shift, gains[2], shifts[2]
        )
        resid_c, norm_c, factor_c = layer_norm(alpha * resid_a + second_sum, gains[1], shifts[1])
        wide_rows = ffn_input_rows(jnp.where(decoder, resid_c, resid_ye).astype(jnp.bfloat16))

        def enc_third():
            kv_made = jnp.dot(wide_rows, cross_proj, preferred_element_type=jnp.float32).astype(
                jnp.bfloat16
            )
            return (
                kv_made,
                zeros_float((full_rows, hidden_width)),
                zeros_float((full_rows, width)),
            )

        def dec_third():
            hidden_made, partial_made = ffn_forward(wide_rows, in_proj, in_shift, down_proj)
            return (zeros_low((full_rows, 2 * head_cols)), hidden_made, partial_made)

        kv_out, hidden_dec, partial_third = lax.cond(decoder, dec_third, enc_third)
        third_sum = ffn_sum_rows(partial_third)
        resid_yd, norm_yd, factor_yd = layer_norm(
            alpha * resid_c + third_sum + down_shift, gains[2], shifts[2]
        )
        resid_y = jnp.where(decoder, resid_yd, resid_ye)
        norm_y = jnp.where(decoder, norm_yd, norm_ye)
        factor_y = jnp.where(decoder, factor_yd, factor_ye)
        hidden = jnp.where(decoder, hidden_dec, hidden_enc)
        ffn_rows = jnp.where(decoder, wide_rows, a_full)
        y_shard = resid_y.astype(jnp.bfloat16)
        kv_held = from_behind(kv_out, "section", 1)
        kv_ticks.append(kv_held)
        out_ticks.append(y_shard)
        kept_ticks.append(
            dict(
                x_rows=x_full,
                qkv=qkv,
                mixed=mixed,
                lse_self=lse_self,
                a_rows=a_full,
                kv_rows=wide_rows,
                ffn_rows=ffn_rows,
                hidden=hidden,
                query_c=query_c,
                mixed_c=mixed_c,
                lse_cross=lse_cross,
                norm_a=norm_a,
                factor_a=factor_a,
                norm_c=norm_c,
                factor_c=factor_c,
                norm_y=norm_y,
                factor_y=factor_y,
            )
        )
    kept_all = jax.tree.map(lambda *leaves: jnp.stack(leaves), *kept_ticks)
    kv_stack = jnp.stack(kv_ticks)
    outputs = lax.dynamic_slice_in_dim(jnp.stack(out_ticks), section, batches, 0)
    totals = dict(
        qkv=zeros_float(qkv_proj.shape),
        outer=zeros_float(out_proj.shape),
        cross=zeros_float(cross_proj.shape),
        inner=zeros_float(in_proj.shape),
        inner_shift=zeros_float(in_shift.shape),
        down=zeros_float(down_proj.shape),
        down_shift=zeros_float(down_shift.shape),
        gain=zeros_float(gains.shape),
        shift=zeros_float(shifts.shape),
    )
    zero_ffn = (
        zeros_float(in_proj.shape),
        zeros_float(in_shift.shape),
        zeros_float(down_proj.shape),
    )
    zero_cross = zeros_float((width, 2 * head_cols))
    dkv_held = zeros_low((full_rows, 2 * head_cols))
    grad_ticks = []
    for tick_index in range(batches + 1):
        batch_raw = batches - tick_index - section
        live = (batch_raw >= 0) & (batch_raw < batches)
        batch = jnp.clip(batch_raw, 0, batches - 1)
        kept = jax.tree.map(
            lambda leaf_value: lax.dynamic_index_in_dim(
                leaf_value, batch + section, 0, keepdims=False
            ),
            kept_all,
        )
        own_len = lax.dynamic_index_in_dim(own_lengths, batch, 0, keepdims=False)
        source_len = lax.dynamic_index_in_dim(source_lengths, batch, 0, keepdims=False)
        kv_now = lax.dynamic_index_in_dim(kv_stack, batch, 0, keepdims=False)
        kv_split = kv_now.reshape(seq_count, slots, head_local, 2, HS)
        own_rows = jnp.sum(
            jnp.where(row_seq[:, None] == seq_ids[None, :], own_len[None, :], 0), axis=1
        )
        grad_top = lax.dynamic_index_in_dim(cotangent, batch, 0, keepdims=False).astype(jnp.float32)
        grad_top = jnp.where((row_pos < own_rows)[:, None], grad_top, 0.0)
        grad_r3d, gain_yd, shift_yd = norm_back(
            grad_top, kept["norm_y"], kept["factor_y"], gains[2]
        )
        dkv_now = dkv_held

        def kv_back():
            partial_value = lax.dot_general(
                dkv_now, cross_proj, COL_DIMS, preferred_element_type=jnp.float32
            )
            grad_cross_enc = lax.dot_general(
                kept["kv_rows"], dkv_now, ROW_DIMS, preferred_element_type=jnp.float32
            )
            return (partial_value, grad_cross_enc)

        def cross_back(grad_full):
            grad_mixed_c = jnp.dot(
                grad_full, second_cols, preferred_element_type=jnp.float32
            ).astype(jnp.bfloat16)
            grad_second = lax.dot_general(
                grad_full, kept["mixed_c"], ROW_DIMS, preferred_element_type=jnp.float32
            )
            grad_qc, grad_kc, grad_vc = attend_back(
                to_heads(grad_mixed_c),
                to_heads(kept["query_c"]),
                kv_split[:, :, :, 0],
                kv_split[:, :, :, 1],
                kept["lse_cross"],
                source_len,
                False,
            )
            grad_qc = to_rows(grad_qc).astype(jnp.bfloat16)
            grad_first = lax.dot_general(
                kept["a_rows"], grad_qc, ROW_DIMS, preferred_element_type=jnp.float32
            )
            partial_value = lax.dot_general(
                grad_qc, first_cols, COL_DIMS, preferred_element_type=jnp.float32
            )
            grad_kv = (
                jnp.stack([grad_kc, grad_vc], axis=3)
                .astype(jnp.bfloat16)
                .reshape(full_rows, 2 * head_cols)
            )
            grad_cross_dec = jnp.stack(
                [
                    grad_first.reshape(width, head_local, HS),
                    grad_second.reshape(width, head_local, HS),
                ],
                axis=2,
            ).reshape(width, 2 * head_cols)
            return (partial_value, grad_cross_dec, grad_kv)

        first_full = grad_rows(jnp.where(decoder, grad_r3d, 0.0).astype(jnp.bfloat16))

        def enc_first():
            partial_value, grad_cross_enc = kv_back()
            return (partial_value, grad_cross_enc) + zero_ffn

        def dec_first():
            partial_value, inner_made, shift_made, down_made = ffn_backward(
                first_full, kept["ffn_rows"], kept["hidden"], in_proj, down_proj
            )
            return (partial_value, zero_cross, inner_made, shift_made, down_made)

        partial_one, cross_enc, inner_one, inner_shift_one, down_one = lax.cond(
            decoder, dec_first, enc_first
        )
        first_sum = grad_sums(partial_one)
        grad_r3e, gain_ye, shift_ye = norm_back(
            first_sum, kept["norm_y"], kept["factor_y"], gains[2]
        )
        grad_r2, gain_c, shift_c = norm_back(
            alpha * grad_r3d + first_sum, kept["norm_c"], kept["factor_c"], gains[1]
        )
        grad_r3 = jnp.where(decoder, grad_r3d, grad_r3e)
        gain_y = jnp.where(decoder, gain_yd, gain_ye)
        shift_y = jnp.where(decoder, shift_yd, shift_ye)
        middle_grad = jnp.where(decoder, grad_r2, grad_r3e)
        second_full = ffn_grad_rows(middle_grad.astype(jnp.bfloat16))

        def enc_second():
            partial_value, inner_made, shift_made, down_made = ffn_backward(
                second_full, kept["ffn_rows"], kept["hidden"], in_proj, down_proj
            )
            return (
                partial_value,
                inner_made,
                shift_made,
                down_made,
                zero_cross,
                zeros_low((full_rows, 2 * head_cols)),
            )

        def dec_second():
            partial_value, grad_cross_dec, grad_kv_made = cross_back(second_full)
            return (partial_value,) + zero_ffn + (grad_cross_dec, grad_kv_made)

        partial_two, inner_two, inner_shift_two, down_two, cross_dec, grad_kv = lax.cond(
            decoder, dec_second, enc_second
        )
        grad_a = alpha * middle_grad + ffn_grad_sums(partial_two)
        dkv_held = from_behind(grad_kv, "section", -1)
        grad_r1, gain_a, shift_a = norm_back(grad_a, kept["norm_a"], kept["factor_a"], gains[0])
        attn_full = grad_rows(grad_r1.astype(jnp.bfloat16))
        grad_mixed = lax.dot_general(
            attn_full, out_proj, COL_DIMS, preferred_element_type=jnp.float32
        ).astype(jnp.bfloat16)
        grad_outer = lax.dot_general(
            kept["mixed"], attn_full, ROW_DIMS, preferred_element_type=jnp.float32
        )
        qkv_split = kept["qkv"].reshape(seq_count, slots, head_local, 3, HS)
        grad_q, grad_k, grad_v = attend_back(
            to_heads(grad_mixed),
            qkv_split[:, :, :, 0],
            qkv_split[:, :, :, 1],
            qkv_split[:, :, :, 2],
            kept["lse_self"],
            own_len,
            decoder,
        )
        grad_qkv = (
            jnp.stack([grad_q, grad_k, grad_v], axis=3)
            .astype(jnp.bfloat16)
            .reshape(full_rows, 3 * head_cols)
        )
        grad_qkv_proj = lax.dot_general(
            kept["x_rows"], grad_qkv, ROW_DIMS, preferred_element_type=jnp.float32
        )
        grad_x = alpha * grad_r1 + grad_sums(
            lax.dot_general(grad_qkv, qkv_proj, COL_DIMS, preferred_element_type=jnp.float32)
        )
        grad_ticks.append(grad_x)
        gain_step = jnp.stack([gain_a, jnp.where(decoder, gain_c, 0.0), gain_y])
        shift_step = jnp.stack([shift_a, jnp.where(decoder, shift_c, 0.0), shift_y])
        steps = dict(
            qkv=grad_qkv_proj,
            outer=grad_outer,
            cross=cross_enc + cross_dec,
            inner=inner_one + inner_two,
            inner_shift=inner_shift_one + inner_shift_two,
            down=down_one + down_two,
            down_shift=jnp.sum(grad_r3, axis=0),
            gain=gain_step,
            shift=shift_step,
        )
        totals = {name: totals[name] + jnp.where(live, steps[name], 0.0) for name in totals}
    input_grad = lax.dynamic_slice_in_dim(jnp.stack(grad_ticks[::-1]), section, batches, 0)
    inner_total, inner_shift_total, down_total = (
        totals["inner"],
        totals["inner_shift"],
        totals["down"],
    )
    summed = (
        lax.psum(totals["qkv"].astype(jnp.bfloat16), "dp").astype(jnp.float32),
        lax.psum(totals["outer"].astype(jnp.bfloat16), "dp").astype(jnp.float32),
        lax.psum(totals["cross"].astype(jnp.bfloat16), "dp").astype(jnp.float32),
        lax.psum(inner_total.astype(jnp.bfloat16), "dp").astype(jnp.float32),
        lax.psum(inner_shift_total.astype(jnp.bfloat16), "dp").astype(jnp.float32),
        lax.psum(down_total.astype(jnp.bfloat16), "dp").astype(jnp.float32),
    )
    vectors = lax.psum((totals["gain"], totals["shift"], totals["down_shift"]), ("dp", "tensor"))
    return (
        outputs[None],
        input_grad[None],
        summed[0][None],
        summed[1][None],
        summed[2][None],
        summed[3][None],
        summed[4][None],
        summed[5][None],
        vectors[2][None],
        vectors[0][None],
        vectors[1][None],
    )


def lanes_of(rows):
    return lax.broadcasted_iota(jnp.int32, (rows, LANES), 1)


def swap_halves(tile):
    return pltpu.roll(tile, HS, 1)


def pair_of(packed, left):
    first, second, third = (packed[:, :LANES], packed[:, LANES : 2 * LANES], packed[:, 2 * LANES :])
    swap = lambda tile: jnp.concatenate([tile[:, HS:], tile[:, :HS]], axis=1)
    queries = jnp.where(left, first, second)
    keys_in = jnp.where(left, swap(first), swap(third))
    values = jnp.where(left, second, third)
    return (queries, keys_in, values)


def wide(value):
    return value.astype(jnp.float32)


def low(values):
    return values.astype(jnp.bfloat16)


def half_tiles(tile, fill_right, fill_left, left):
    return (jnp.where(left, tile, fill_right), jnp.where(left, fill_left, tile))


def key_tiles(keys_in, length, ones):
    slots = keys_in.shape[0]
    lane = lanes_of(slots)
    hidden = lax.broadcasted_iota(jnp.int32, (slots, LANES), 0) >= length
    left = lane < HS

    def fill(start):
        outside = jnp.where((lane == start) & hidden, NEG, 0.0)
        return jnp.where((lane > start) & (lane <= start + ones), 1.0, outside)

    first, second = half_tiles(wide(keys_in), fill(HS), fill(0), left)
    return (low(first), low(second))


def attend_forward(length, causal, queries_ref, key_refs, value_refs, mixed_ref, lse_ref):
    slots = queries_ref.shape[0]
    lane = lanes_of(ROWS)
    left = lane < HS

    def block(first_row, key_count, triangle):
        queries = wide(queries_ref[pl.ds(first_row, ROWS), :]) * SCALE
        query_halves = half_tiles(
            queries, jnp.where(lane == HS, 1.0, 0.0), jnp.where(lane == 0, 1.0, 0.0), left
        )
        totals, tops = ([], [])
        for half in range(2):
            scores = lax.dot_general(
                low(query_halves[half]),
                key_refs[half][pl.ds(0, key_count), :],
                COL_DIMS,
                preferred_element_type=jnp.float32,
            )
            if triangle:
                column = lax.broadcasted_iota(jnp.int32, (ROWS, key_count), 1)
                row = first_row + lax.broadcasted_iota(jnp.int32, (ROWS, key_count), 0)
                scores = jnp.where(column <= row, scores, NEG)
            top = jnp.max(scores, axis=1, keepdims=True)
            tops.append(top)
            totals.append(
                jnp.dot(
                    low(jnp.exp(scores - top)),
                    value_refs[half][pl.ds(0, key_count), :],
                    preferred_element_type=jnp.float32,
                )
            )
        norm = swap_halves(jnp.where(left, totals[1], totals[0]))
        mixed_ref[pl.ds(first_row, ROWS), :] = low(jnp.where(left, totals[0], totals[1]) / norm)
        logs = jnp.where(left, tops[0], tops[1]) + jnp.log(norm)
        lse_ref[pl.ds(first_row, ROWS), :] = swap_halves(logs)

    @pl.when(causal == 0)
    def _():
        def step(index, carry):
            block(pl.multiple_of(index * ROWS, ROWS), slots, False)
            return carry

        lax.fori_loop(0, slots // ROWS, step, 0)

    @pl.when(causal != 0)
    def _():
        for first_row in range(0, slots, ROWS):
            block(first_row, first_row + ROWS, True)


def fill_forward(length, keys_in, values, key_refs, value_refs):
    left = lanes_of(keys_in.shape[0]) < HS
    for ref, tile in zip(key_refs, key_tiles(keys_in, length, 0)):
        ref[...] = tile
    one = jnp.ones((), values.dtype)
    for ref, tile in zip(value_refs, half_tiles(values, one, one, left)):
        ref[...] = tile


def self_forward_kernel(scalars, packed_ref, mixed_ref, lse_ref, queries_ref, k0, k1, v0, v1):
    left = lanes_of(packed_ref.shape[0]) < HS
    queries, keys_in, values = pair_of(packed_ref[...], left)
    queries_ref[...] = queries
    fill_forward(scalars[0], keys_in, values, (k0, k1), (v0, v1))
    attend_forward(scalars[0], scalars[1], queries_ref, (k0, k1), (v0, v1), mixed_ref, lse_ref)


def cross_forward_kernel(
    scalars, query_ref, key_ref, value_ref, mixed_ref, lse_ref, k0, k1, v0, v1
):
    fill_forward(scalars[0], key_ref[...], value_ref[...], (k0, k1), (v0, v1))
    attend_forward(scalars[0], 0, query_ref, (k0, k1), (v0, v1), mixed_ref, lse_ref)


def attend_backward(
    causal, queries_ref, key_refs, plain_refs, value_refs, mixed_ref, grad_ref, lse_ref, outs
):
    dq_ref, key_acc, value_acc = outs
    slots = queries_ref.shape[0]
    lane = lanes_of(ROWS)
    left = lane < HS
    key_acc[...] = jnp.zeros_like(key_acc)
    value_acc[...] = jnp.zeros_like(value_acc)

    def extra(start, terms, one):
        filled = jnp.where(lane == start, one, 0.0)
        for number, term in enumerate(terms):
            filled = jnp.where(lane == start + 1 + number, -term, filled)
        return filled

    def parts(value, count):
        found = []
        for _ in range(count):
            found.append(wide(low(value)))
            value = value - found[-1]
        return found

    def block(first_row, key_count, triangle):
        rows = pl.ds(first_row, ROWS)
        keys = pl.ds(0, key_count)
        queries = wide(queries_ref[rows, :]) * SCALE
        grads = wide(grad_ref[rows, :])
        product = grads * wide(mixed_ref[rows, :])
        log_parts = parts(lse_ref[rows, :], 3)
        query_total, key_total, value_total = (None, None, None)
        for half in range(2):
            mine = left if half == 0 else jnp.logical_not(left)
            start = HS if half == 0 else 0
            delta = jnp.sum(jnp.where(mine, product, 0.0), axis=1, keepdims=True)
            query_aug = low(jnp.where(mine, queries, extra(start, log_parts, 1.0)))
            grad_aug = low(jnp.where(mine, grads, extra(start, parts(delta, 2), 0.0)))
            scores = lax.dot_general(
                key_refs[half][keys, :], query_aug, COL_DIMS, preferred_element_type=jnp.float32
            )
            probs = jnp.exp(scores)
            if triangle:
                key_pos = lax.broadcasted_iota(jnp.int32, (key_count, ROWS), 0)
                position = first_row + lax.broadcasted_iota(jnp.int32, (key_count, ROWS), 1)
                probs = jnp.where(key_pos <= position, probs, 0.0)
            grad_probs = lax.dot_general(
                value_refs[half][keys, :], grad_aug, COL_DIMS, preferred_element_type=jnp.float32
            )
            grad_raw = low(probs * grad_probs)
            value_part = jnp.dot(
                low(probs), low(jnp.where(mine, grads, 0.0)), preferred_element_type=jnp.float32
            )
            key_part = jnp.dot(
                grad_raw, low(jnp.where(mine, queries, 0.0)), preferred_element_type=jnp.float32
            )
            query_part = lax.dot_general(
                grad_raw, plain_refs[half][keys, :], ROW_DIMS, preferred_element_type=jnp.float32
            )
            if half == 0:
                query_total, key_total, value_total = (query_part, key_part, value_part)
            else:
                query_total = query_total + query_part
                key_total = key_total + key_part
                value_total = value_total + value_part
        value_acc[keys, :] += value_total
        key_acc[keys, :] += key_total
        dq_ref[rows, :] = low(query_total)

    @pl.when(causal == 0)
    def _():
        def step(index, carry):
            block(pl.multiple_of(index * ROWS, ROWS), slots, False)
            return carry

        lax.fori_loop(0, slots // ROWS, step, 0)

    @pl.when(causal != 0)
    def _():
        for first_row in range(0, slots, ROWS):
            block(first_row, first_row + ROWS, True)


def fill_backward(length, keys_in, values, key_refs, plain_refs, value_refs):
    lane = lanes_of(keys_in.shape[0])
    left = lane < HS
    for ref, tile in zip(key_refs, key_tiles(keys_in, length, 3)):
        ref[...] = tile
    zero = jnp.zeros((), jnp.float32)
    for ref, tile in zip(plain_refs, half_tiles(wide(keys_in) * SCALE, zero, zero, left)):
        ref[...] = low(tile)

    def ones(start):
        return jnp.where((lane > start) & (lane <= start + 2), 1.0, 0.0)

    for ref, tile in zip(value_refs, half_tiles(wide(values), ones(HS), ones(0), left)):
        ref[...] = low(tile)


def self_backward_kernel(
    scalars,
    packed_ref,
    mixed_ref,
    grad_ref,
    lse_ref,
    out_ref,
    queries_ref,
    dq_ref,
    key_acc,
    value_acc,
    k0,
    k1,
    p0,
    p1,
    v0,
    v1,
):
    slots = packed_ref.shape[0]
    left = lanes_of(slots) < HS
    queries, keys_in, values = pair_of(packed_ref[...], left)
    queries_ref[...] = queries
    fill_backward(scalars[0], keys_in, values, (k0, k1), (p0, p1), (v0, v1))
    attend_backward(
        scalars[1],
        queries_ref,
        (k0, k1),
        (p0, p1),
        (v0, v1),
        mixed_ref,
        grad_ref,
        lse_ref,
        (dq_ref, key_acc, value_acc),
    )
    grad_query = dq_ref[...]
    grad_key = low(swap_halves(key_acc[...]))
    grad_value = low(value_acc[...])
    out_ref[:, :LANES] = jnp.where(left, grad_query, grad_key)
    out_ref[:, LANES : 2 * LANES] = jnp.where(left, grad_value, grad_query)
    out_ref[:, 2 * LANES :] = jnp.where(left, grad_key, grad_value)


def cross_backward_kernel(
    scalars,
    query_ref,
    key_ref,
    value_ref,
    mixed_ref,
    grad_ref,
    lse_ref,
    dq_ref,
    dkv_ref,
    key_acc,
    value_acc,
    k0,
    k1,
    p0,
    p1,
    v0,
    v1,
):
    fill_backward(scalars[0], key_ref[...], value_ref[...], (k0, k1), (p0, p1), (v0, v1))
    attend_backward(
        0,
        query_ref,
        (k0, k1),
        (p0, p1),
        (v0, v1),
        mixed_ref,
        grad_ref,
        lse_ref,
        (dq_ref, key_acc, value_acc),
    )
    dkv_ref[:, :LANES] = low(key_acc[...])
    dkv_ref[:, LANES:] = low(value_acc[...])


def head_call(kernel, scalars, pairs, blocks, outs, scratch, products):
    slots = blocks[0][0].shape[0]

    def spec(width, shift, stride):
        return pl.BlockSpec((slots, width), lambda pair, *_: (0, stride * pair + shift))

    out_specs, out_shape = ([], [])
    for kind, width in outs:
        out_specs.append(spec(width, 0, 1))
        made = jnp.float32 if kind == "wide" else jnp.bfloat16
        out_shape.append(jax.ShapeDtypeStruct((slots, pairs * width), made))
    return pl.pallas_call(
        kernel,
        grid_spec=pltpu.PrefetchScalarGridSpec(
            num_scalar_prefetch=1,
            grid=(pairs,),
            in_specs=[spec(width, shift, stride) for _, width, shift, stride in blocks],
            out_specs=out_specs,
            scratch_shapes=[pltpu.VMEM((slots, LANES), kind) for kind in scratch],
        ),
        out_shape=out_shape,
        compiler_params=pltpu.CompilerParams(
            dimension_semantics=("arbitrary",), vmem_limit_bytes=48 * 1024 * 1024
        ),
        cost_estimate=pl.CostEstimate(
            flops=products * pairs * slots * slots * LANES * 16,
            bytes_accessed=2 * slots * pairs * sum(block[1] for block in blocks),
            transcendentals=2 * pairs * slots * slots,
        ),
    )(scalars, *[block[0] for block in blocks])


BF16 = jnp.bfloat16
F32 = jnp.float32


def self_attention(scalars, packed, first, pairs):
    return head_call(
        self_forward_kernel,
        scalars,
        pairs,
        [(packed, 3 * LANES, first, 1)],
        [("low", LANES), ("wide", LANES)],
        [BF16] * 5,
        2,
    )


def cross_attention(scalars, queries, key_values, first, pairs):
    return head_call(
        cross_forward_kernel,
        scalars,
        pairs,
        [
            (queries, LANES, 0, 1),
            (key_values, LANES, 2 * first, 2),
            (key_values, LANES, 2 * first + 1, 2),
        ],
        [("low", LANES), ("wide", LANES)],
        [BF16] * 4,
        2,
    )


def self_attention_back(scalars, packed, mixed, grads, lse, first, pairs):
    return head_call(
        self_backward_kernel,
        scalars,
        pairs,
        [
            (packed, 3 * LANES, first, 1),
            (mixed, LANES, first, 1),
            (grads, LANES, first, 1),
            (lse, LANES, first, 1),
        ],
        [("low", 3 * LANES)],
        [BF16, BF16, F32, F32] + [BF16] * 6,
        5,
    )[0]


def cross_attention_back(scalars, queries, key_values, mixed, grads, lse, first, pairs):
    return head_call(
        cross_backward_kernel,
        scalars,
        pairs,
        [
            (queries, LANES, 0, 1),
            (key_values, LANES, 2 * first, 2),
            (key_values, LANES, 2 * first + 1, 2),
            (mixed, LANES, 0, 1),
            (grads, LANES, 0, 1),
            (lse, LANES, 0, 1),
        ],
        [("low", LANES), ("low", 2 * LANES)],
        [F32, F32] + [BF16] * 6,
        5,
    )


def rows_nt(rows, weight_rows):
    return lax.dot_general(rows, weight_rows, COL_DIMS, preferred_element_type=jnp.float32)


def rows_nn(rows, weight_rows):
    return jnp.dot(rows, weight_rows, preferred_element_type=jnp.float32)


def rows_tn(left_rows, right_rows):
    return lax.dot_general(left_rows, right_rows, ROW_DIMS, preferred_element_type=jnp.float32)


def gelu_and_slope(values):
    square = values * values
    bend = jnp.tanh(GELU_C * values * (1.0 + 0.044715 * square))
    rise = GELU_C * (1.0 + 3 * 0.044715 * square)
    gate = 0.5 + 0.5 * bend
    return (values * gate, gate * (1.0 + values * (1.0 - bend) * rise))


def feed_kernel(
    alpha_ref,
    low_ref,
    wide_ref,
    in_ref,
    bias_ref,
    down_ref,
    down_shift_ref,
    gain_ref,
    shift_ref,
    hidden_ref,
    slope_ref,
    made_ref,
    norm_ref,
    factor_ref,
    acc,
):
    step = pl.program_id(0)
    slots = low_ref.shape[0]

    @pl.when(step == 0)
    def _():
        acc[...] = alpha_ref[0] * wide_ref[...] + down_shift_ref[...]

    for first in range(0, slots, ROWS):
        rows = pl.ds(first, ROWS)
        pre_act = rows_nt(low_ref[rows, :], in_ref[...]) + bias_ref[...]
        made, slope = gelu_and_slope(pre_act)
        hidden = low(made)
        hidden_ref[rows, :] = hidden
        slope_ref[rows, :] = low(slope)
        acc[rows, :] += rows_nn(hidden, down_ref[...])

    @pl.when(step == pl.num_programs(0) - 1)
    def _():
        for first in range(0, slots, ROWS):
            rows = pl.ds(first, ROWS)
            made, normed, factor = layer_norm(acc[rows, :], gain_ref[...], shift_ref[...])
            made_ref[rows, :] = low(made)
            norm_ref[rows, :] = normed
            factor_ref[rows, :] = factor


def whole_spec(shape):
    return pl.BlockSpec(shape, lambda *_: (0,) * len(shape))


def feed_call(alpha, rows_low, rows_wide, in_rows, in_shift, down_rows, down_shift, gain, shift):
    slots, width = rows_low.shape
    hidden = in_rows.shape[0]
    block = min(BLOCK, hidden)
    square, row = (whole_spec((slots, width)), whole_spec((1, width)))
    weight = pl.BlockSpec((block, width), lambda step: (step, 0))
    column = pl.BlockSpec((slots, block), lambda step: (0, step))
    return pl.pallas_call(
        feed_kernel,
        grid=(hidden // block,),
        in_specs=[
            pl.BlockSpec(memory_space=pltpu.SMEM),
            square,
            square,
            weight,
            pl.BlockSpec((1, block), lambda step: (0, step)),
            weight,
            row,
            row,
            row,
        ],
        out_specs=[column, column, square, square, whole_spec((slots, 1))],
        out_shape=[
            jax.ShapeDtypeStruct((slots, hidden), BF16),
            jax.ShapeDtypeStruct((slots, hidden), BF16),
            jax.ShapeDtypeStruct((slots, width), BF16),
            jax.ShapeDtypeStruct((slots, width), F32),
            jax.ShapeDtypeStruct((slots, 1), F32),
        ],
        scratch_shapes=[pltpu.VMEM((slots, width), F32)],
        compiler_params=pltpu.CompilerParams(
            dimension_semantics=("arbitrary",), vmem_limit_bytes=56 * 1024 * 1024
        ),
        cost_estimate=pl.CostEstimate(
            flops=4 * slots * width * hidden,
            bytes_accessed=4 * hidden * (width + slots),
            transcendentals=slots * hidden,
        ),
    )(alpha, rows_low, rows_wide, in_rows, in_shift, down_rows, down_shift, gain, shift)


def feed_back_kernel(
    alpha_ref, low_ref, wide_ref, in_ref, down_ref, slope_ref, pre_ref, bias_ref, total_ref, acc
):
    step = pl.program_id(0)
    slots = low_ref.shape[0]

    @pl.when(step == 0)
    def _():
        acc[...] = alpha_ref[0] * wide_ref[...]

    sums = None
    for first in range(0, slots, ROWS):
        rows = pl.ds(first, ROWS)
        made = rows_nt(low_ref[rows, :], down_ref[...]) * wide(slope_ref[rows, :])
        grad_pre = low(made)
        pre_ref[rows, :] = grad_pre
        part = jnp.sum(wide(grad_pre), axis=0, keepdims=True)
        sums = part if sums is None else sums + part
        acc[rows, :] += rows_nn(grad_pre, in_ref[...])
    bias_ref[...] = sums

    @pl.when(step == pl.num_programs(0) - 1)
    def _():
        total_ref[...] = acc[...]


def feed_back_call(alpha, grad_low, grad_wide, in_rows, down_rows, slopes):
    slots, width = grad_low.shape
    hidden = in_rows.shape[0]
    block = min(BLOCK, hidden)
    square = whole_spec((slots, width))
    weight = pl.BlockSpec((block, width), lambda step: (step, 0))
    column = pl.BlockSpec((slots, block), lambda step: (0, step))
    return pl.pallas_call(
        feed_back_kernel,
        grid=(hidden // block,),
        in_specs=[pl.BlockSpec(memory_space=pltpu.SMEM), square, square, weight, weight, column],
        out_specs=[column, pl.BlockSpec((1, block), lambda step: (0, step)), square],
        out_shape=[
            jax.ShapeDtypeStruct((slots, hidden), BF16),
            jax.ShapeDtypeStruct((1, hidden), F32),
            jax.ShapeDtypeStruct((slots, width), F32),
        ],
        scratch_shapes=[pltpu.VMEM((slots, width), F32)],
        compiler_params=pltpu.CompilerParams(
            dimension_semantics=("arbitrary",), vmem_limit_bytes=56 * 1024 * 1024
        ),
        cost_estimate=pl.CostEstimate(
            flops=4 * slots * width * hidden,
            bytes_accessed=4 * hidden * (width + slots),
            transcendentals=0,
        ),
    )(alpha, grad_low, grad_wide, in_rows, down_rows, slopes)


def norm_back_kernel(limit_ref, grad_ref, norm_ref, factor_ref, gain_ref, made_ref, low_ref, sums_ref):
    step = pl.program_id(0)
    rows = grad_ref.shape[0]
    position = step * rows + lax.broadcasted_iota(jnp.int32, (rows, 1), 0)
    gradient = jnp.where(position < limit_ref[0], wide(grad_ref[...]), 0.0)
    normed = norm_ref[...]
    made, gain_sum, shift_sum = norm_back(gradient, normed, factor_ref[...], gain_ref[...])
    made_ref[...] = made
    low_ref[...] = low(made)
    rows_made = jnp.concatenate(
        [
            gain_sum[None],
            shift_sum[None],
            jnp.sum(made, axis=0, keepdims=True),
            jnp.zeros((5, made.shape[1]), jnp.float32),
        ]
    )

    @pl.when(step == 0)
    def _():
        sums_ref[...] = rows_made

    @pl.when(step != 0)
    def _():
        sums_ref[...] += rows_made


def norm_back_call(limit, gradient, normed, factor, gain):
    slots, width = gradient.shape
    block = pl.BlockSpec((ROWS, width), lambda step, *_: (step, 0))
    return pl.pallas_call(
        norm_back_kernel,
        grid_spec=pltpu.PrefetchScalarGridSpec(
            num_scalar_prefetch=1,
            grid=(slots // ROWS,),
            in_specs=[
                block,
                block,
                pl.BlockSpec((ROWS, 1), lambda step, *_: (step, 0)),
                whole_spec((1, width)),
            ],
            out_specs=[block, block, whole_spec((8, width))],
        ),
        out_shape=[
            jax.ShapeDtypeStruct((slots, width), F32),
            jax.ShapeDtypeStruct((slots, width), BF16),
            jax.ShapeDtypeStruct((8, width), F32),
        ],
        compiler_params=pltpu.CompilerParams(
            dimension_semantics=("arbitrary",), vmem_limit_bytes=32 * 1024 * 1024
        ),
    )(limit, gradient, normed, factor, gain)


def mesh_place():
    return (
        lax.axis_index("dp"),
        lax.axis_index("tensor"),
        lax.axis_size("tensor"),
    )


def greet(unit, place, count):
    partners = [{"tensor": lax.rem(place + d, count)} for d in range(1, count)]
    partners.append({"dp": lax.rem(unit + 2, 4)})
    partners.append({"dp": unit + 1 - 2 * lax.rem(unit, 2)})
    barrier = pltpu.get_barrier_semaphore()
    for partner_id in partners:
        pl.semaphore_signal(barrier, inc=1, device_id=partner_id, device_id_type=MESH)
    pl.semaphore_wait(barrier, len(partners))
    return partners


def remote(source, target, send_sem, recv_sem, device_id):
    return pltpu.make_async_remote_copy(
        src_ref=source,
        dst_ref=target,
        send_sem=send_sem,
        recv_sem=recv_sem,
        device_id=device_id,
        device_id_type=MESH,
    )


def at_slot(ref, paired, half, slot):
    outer, inner = divmod(slot, 2)
    return ref.at[half, outer, :, inner] if paired else ref.at[half, outer, inner]


def gather_kernel(axes, *refs):
    groups = len(axes)
    blocks, own, across = (refs[0], refs[1 : 1 + groups], refs[1 + groups : 1 + 2 * groups])
    rest = refs[1 + 2 * groups :]
    rows, filled = (rest[0], rest[1 : 1 + groups])
    near, far = (0, 1)
    local_sem, block_send, block_recv, ring_send, ring_recv = rest[1 + groups : 6 + groups]
    side_send, side_recv, core_send, core_recv = rest[6 + groups :]
    unit, place, count = mesh_place()
    partners = greet(unit, place, count)
    right, side, core = (partners[0], partners[-2], partners[-1])
    started = []

    def begin(copy):
        copy.start()
        started.append(copy)
        return copy

    local = []

    def begin_local(source, target, index):
        copy = pltpu.make_async_copy(source, target, local_sem.at[index])
        copy.start()
        local.append(copy)

    def slot(half, group, index):
        return at_slot(filled[group], axes[group], half, index)

    def hop(group, step):
        source = own[group] if step == 1 else slot(near, group, step - 1)
        return begin(
            remote(
                source,
                slot(near, group, step),
                ring_send.at[group, step - 1],
                ring_recv.at[group, step - 1],
                right,
            )
        )

    def to_side(group, step):
        return begin(
            remote(
                slot(near, group, step),
                slot(near, group, count + step),
                side_send.at[group, step - 1],
                side_recv.at[group, step - 1],
                side,
            )
        )

    def to_core(group, index, source):
        return begin(
            remote(
                source,
                slot(far, group, index),
                core_send.at[group, index],
                core_recv.at[group, index],
                core,
            )
        )

    hops = {(0, 1): hop(0, 1)}
    block_copies = []
    for distance in range(1, count):
        block_copies.append(
            begin(
                remote(
                    blocks.at[lax.rem(place + distance, count)],
                    rows.at[place],
                    block_send.at[distance - 1],
                    block_recv.at[distance - 1],
                    partners[distance - 1],
                )
            )
        )
    for group in range(1, groups):
        hops[group, 1] = hop(group, 1)
    begin_local(blocks.at[place], rows.at[place], 0)
    cores, sides = ([], {})
    for group in range(groups):
        begin_local(own[group], slot(near, group, 0), 1 + 2 * group)
        begin_local(across[group], slot(near, group, count), 2 + 2 * group)
        cores.append(to_core(group, 0, own[group]))
        cores.append(to_core(group, count, across[group]))
    for step in range(1, count):
        for group in range(groups):
            hops[group, step].wait_recv()
            if step + 1 < count:
                hops[group, step + 1] = hop(group, step + 1)
            sides[group, step] = to_side(group, step)
            cores.append(to_core(group, step, slot(near, group, step)))
            earlier = (group, step - 1)
            if step > 1:
                sides[earlier].wait_recv()
                cores.append(to_core(group, count + step - 1, slot(near, group, count + step - 1)))
    for group in range(groups):
        last = count - 1
        sides[group, last].wait_recv()
        cores.append(to_core(group, count + last, slot(near, group, count + last)))
    for copy in block_copies:
        copy.wait_recv()
    for copy in cores:
        copy.wait_recv()
    for copy in local:
        copy.wait()
    for copy in started:
        copy.wait_send()


def gather_all(blocks, own, across, paired):
    count = lax.axis_size("tensor")
    groups = len(paired)
    anywhere = pl.BlockSpec(memory_space=pl.ANY)
    filled = []
    for array, in_pairs in zip(own, paired):
        if in_pairs:
            shape = (2, count, array.shape[0], 2) + array.shape[1:]
        else:
            shape = (2, count, 2) + array.shape
        filled.append(jax.ShapeDtypeStruct(shape, array.dtype))
    dma = pltpu.SemaphoreType.DMA
    made = pl.pallas_call(
        functools.partial(gather_kernel, paired),
        in_specs=[anywhere] * (1 + 2 * groups),
        out_specs=[anywhere] * (1 + groups),
        out_shape=[jax.ShapeDtypeStruct(blocks.shape, blocks.dtype)] + filled,
        scratch_shapes=[
            dma((1 + 2 * groups,)),
            dma((count - 1,)),
            dma((count - 1,)),
            dma((groups, count - 1)),
            dma((groups, count - 1)),
            dma((groups, count - 1)),
            dma((groups, count - 1)),
            dma((groups, 2 * count)),
            dma((groups, 2 * count)),
        ],
        compiler_params=pltpu.CompilerParams(collective_id=0, has_side_effects=True),
    )(blocks, *own, *across)
    return (made[0], made[1:])


def exchange_kernel(active, blocks, rows, local_sem, send_sem, recv_sem):
    @pl.when(lax.axis_index("section") == active)
    def _():
        place, count = (lax.axis_index("tensor"), lax.axis_size("tensor"))
        partners = [{"tensor": lax.rem(place + d, count)} for d in range(1, count)]
        barrier = pltpu.get_barrier_semaphore()
        for partner_id in partners:
            pl.semaphore_signal(barrier, inc=1, device_id=partner_id, device_id_type=MESH)
        pl.semaphore_wait(barrier, count - 1)
        own = pltpu.make_async_copy(blocks.at[place], rows.at[place], local_sem.at[0])
        own.start()
        copies = []
        for distance in range(1, count):
            copy = remote(
                blocks.at[lax.rem(place + distance, count)],
                rows.at[place],
                send_sem.at[distance - 1],
                recv_sem.at[distance - 1],
                partners[distance - 1],
            )
            copy.start()
            copies.append(copy)
        own.wait()
        for copy in copies:
            copy.wait()


def exchange_in(active, number, blocks):
    count = lax.axis_size("tensor")
    anywhere = pl.BlockSpec(memory_space=pl.ANY)
    return pl.pallas_call(
        functools.partial(exchange_kernel, active),
        in_specs=[anywhere],
        out_specs=anywhere,
        out_shape=jax.ShapeDtypeStruct(blocks.shape, blocks.dtype),
        scratch_shapes=[
            pltpu.SemaphoreType.DMA((1,)),
            pltpu.SemaphoreType.DMA((count - 1,)),
            pltpu.SemaphoreType.DMA((count - 1,)),
        ],
        compiler_params=pltpu.CompilerParams(collective_id=number, has_side_effects=True),
    )(blocks)


def reduce_kernel(paired, depths, *refs):
    groups = len(paired)
    blocks, small = refs[:2]
    made = refs[2 : 2 + groups]
    rest = refs[2 + groups :]
    rows, small_out, out = (rest[0], rest[1], rest[2 : 2 + groups])
    (
        near_buf,
        sums,
        side_in,
        ring_in,
        pair,
        other,
        small_core,
        small_side,
        small_far,
        near_sem,
        core_send,
        core_recv,
        side_send,
        side_recv,
        ring_send,
        ring_recv,
        pair_send,
        pair_recv,
        last_send,
        last_recv,
        out_sem,
        block_sem,
        block_send,
        block_recv,
        tiny_send,
        tiny_recv,
    ) = rest[2 + groups :]
    unit, place, count = mesh_place()
    partners = greet(unit, place, count)
    side, core = (partners[-2], partners[-1])
    units = (
        unit,
        lax.rem(unit + 2, 4),
        unit + 1 - 2 * lax.rem(unit, 2),
        lax.rem(unit + 3 - 2 * lax.rem(unit, 2), 4),
    )
    sends = []

    def begin(copy):
        copy.start()
        sends.append(copy)
        return copy

    chunks = []
    for group in range(groups):
        if not paired[group]:
            for first in range(0, depths[group], CHUNK):
                chunks.append((group, (pl.ds(first, CHUNK),)))
        else:
            for part in range(2):
                for first in range(0, depths[group], CHUNK):
                    chunks.append((group, (part, pl.ds(first, CHUNK))))

    def rows_of(chunk, half):
        group, place_in = chunk
        ref = made[group]
        if paired[group]:
            return ref.at[half, :, place_in[0], :, place_in[1]]
        return ref.at[half, :, :, place_in[0]]

    def result_of(chunk, owner):
        group, place_in = chunk
        if paired[group]:
            return out[group].at[owner, place_in[0], place_in[1]]
        return out[group].at[owner, place_in[0]]

    block_copies = []
    for distance in range(1, count):
        block_copies.append(
            begin(
                remote(
                    blocks.at[lax.rem(place + distance, count)],
                    rows.at[place],
                    block_send.at[distance - 1],
                    block_recv.at[distance - 1],
                    partners[distance - 1],
                )
            )
        )
    own_block = pltpu.make_async_copy(blocks.at[place], rows.at[place], block_sem.at[0])
    own_block.start()
    tiny = begin(remote(small, small_core, tiny_send.at[0], tiny_recv.at[0], core))
    state = {}
    outs = []

    def enter(index):
        chunk = chunks[index]
        copy = pltpu.make_async_copy(
            rows_of(chunk, 0), near_buf.at[index % 3], near_sem.at[index]
        )
        copy.start()
        state["near", index] = copy
        state["core", index] = begin(
            remote(
                rows_of(chunk, 1),
                sums.at[index],
                core_send.at[index],
                core_recv.at[index],
                core,
            )
        )

    def first_sum(index):
        state["near", index].wait()
        state["core", index].wait_recv()
        upper = pl.ds(count // 2, count // 2)
        total = wide(near_buf[index % 3, upper]) + wide(sums[index, upper])
        sums[index, upper] = total.astype(jnp.bfloat16)
        state["side", index] = begin(
            remote(
                sums.at[index, upper],
                side_in.at[index],
                side_send.at[index],
                side_recv.at[index],
                side,
            )
        )

    def second_sum(index):
        state["side", index].wait_recv()
        lower = pl.ds(0, count // 2)
        total = wide(near_buf[index % 3, lower]) + wide(sums[index, lower]) + wide(side_in[index])
        sums[index, lower] = total.astype(jnp.bfloat16)
        for distance in range(1, count):
            state["ring", index, distance] = begin(
                remote(
                    sums.at[index, distance // 2, distance % 2],
                    ring_in.at[index, distance - 1],
                    ring_send.at[index, distance - 1],
                    ring_recv.at[index, distance - 1],
                    partners[count - distance - 1],
                )
            )

    def third_sum(index):
        total = wide(sums[index, 0, 0])
        for distance in range(1, count):
            state["ring", index, distance].wait_recv()
            total = total + wide(ring_in[index, distance - 1])
        pair[index, 0] = total.astype(jnp.bfloat16)
        state["pair", index] = begin(
            remote(
                pair.at[index, 0],
                pair.at[index, 1],
                pair_send.at[index],
                pair_recv.at[index],
                side,
            )
        )

    def spread_pair(index):
        state["pair", index].wait_recv()
        state["last", index] = begin(
            remote(pair.at[index], other.at[index], last_send.at[index], last_recv.at[index], core)
        )

    def leave(index):
        state["last", index].wait_recv()
        chunk = chunks[index]
        found = (pair.at[index, 0], pair.at[index, 1], other.at[index, 0], other.at[index, 1])
        for bits in range(4):
            copy = pltpu.make_async_copy(
                found[bits], result_of(chunk, units[bits]), out_sem.at[index, bits]
            )
            copy.start()
            outs.append(copy)

    stages = (enter, first_sum, second_sum, third_sum, spread_pair, leave)
    for tick in range(len(chunks) + len(stages) - 1):
        for number, stage in enumerate(stages):
            if 0 <= tick - number < len(chunks):
                stage(tick - number)
        if tick == 2:
            tiny.wait_recv()
            small_core[...] += small[...]
            tiny = begin(remote(small_core, small_side, tiny_send.at[1], tiny_recv.at[1], side))
        if tick == 4:
            tiny.wait_recv()
            small_side[...] += small_core[...]
            tiny = [
                begin(
                    remote(
                        small_side,
                        small_far.at[distance - 1],
                        tiny_send.at[1 + distance],
                        tiny_recv.at[1 + distance],
                        partners[distance - 1],
                    )
                )
                for distance in range(1, count)
            ]
        if tick == 6:
            total = small_side[...]
            for distance in range(1, count):
                tiny[distance - 1].wait_recv()
                total = total + small_far[distance - 1]
            small_out[...] = total
    for copy in block_copies:
        copy.wait_recv()
    own_block.wait()
    for copy in outs:
        copy.wait()
    for copy in sends:
        copy.wait_send()


def reduce_all(blocks, small, made, paired):
    count = lax.axis_size("tensor")
    units = lax.axis_size("dp")
    groups = len(paired)
    anywhere = pl.BlockSpec(memory_space=pl.ANY)
    vmem = pl.BlockSpec(memory_space=pltpu.VMEM)
    width = blocks.shape[-1]
    depths = [array.shape[-2] for array in made]
    total = sum(depth * (2 if double else 1) for depth, double in zip(depths, paired)) // CHUNK
    results = []
    for array, double in zip(made, paired):
        shape = (units,) + ((2,) if double else ()) + array.shape[-2:]
        results.append(jax.ShapeDtypeStruct(shape, array.dtype))
    dma = pltpu.SemaphoreType.DMA
    bf16 = jnp.bfloat16
    found = pl.pallas_call(
        functools.partial(reduce_kernel, paired, depths),
        in_specs=[anywhere, vmem] + [anywhere] * groups,
        out_specs=[anywhere, vmem] + [anywhere] * groups,
        out_shape=[
            jax.ShapeDtypeStruct(blocks.shape, blocks.dtype),
            jax.ShapeDtypeStruct(small.shape, small.dtype),
        ]
        + results,
        scratch_shapes=[
            pltpu.VMEM((3, count, 2, CHUNK, width), bf16),
            pltpu.VMEM((total, count, 2, CHUNK, width), bf16),
            pltpu.VMEM((total, count // 2, 2, CHUNK, width), bf16),
            pltpu.VMEM((total, count - 1, CHUNK, width), bf16),
            pltpu.VMEM((total, 2, CHUNK, width), bf16),
            pltpu.VMEM((total, 2, CHUNK, width), bf16),
            pltpu.VMEM(small.shape, small.dtype),
            pltpu.VMEM(small.shape, small.dtype),
            pltpu.VMEM((count - 1,) + small.shape, small.dtype),
            dma((total,)),
            dma((total,)),
            dma((total,)),
            dma((total,)),
            dma((total,)),
            dma((total, count - 1)),
            dma((total, count - 1)),
            dma((total,)),
            dma((total,)),
            dma((total,)),
            dma((total,)),
            dma((total, 4)),
            dma((1,)),
            dma((count - 1,)),
            dma((count - 1,)),
            dma((count + 1,)),
            dma((count + 1,)),
        ],
        compiler_params=pltpu.CompilerParams(
            collective_id=1, has_side_effects=True, vmem_limit_bytes=56 * 1024 * 1024
        ),
    )(blocks, small, *made)
    return (found[0], found[1], found[2:])


def after(value, *earlier):
    return lax.optimization_barrier((value, earlier))[0]


def sequence_body(
    inputs,
    lengths,
    cotangent,
    qkv_weight,
    attn_out_weight,
    cross_weight,
    ffn_in_weight,
    ffn_in_bias,
    ffn_out_weight,
    ffn_out_bias,
    norm_gain,
    norm_bias,
):
    section = lax.axis_index("section")
    tensor_index = lax.axis_index("tensor")
    tensor_count = lax.axis_size("tensor")
    unit = lax.axis_index("dp")
    units = lax.axis_size("dp")
    decoder = section == 1
    alpha = jnp.where(decoder, ALPHA_DEC, ALPHA_ENC).astype(jnp.float32)
    alpha_row = alpha.reshape(1)
    batches, shard_rows, width = (inputs.shape[1], inputs.shape[2], inputs.shape[3])
    slots = batches * shard_rows
    gains = norm_gain[0].astype(jnp.float32)
    shifts = norm_bias[0].astype(jnp.float32)
    down_shift = ffn_out_bias.astype(jnp.float32)

    def unit_of(array, axis, bits):
        size = array.shape[axis] // units
        piece = lax.dynamic_slice_in_dim(array, (unit ^ bits) * size, size, axis)
        return piece.T if axis == 1 else piece

    bias_size = ffn_in_bias.shape[1] // units

    def units_of(bits):
        return (
            unit_of(qkv_weight[0], 1, bits),
            unit_of(attn_out_weight[0], 0, bits),
            unit_of(ffn_in_weight[0], 1, bits),
            unit_of(ffn_out_weight[0], 0, bits),
            unit_of(cross_weight[0], 1, bits).reshape(2, HS, width),
            jnp.broadcast_to(unit_of(ffn_in_bias[0], 0, bits)[None], (16, bias_size)),
        )

    x, filled = gather_all(
        inputs[0], units_of(0), units_of(2), (False, False, False, False, True, False)
    )
    x = x.reshape(slots, width)
    qkv_rows, out_rows, in_rows, down_rows, cross_rows = [
        array.reshape(-1, width) for array in filled[:5]
    ]
    in_shift = filled[5][:, :, :, 0].reshape(1, -1).astype(jnp.float32)
    cross_parts = cross_rows.reshape(-1, 2, LANES, width)
    half = width // 2

    source_len = lax.dynamic_index_in_dim(lengths[0, :, 0], tensor_index, 0, keepdims=False)
    target_len = lax.dynamic_index_in_dim(lengths[1, :, 0], tensor_index, 0, keepdims=False)
    own_len = jnp.where(decoder, target_len, source_len)
    self_scalars = jnp.stack([own_len, decoder.astype(jnp.int32)])
    cross_scalars = jnp.stack([source_len, jnp.zeros_like(source_len)])
    no_limit = jnp.full((1,), 1 << 20, jnp.int32)
    pairs = width // LANES
    sides = (0, 1)

    qkv = low(rows_nt(x, qkv_rows))
    mixed, lse_self = self_attention(self_scalars, qkv, 0, pairs)
    resid_a, norm_a, factor_a = layer_norm(
        alpha * x.astype(jnp.float32) + rows_nn(mixed, out_rows), gains[0], shifts[0]
    )
    a_low = low(resid_a)

    def zeros_like_of(branch):
        shapes = jax.eval_shape(branch)
        return lambda: jax.tree.map(lambda leaf: jnp.zeros(leaf.shape, leaf.dtype), shapes)

    def dec_query():
        first = cross_parts[:, 0].reshape(-1, width)
        made = low(rows_nt(a_low, first))
        return (made[:, :half], made[:, half:], first, cross_parts[:, 1].reshape(-1, width))

    query_left, query_right, cross_first, cross_second = lax.cond(
        decoder, dec_query, zeros_like_of(dec_query)
    )
    query_held = [lax.ppermute(piece, "section", [(1, 0)]) for piece in (query_left, query_right)]
    cotangent_rows = exchange_in(1, 2, after(cotangent, query_held)).reshape(slots, width)

    def feed(rows_low, rows_wide):
        return feed_call(
            alpha_row,
            rows_low,
            rows_wide,
            in_rows,
            in_shift,
            down_rows,
            down_shift,
            gains[2:3],
            shifts[2:3],
        )

    def enc_feed():
        hidden, slopes, memory_low, norm_y, factor_y = feed(a_low, resid_a)
        key_values = low(rows_nt(memory_low, cross_rows))
        return (hidden, slopes, memory_low, norm_y, factor_y, key_values)

    hidden_e, slopes_e, memory_low, norm_e, factor_e, key_values = lax.cond(
        decoder, zeros_like_of(enc_feed), enc_feed
    )

    mixed_c, lse_c, mixed_held = ([], [], [])
    for side in sides:

        def enc_mix():
            return tuple(
                cross_attention(
                    cross_scalars, query_held[side], key_values, side * pairs // 2, pairs // 2
                )
            )

        mix_made, lse_made = lax.cond(decoder, zeros_like_of(enc_mix), enc_mix)
        mixed_c.append(mix_made)
        lse_c.append(lse_made)
        mixed_held.append(lax.ppermute(mix_made, "section", [(0, 1)]))

    def sharded(rows):
        return rows.reshape(batches, shard_rows, width)

    outputs_e = exchange_in(0, 3, after(sharded(memory_low), mixed_held))
    mixed_held = after(mixed_held, outputs_e)

    def dec_middle():
        crossed = rows_nn(mixed_held[0], cross_second[:half]) + rows_nn(
            mixed_held[1], cross_second[half:]
        )
        resid_c, norm_c, factor_c = layer_norm(alpha * resid_a + crossed, gains[1], shifts[1])
        c_low = low(resid_c)
        hidden, slopes, decoded_low, norm_y, factor_y = feed(c_low, resid_c)
        grad_y, grad_low, sums_y = norm_back_call(
            target_len.reshape(1), cotangent_rows, norm_y, factor_y, gains[2:3]
        )
        grad_pre, bias_sum, grad_c = feed_back_call(
            alpha_row, grad_low, grad_y, in_rows, down_rows, slopes
        )
        grad_mid, mid_low, sums_c = norm_back_call(
            no_limit, grad_c, norm_c, factor_c, gains[1:2]
        )
        grad_mixed_c = tuple(
            low(rows_nt(mid_low, cross_second[side * half : side * half + half]))
            for side in sides
        )
        return (
            decoded_low,
            hidden,
            c_low,
            grad_low,
            grad_pre,
            bias_sum,
            grad_mid,
            mid_low,
            grad_mixed_c,
            sums_y,
            sums_c,
        )

    (
        decoded_low,
        hidden_d,
        c_low,
        grad_low_d,
        grad_pre_d,
        bias_sum_d,
        grad_mid,
        mid_low,
        grad_mixed_c,
        sums_yd,
        sums_cd,
    ) = lax.cond(decoder, dec_middle, zeros_like_of(dec_middle))
    grad_mixed_held = [lax.ppermute(piece, "section", [(1, 0)]) for piece in grad_mixed_c]

    grad_query_held, grad_kv = ([], [])
    for side in sides:

        def enc_cross():
            return tuple(
                cross_attention_back(
                    cross_scalars,
                    query_held[side],
                    key_values,
                    mixed_c[side],
                    grad_mixed_held[side],
                    lse_c[side],
                    side * pairs // 2,
                    pairs // 2,
                )
            )

        query_made, kv_made = lax.cond(decoder, zeros_like_of(enc_cross), enc_cross)
        grad_kv.append(kv_made)
        grad_query_held.append(lax.ppermute(query_made, "section", [(0, 1)]))

    outputs_d = exchange_in(1, 4, after(sharded(decoded_low), grad_mixed_held))
    grad_query_held = after(grad_query_held, outputs_d)
    outputs = jnp.where(decoder, outputs_d, outputs_e)

    def enc_back():
        grad_memory = rows_nn(grad_kv[0], cross_rows[:width]) + rows_nn(
            grad_kv[1], cross_rows[width:]
        )
        grad_y, grad_low, sums_y = norm_back_call(
            no_limit, grad_memory, norm_e, factor_e, gains[2:3]
        )
        grad_pre, bias_sum, grad_a = feed_back_call(
            alpha_row, grad_low, grad_y, in_rows, down_rows, slopes_e
        )
        made = [rows_tn(piece, memory_low) for piece in grad_kv]
        return (grad_low, grad_pre, bias_sum, grad_a, sums_y, low(jnp.concatenate(made)))

    def dec_back():
        grad_query = jnp.concatenate(grad_query_held, axis=1)
        grad_a = alpha * grad_mid + rows_nn(grad_query, cross_first)
        mixed_all = jnp.concatenate(mixed_held, axis=1)
        made = [rows_tn(grad_query, a_low), rows_tn(mixed_all, mid_low)]
        made = [piece.reshape(-1, 1, LANES, width) for piece in made]
        cross_made = low(jnp.concatenate(made, axis=1)).reshape(-1, width)
        return (grad_low_d, grad_pre_d, bias_sum_d, grad_a, sums_yd, cross_made)

    grad_low, grad_pre, bias_sum, grad_a, sums_y, cross_made = lax.cond(
        decoder, dec_back, enc_back
    )

    def down_grads():
        return lax.cond(
            decoder,
            lambda: low(rows_tn(hidden_d, grad_low)),
            lambda: low(rows_tn(hidden_e, grad_low)),
        )

    def in_grads():
        return lax.cond(
            decoder,
            lambda: low(rows_tn(grad_pre, c_low)),
            lambda: low(rows_tn(grad_pre, a_low)),
        )

    grad_r, r_low, sums_a = norm_back_call(no_limit, grad_a, norm_a, factor_a, gains[0:1])
    grad_mixed = low(rows_nt(r_low, out_rows))
    grad_qkv = self_attention_back(self_scalars, qkv, mixed, grad_mixed, lse_self, 0, pairs)
    grad_x = low(alpha * grad_r + rows_nn(grad_qkv, qkv_rows))

    slot_bits = jnp.asarray([0, 2, 1, 3], jnp.int32)[:, None]
    slot_unit = unit ^ slot_bits
    slot_tensor = (tensor_index - lax.iota(jnp.int32, tensor_count)[None]) % tensor_count
    slot_index = (slot_tensor * units + slot_unit).reshape(-1)
    hot = (slot_index[None, :] == lax.iota(jnp.int32, slot_index.shape[0])[:, None]).astype(
        jnp.float32
    )
    shift_abs = jnp.dot(
        hot, bias_sum.reshape(-1, bias_size), precision=lax.Precision.HIGHEST
    ).reshape(-1, width)
    small = jnp.concatenate([sums_a[:2], sums_cd[:2], sums_y[:3], shift_abs])
    small = jnp.pad(small, ((0, -small.shape[0] % 8), (0, 0)))
    made = (
        low(rows_tn(grad_qkv, x)),
        low(rows_tn(mixed, r_low)),
        in_grads(),
        down_grads(),
        cross_made,
    )
    input_rows, small, grads = reduce_all(
        sharded(grad_x),
        small,
        [array.reshape(like.shape) for array, like in zip(made, filled)],
        (False, False, False, False, True),
    )
    input_grad = input_rows.astype(jnp.float32)
    qkv_grad, out_grad, in_grad, down_grad, cross_grad = [
        array.astype(jnp.float32) for array in grads
    ]
    in_shift_grad = lax.dynamic_index_in_dim(
        small[7:11].reshape(tensor_count, -1), tensor_index, 0, keepdims=False
    )

    def columns(ordered):
        return ordered.reshape(-1, width).T[None]

    return (
        outputs[None],
        input_grad[None],
        columns(qkv_grad),
        out_grad.reshape(1, -1, width),
        columns(cross_grad),
        columns(in_grad),
        in_shift_grad[None],
        down_grad.reshape(1, -1, width),
        small[6][None],
        small[jnp.asarray([0, 2, 4])][None],
        small[jnp.asarray([1, 3, 5])][None],
    )


def solution(mesh):
    placed = (
        P("section", None, ("dp", "tensor"), None),
        P(None, None, "dp"),
        P(None, ("dp", "tensor"), None),
        P("section", None, "tensor"),
        P("section", "tensor", None),
        P("section", None, "tensor"),
        P("section", None, "tensor"),
        P("section", "tensor"),
        P("section", "tensor", None),
        P("section", None),
        P("section", None, None),
        P("section", None, None),
    )
    returned = (
        P("section", None, ("dp", "tensor"), None),
        P("section", None, ("dp", "tensor"), None),
        P("section", None, "tensor"),
        P("section", "tensor", None),
        P("section", None, "tensor"),
        P("section", None, "tensor"),
        P("section", "tensor"),
        P("section", "tensor", None),
        P("section", None),
        P("section", None, None),
        P("section", None, None),
    )
    sizes = dict(mesh.shape)

    def whole(*arrays):
        batches, sequences = arrays[1].shape[1:]
        heads = arrays[3].shape[2] // (3 * HS)
        group = sizes["dp"] * sizes["tensor"]
        one_each = batches == sizes["tensor"] and sizes["dp"] == 4 and sequences == sizes["dp"] and heads % group == 0
        chosen = sequence_body if one_each else body
        return jax.shard_map(
            chosen, mesh=mesh, in_specs=placed, out_specs=returned, check_vma=False
        )(*arrays)

    return whole
```

```python
import functools

import jax
import jax.numpy as jnp
from jax import lax
from jax.experimental import pallas as pl
from jax.experimental.pallas import tpu as pltpu
from jax.sharding import PartitionSpec as P

HS = 64
QBLOCK = 512


ALPHA_ENC = 0.81 * (100.0**5) ** (1.0 / 16.0)
ALPHA_DEC = (3.0 * 100.0) ** 0.25
EPS = 1e-05
NEG = -1e30
ROW_DIMS = (((0,), (0,)), ((), ()))
COL_DIMS = (((1,), (1,)), ((), ()))
LANES = 2 * HS
ROWS = 256
CHUNK = 32
AHEAD = 1
FEED_ROWS = 512
BLOCK = 1024
MESH = pl.DeviceIdType.MESH
SCALE = HS ** (-0.5)
GELU_C = (2.0 / 3.141592653589793) ** 0.5


def from_behind(block, axis, distance):
    devices = range(lax.axis_size(axis))
    route = [(i - distance, i) for i in devices if i - distance in devices]
    return lax.ppermute(block, axis, route)


def layer_norm(values, gain_row, shift_row):
    centered = values - jnp.mean(values, axis=-1, keepdims=True)
    factor = lax.rsqrt(jnp.mean(centered * centered, axis=-1, keepdims=True) + EPS)
    normed = centered * factor
    return (normed * gain_row + shift_row, normed, factor)


def norm_back(gradient, normed, factor, gain_row):
    scaled = gradient * gain_row
    centred = (
        scaled
        - jnp.mean(scaled, axis=-1, keepdims=True)
        - normed * jnp.mean(scaled * normed, axis=-1, keepdims=True)
    )
    return (centred * factor, jnp.sum(gradient * normed, axis=0), jnp.sum(gradient, axis=0))


def visible(first_row, row_count, key_count, seq_lengths, causal):
    key_pos = lax.broadcasted_iota(jnp.int32, (1, row_count, key_count), 2)
    query_pos = first_row + lax.broadcasted_iota(jnp.int32, (1, row_count, key_count), 1)
    inside = key_pos < seq_lengths[:, None, None]
    return inside & ((key_pos <= query_pos) | jnp.logical_not(causal))


def attend(queries, keys_in, values, seq_lengths, causal):
    key_count = queries.shape[1]
    score_scale = queries.shape[3] ** (-0.5)
    row_block = min(QBLOCK, key_count)
    mixed_parts, lse_parts = ([], [])
    for first_row in range(0, key_count, row_block):
        allowed = visible(first_row, row_block, key_count, seq_lengths, causal)
        raw_scores = jnp.einsum(
            "bqhe,bkhe->bhqk",
            queries[:, first_row : first_row + row_block],
            keys_in,
            preferred_element_type=jnp.float32,
        )
        scores = jnp.where(allowed[:, None], raw_scores * score_scale, NEG)
        row_max = jnp.max(scores, axis=-1, keepdims=True)
        expo_vals = jnp.exp(scores - row_max)
        row_total = jnp.sum(expo_vals, axis=-1, keepdims=True)
        weights = (expo_vals / row_total).astype(jnp.bfloat16)
        mixed_block = jnp.einsum(
            "bhqk,bkhe->bqhe", weights, values, preferred_element_type=jnp.float32
        )
        mixed_parts.append(mixed_block.astype(jnp.bfloat16))
        lse_parts.append(row_max + jnp.log(row_total))
    return (jnp.concatenate(mixed_parts, axis=1), jnp.concatenate(lse_parts, axis=2))


def attend_back(grad_mixed, queries, keys_in, values, log_totals, seq_lengths, causal):
    key_count = queries.shape[1]
    score_scale = queries.shape[3] ** (-0.5)
    row_block = min(QBLOCK, key_count)
    query_parts = []
    grad_keys = jnp.zeros(keys_in.shape, jnp.float32)
    grad_values = jnp.zeros(values.shape, jnp.float32)
    for first_row in range(0, key_count, row_block):
        query_part = queries[:, first_row : first_row + row_block]
        grad_part = grad_mixed[:, first_row : first_row + row_block]
        allowed = visible(first_row, row_block, key_count, seq_lengths, causal)
        raw_scores = jnp.einsum(
            "bqhe,bkhe->bhqk", query_part, keys_in, preferred_element_type=jnp.float32
        )
        scores = jnp.where(allowed[:, None], raw_scores * score_scale, NEG)
        probs = jnp.exp(scores - log_totals[:, :, first_row : first_row + row_block])
        grad_probs = jnp.einsum(
            "bqhe,bkhe->bhqk", grad_part, values, preferred_element_type=jnp.float32
        )
        grad_scores = probs * (grad_probs - jnp.sum(probs * grad_probs, axis=-1, keepdims=True))
        grad_raw = (grad_scores * score_scale).astype(jnp.bfloat16)
        query_parts.append(
            jnp.einsum("bhqk,bkhe->bqhe", grad_raw, keys_in, preferred_element_type=jnp.float32)
        )
        grad_keys = grad_keys + jnp.einsum(
            "bhqk,bqhe->bkhe", grad_raw, query_part, preferred_element_type=jnp.float32
        )
        grad_values = grad_values + jnp.einsum(
            "bhqk,bqhe->bkhe",
            probs.astype(jnp.bfloat16),
            grad_part,
            preferred_element_type=jnp.float32,
        )
    return (jnp.concatenate(query_parts, axis=1), grad_keys, grad_values)


def ffn_forward(rows_in, in_proj, in_shift, down_proj):
    pre_act = jnp.dot(rows_in, in_proj, preferred_element_type=jnp.float32) + in_shift
    hidden = jax.nn.gelu(pre_act).astype(jnp.bfloat16)
    return (pre_act, jnp.dot(hidden, down_proj, preferred_element_type=jnp.float32))


def ffn_backward(grad_in, rows_in, pre_act, in_proj, down_proj):
    activated, slope_back = jax.vjp(jax.nn.gelu, pre_act)
    hidden = activated.astype(jnp.bfloat16)
    grad_down = lax.dot_general(hidden, grad_in, ROW_DIMS, preferred_element_type=jnp.float32)
    grad_hidden = lax.dot_general(grad_in, down_proj, COL_DIMS, preferred_element_type=jnp.float32)
    grad_pre = slope_back(grad_hidden)[0].astype(jnp.bfloat16)
    grad_shift = jnp.sum(grad_pre.astype(jnp.float32), axis=0)
    grad_inner = lax.dot_general(rows_in, grad_pre, ROW_DIMS, preferred_element_type=jnp.float32)
    grad_rows_out = lax.dot_general(grad_pre, in_proj, COL_DIMS, preferred_element_type=jnp.float32)
    return (grad_rows_out, grad_inner, grad_shift, grad_down)


def gather_rows(shard):
    return lax.all_gather(shard, "tensor", axis=0, tiled=True)


def sum_rows(partial_value):
    return lax.psum_scatter(partial_value, "tensor", scatter_dimension=0, tiled=True)


def ffn_input_rows(shard):
    return lax.all_gather(shard, "tensor", axis=0, tiled=True)


def ffn_sum_rows(partial_value):
    return lax.psum_scatter(
        partial_value.astype(jnp.bfloat16), "tensor", scatter_dimension=0, tiled=True
    ).astype(jnp.float32)


def grad_rows(shard):
    return lax.all_gather(shard, "tensor", axis=0, tiled=True)


def grad_sums(partial_value):
    return lax.psum_scatter(
        partial_value.astype(jnp.bfloat16), "tensor", scatter_dimension=0, tiled=True
    ).astype(jnp.float32)


def ffn_grad_rows(shard):
    return lax.all_gather(shard, "tensor", axis=0, tiled=True)


def ffn_grad_sums(partial_value):
    return lax.psum_scatter(
        partial_value.astype(jnp.bfloat16), "tensor", scatter_dimension=0, tiled=True
    ).astype(jnp.float32)


def body(
    inputs,
    lengths,
    cotangent,
    qkv_weight,
    attn_out_weight,
    cross_weight,
    ffn_in_weight,
    ffn_in_bias,
    ffn_out_weight,
    ffn_out_bias,
    norm_gain,
    norm_bias,
):
    tensor_count = lax.axis_size("tensor")
    section = lax.axis_index("section")
    tensor_index = lax.axis_index("tensor")
    decoder = section == 1
    alpha = jnp.where(decoder, ALPHA_DEC, ALPHA_ENC).astype(jnp.float32)
    batches, shard_rows, width = (inputs.shape[1], inputs.shape[2], inputs.shape[3])
    seq_count = lengths.shape[2]
    full_rows = shard_rows * tensor_count
    slots = full_rows // seq_count
    qkv_proj = qkv_weight[0]
    head_local = qkv_proj.shape[1] // (3 * HS)
    head_cols = head_local * HS
    out_proj = attn_out_weight[0]
    cross_proj = cross_weight[0]
    cross_split = cross_proj.reshape(width, head_local, 2, HS)
    first_cols = cross_split[:, :, 0].reshape(width, head_cols)
    second_cols = cross_split[:, :, 1].reshape(width, head_cols)
    in_proj = ffn_in_weight[0]
    in_shift = ffn_in_bias[0].astype(jnp.float32)
    down_proj = ffn_out_weight[0]
    hidden_width = in_proj.shape[1]
    down_shift = ffn_out_bias[0].astype(jnp.float32)
    gains = norm_gain[0].astype(jnp.float32)
    shifts = norm_bias[0].astype(jnp.float32)
    own_lengths = lax.dynamic_index_in_dim(lengths, section, 0, keepdims=False)
    source_lengths = lengths[0]
    row_index = tensor_index * shard_rows + lax.iota(jnp.int32, shard_rows)
    row_seq = row_index // slots
    row_pos = row_index % slots
    seq_ids = lax.iota(jnp.int32, seq_count)
    lse_shape = (seq_count, head_local, slots, 1)

    def zeros_float(shape):
        return jnp.zeros(shape, jnp.float32)

    def zeros_low(shape):
        return jnp.zeros(shape, jnp.bfloat16)

    def to_heads(flat_rows):
        return flat_rows.reshape(seq_count, slots, flat_rows.shape[1] // HS, HS)

    def to_rows(split_rows):
        return split_rows.reshape(full_rows, -1)

    def cross_forward(query_rows, kv_source, source_len):
        kv_split = kv_source.reshape(seq_count, slots, head_local, 2, HS)
        query_c = jnp.dot(query_rows, first_cols, preferred_element_type=jnp.float32).astype(
            jnp.bfloat16
        )
        mixed_c, lse_cross = attend(
            to_heads(query_c), kv_split[:, :, :, 0], kv_split[:, :, :, 1], source_len, False
        )
        mixed_c = to_rows(mixed_c)
        partial_value = lax.dot_general(
            mixed_c, second_cols, COL_DIMS, preferred_element_type=jnp.float32
        )
        return (query_c, mixed_c, lse_cross, partial_value)

    kv_held = zeros_low((full_rows, 2 * head_cols))
    kv_ticks, kept_ticks, out_ticks = ([], [], [])
    for tick_index in range(batches + 1):
        batch = jnp.clip(tick_index - section, 0, batches - 1)
        x_shard = lax.dynamic_index_in_dim(inputs[0], batch, 0, keepdims=False)
        own_len = lax.dynamic_index_in_dim(own_lengths, batch, 0, keepdims=False)
        source_len = lax.dynamic_index_in_dim(source_lengths, batch, 0, keepdims=False)
        x_full = gather_rows(x_shard)
        qkv = jnp.dot(x_full, qkv_proj, preferred_element_type=jnp.float32).astype(jnp.bfloat16)
        qkv_split = qkv.reshape(seq_count, slots, head_local, 3, HS)
        mixed, lse_self = attend(
            qkv_split[:, :, :, 0], qkv_split[:, :, :, 1], qkv_split[:, :, :, 2], own_len, decoder
        )
        mixed = to_rows(mixed)
        attn_sum = sum_rows(jnp.dot(mixed, out_proj, preferred_element_type=jnp.float32))
        resid_a, norm_a, factor_a = layer_norm(
            alpha * x_shard.astype(jnp.float32) + attn_sum, gains[0], shifts[0]
        )
        a_shard = resid_a.astype(jnp.bfloat16)
        a_full = gather_rows(a_shard)

        def enc_second():
            hidden_made, partial_value = ffn_forward(a_full, in_proj, in_shift, down_proj)
            return (
                hidden_made,
                zeros_low((full_rows, head_cols)),
                zeros_low((full_rows, head_cols)),
                zeros_float(lse_shape),
                partial_value,
            )

        def dec_second():
            query_c, mixed_c, lse_cross, partial_value = cross_forward(a_full, kv_held, source_len)
            return (
                zeros_float((full_rows, hidden_width)),
                query_c,
                mixed_c,
                lse_cross,
                partial_value,
            )

        hidden_enc, query_c, mixed_c, lse_cross, partial_value = lax.cond(
            decoder, dec_second, enc_second
        )
        second_sum = sum_rows(partial_value)
        resid_ye, norm_ye, factor_ye = layer_norm(
            alpha * resid_a + second_sum + down_shift, gains[2], shifts[2]
        )
        resid_c, norm_c, factor_c = layer_norm(alpha * resid_a + second_sum, gains[1], shifts[1])
        wide_rows = ffn_input_rows(jnp.where(decoder, resid_c, resid_ye).astype(jnp.bfloat16))

        def enc_third():
            kv_made = jnp.dot(wide_rows, cross_proj, preferred_element_type=jnp.float32).astype(
                jnp.bfloat16
            )
            return (
                kv_made,
                zeros_float((full_rows, hidden_width)),
                zeros_float((full_rows, width)),
            )

        def dec_third():
            hidden_made, partial_made = ffn_forward(wide_rows, in_proj, in_shift, down_proj)
            return (zeros_low((full_rows, 2 * head_cols)), hidden_made, partial_made)

        kv_out, hidden_dec, partial_third = lax.cond(decoder, dec_third, enc_third)
        third_sum = ffn_sum_rows(partial_third)
        resid_yd, norm_yd, factor_yd = layer_norm(
            alpha * resid_c + third_sum + down_shift, gains[2], shifts[2]
        )
        resid_y = jnp.where(decoder, resid_yd, resid_ye)
        norm_y = jnp.where(decoder, norm_yd, norm_ye)
        factor_y = jnp.where(decoder, factor_yd, factor_ye)
        hidden = jnp.where(decoder, hidden_dec, hidden_enc)
        ffn_rows = jnp.where(decoder, wide_rows, a_full)
        y_shard = resid_y.astype(jnp.bfloat16)
        kv_held = from_behind(kv_out, "section", 1)
        kv_ticks.append(kv_held)
        out_ticks.append(y_shard)
        kept_ticks.append(
            dict(
                x_rows=x_full,
                qkv=qkv,
                mixed=mixed,
                lse_self=lse_self,
                a_rows=a_full,
                kv_rows=wide_rows,
                ffn_rows=ffn_rows,
                hidden=hidden,
                query_c=query_c,
                mixed_c=mixed_c,
                lse_cross=lse_cross,
                norm_a=norm_a,
                factor_a=factor_a,
                norm_c=norm_c,
                factor_c=factor_c,
                norm_y=norm_y,
                factor_y=factor_y,
            )
        )
    kept_all = jax.tree.map(lambda *leaves: jnp.stack(leaves), *kept_ticks)
    kv_stack = jnp.stack(kv_ticks)
    outputs = lax.dynamic_slice_in_dim(jnp.stack(out_ticks), section, batches, 0)
    totals = dict(
        qkv=zeros_float(qkv_proj.shape),
        outer=zeros_float(out_proj.shape),
        cross=zeros_float(cross_proj.shape),
        inner=zeros_float(in_proj.shape),
        inner_shift=zeros_float(in_shift.shape),
        down=zeros_float(down_proj.shape),
        down_shift=zeros_float(down_shift.shape),
        gain=zeros_float(gains.shape),
        shift=zeros_float(shifts.shape),
    )
    zero_ffn = (
        zeros_float(in_proj.shape),
        zeros_float(in_shift.shape),
        zeros_float(down_proj.shape),
    )
    zero_cross = zeros_float((width, 2 * head_cols))
    dkv_held = zeros_low((full_rows, 2 * head_cols))
    grad_ticks = []
    for tick_index in range(batches + 1):
        batch_raw = batches - tick_index - section
        live = (batch_raw >= 0) & (batch_raw < batches)
        batch = jnp.clip(batch_raw, 0, batches - 1)
        kept = jax.tree.map(
            lambda leaf_value: lax.dynamic_index_in_dim(
                leaf_value, batch + section, 0, keepdims=False
            ),
            kept_all,
        )
        own_len = lax.dynamic_index_in_dim(own_lengths, batch, 0, keepdims=False)
        source_len = lax.dynamic_index_in_dim(source_lengths, batch, 0, keepdims=False)
        kv_now = lax.dynamic_index_in_dim(kv_stack, batch, 0, keepdims=False)
        kv_split = kv_now.reshape(seq_count, slots, head_local, 2, HS)
        own_rows = jnp.sum(
            jnp.where(row_seq[:, None] == seq_ids[None, :], own_len[None, :], 0), axis=1
        )
        grad_top = lax.dynamic_index_in_dim(cotangent, batch, 0, keepdims=False).astype(jnp.float32)
        grad_top = jnp.where((row_pos < own_rows)[:, None], grad_top, 0.0)
        grad_r3d, gain_yd, shift_yd = norm_back(
            grad_top, kept["norm_y"], kept["factor_y"], gains[2]
        )
        dkv_now = dkv_held

        def kv_back():
            partial_value = lax.dot_general(
                dkv_now, cross_proj, COL_DIMS, preferred_element_type=jnp.float32
            )
            grad_cross_enc = lax.dot_general(
                kept["kv_rows"], dkv_now, ROW_DIMS, preferred_element_type=jnp.float32
            )
            return (partial_value, grad_cross_enc)

        def cross_back(grad_full):
            grad_mixed_c = jnp.dot(
                grad_full, second_cols, preferred_element_type=jnp.float32
            ).astype(jnp.bfloat16)
            grad_second = lax.dot_general(
                grad_full, kept["mixed_c"], ROW_DIMS, preferred_element_type=jnp.float32
            )
            grad_qc, grad_kc, grad_vc = attend_back(
                to_heads(grad_mixed_c),
                to_heads(kept["query_c"]),
                kv_split[:, :, :, 0],
                kv_split[:, :, :, 1],
                kept["lse_cross"],
                source_len,
                False,
            )
            grad_qc = to_rows(grad_qc).astype(jnp.bfloat16)
            grad_first = lax.dot_general(
                kept["a_rows"], grad_qc, ROW_DIMS, preferred_element_type=jnp.float32
            )
            partial_value = lax.dot_general(
                grad_qc, first_cols, COL_DIMS, preferred_element_type=jnp.float32
            )
            grad_kv = (
                jnp.stack([grad_kc, grad_vc], axis=3)
                .astype(jnp.bfloat16)
                .reshape(full_rows, 2 * head_cols)
            )
            grad_cross_dec = jnp.stack(
                [
                    grad_first.reshape(width, head_local, HS),
                    grad_second.reshape(width, head_local, HS),
                ],
                axis=2,
            ).reshape(width, 2 * head_cols)
            return (partial_value, grad_cross_dec, grad_kv)

        first_full = grad_rows(jnp.where(decoder, grad_r3d, 0.0).astype(jnp.bfloat16))

        def enc_first():
            partial_value, grad_cross_enc = kv_back()
            return (partial_value, grad_cross_enc) + zero_ffn

        def dec_first():
            partial_value, inner_made, shift_made, down_made = ffn_backward(
                first_full, kept["ffn_rows"], kept["hidden"], in_proj, down_proj
            )
            return (partial_value, zero_cross, inner_made, shift_made, down_made)

        partial_one, cross_enc, inner_one, inner_shift_one, down_one = lax.cond(
            decoder, dec_first, enc_first
        )
        first_sum = grad_sums(partial_one)
        grad_r3e, gain_ye, shift_ye = norm_back(
            first_sum, kept["norm_y"], kept["factor_y"], gains[2]
        )
        grad_r2, gain_c, shift_c = norm_back(
            alpha * grad_r3d + first_sum, kept["norm_c"], kept["factor_c"], gains[1]
        )
        grad_r3 = jnp.where(decoder, grad_r3d, grad_r3e)
        gain_y = jnp.where(decoder, gain_yd, gain_ye)
        shift_y = jnp.where(decoder, shift_yd, shift_ye)
        middle_grad = jnp.where(decoder, grad_r2, grad_r3e)
        second_full = ffn_grad_rows(middle_grad.astype(jnp.bfloat16))

        def enc_second():
            partial_value, inner_made, shift_made, down_made = ffn_backward(
                second_full, kept["ffn_rows"], kept["hidden"], in_proj, down_proj
            )
            return (
                partial_value,
                inner_made,
                shift_made,
                down_made,
                zero_cross,
                zeros_low((full_rows, 2 * head_cols)),
            )

        def dec_second():
            partial_value, grad_cross_dec, grad_kv_made = cross_back(second_full)
            return (partial_value,) + zero_ffn + (grad_cross_dec, grad_kv_made)

        partial_two, inner_two, inner_shift_two, down_two, cross_dec, grad_kv = lax.cond(
            decoder, dec_second, enc_second
        )
        grad_a = alpha * middle_grad + ffn_grad_sums(partial_two)
        dkv_held = from_behind(grad_kv, "section", -1)
        grad_r1, gain_a, shift_a = norm_back(grad_a, kept["norm_a"], kept["factor_a"], gains[0])
        attn_full = grad_rows(grad_r1.astype(jnp.bfloat16))
        grad_mixed = lax.dot_general(
            attn_full, out_proj, COL_DIMS, preferred_element_type=jnp.float32
        ).astype(jnp.bfloat16)
        grad_outer = lax.dot_general(
            kept["mixed"], attn_full, ROW_DIMS, preferred_element_type=jnp.float32
        )
        qkv_split = kept["qkv"].reshape(seq_count, slots, head_local, 3, HS)
        grad_q, grad_k, grad_v = attend_back(
            to_heads(grad_mixed),
            qkv_split[:, :, :, 0],
            qkv_split[:, :, :, 1],
            qkv_split[:, :, :, 2],
            kept["lse_self"],
            own_len,
            decoder,
        )
        grad_qkv = (
            jnp.stack([grad_q, grad_k, grad_v], axis=3)
            .astype(jnp.bfloat16)
            .reshape(full_rows, 3 * head_cols)
        )
        grad_qkv_proj = lax.dot_general(
            kept["x_rows"], grad_qkv, ROW_DIMS, preferred_element_type=jnp.float32
        )
        grad_x = alpha * grad_r1 + grad_sums(
            lax.dot_general(grad_qkv, qkv_proj, COL_DIMS, preferred_element_type=jnp.float32)
        )
        grad_ticks.append(grad_x)
        gain_step = jnp.stack([gain_a, jnp.where(decoder, gain_c, 0.0), gain_y])
        shift_step = jnp.stack([shift_a, jnp.where(decoder, shift_c, 0.0), shift_y])
        steps = dict(
            qkv=grad_qkv_proj,
            outer=grad_outer,
            cross=cross_enc + cross_dec,
            inner=inner_one + inner_two,
            inner_shift=inner_shift_one + inner_shift_two,
            down=down_one + down_two,
            down_shift=jnp.sum(grad_r3, axis=0),
            gain=gain_step,
            shift=shift_step,
        )
        totals = {name: totals[name] + jnp.where(live, steps[name], 0.0) for name in totals}
    input_grad = lax.dynamic_slice_in_dim(jnp.stack(grad_ticks[::-1]), section, batches, 0)
    inner_total, inner_shift_total, down_total = (
        totals["inner"],
        totals["inner_shift"],
        totals["down"],
    )
    summed = (
        lax.psum(totals["qkv"].astype(jnp.bfloat16), "dp").astype(jnp.float32),
        lax.psum(totals["outer"].astype(jnp.bfloat16), "dp").astype(jnp.float32),
        lax.psum(totals["cross"].astype(jnp.bfloat16), "dp").astype(jnp.float32),
        lax.psum(inner_total.astype(jnp.bfloat16), "dp").astype(jnp.float32),
        lax.psum(inner_shift_total.astype(jnp.bfloat16), "dp").astype(jnp.float32),
        lax.psum(down_total.astype(jnp.bfloat16), "dp").astype(jnp.float32),
    )
    vectors = lax.psum((totals["gain"], totals["shift"], totals["down_shift"]), ("dp", "tensor"))
    return (
        outputs[None],
        input_grad[None],
        summed[0][None],
        summed[1][None],
        summed[2][None],
        summed[3][None],
        summed[4][None],
        summed[5][None],
        vectors[2][None],
        vectors[0][None],
        vectors[1][None],
    )


def lanes_of(rows):
    return lax.broadcasted_iota(jnp.int32, (rows, LANES), 1)


def swap_halves(tile):
    return pltpu.roll(tile, HS, 1)


def pair_of(packed, left):
    first, second, third = (packed[:, :LANES], packed[:, LANES : 2 * LANES], packed[:, 2 * LANES :])
    swap = lambda tile: jnp.concatenate([tile[:, HS:], tile[:, :HS]], axis=1)
    queries = jnp.where(left, first, second)
    keys_in = jnp.where(left, swap(first), swap(third))
    values = jnp.where(left, second, third)
    return (queries, keys_in, values)


def wide(value):
    return value.astype(jnp.float32)


def low(values):
    return values.astype(jnp.bfloat16)


def half_tiles(tile, fill_right, fill_left, left):
    return (jnp.where(left, tile, fill_right), jnp.where(left, fill_left, tile))


def key_tiles(keys_in, length, ones):
    slots = keys_in.shape[0]
    lane = lanes_of(slots)
    hidden = lax.broadcasted_iota(jnp.int32, (slots, LANES), 0) >= length
    left = lane < HS

    def fill(start):
        outside = jnp.where((lane == start) & hidden, NEG, 0.0)
        return jnp.where((lane > start) & (lane <= start + ones), 1.0, outside)

    first, second = half_tiles(wide(keys_in), fill(HS), fill(0), left)
    return (low(first), low(second))


def attend_forward(length, causal, queries_ref, key_refs, value_refs, mixed_ref, lse_ref):
    slots = queries_ref.shape[0]
    lane = lanes_of(ROWS)
    left = lane < HS

    def score(first_row, key_count, triangle, half):
        queries = wide(queries_ref[pl.ds(first_row, ROWS), :]) * SCALE
        start = HS if half == 0 else 0
        mine = left if half == 0 else jnp.logical_not(left)
        augmented = low(jnp.where(mine, queries, jnp.where(lane == start, 1.0, 0.0)))
        scores = lax.dot_general(
            augmented,
            key_refs[half][pl.ds(0, key_count), :],
            COL_DIMS,
            preferred_element_type=jnp.float32,
        )
        if triangle:
            column = lax.broadcasted_iota(jnp.int32, (ROWS, key_count), 1)
            row = first_row + lax.broadcasted_iota(jnp.int32, (ROWS, key_count), 0)
            scores = jnp.where(column <= row, scores, NEG)
        return scores

    def finish(first_row, totals, tops):
        norm = swap_halves(jnp.where(left, totals[1], totals[0]))
        mixed_ref[pl.ds(first_row, ROWS), :] = low(jnp.where(left, totals[0], totals[1]) / norm)
        logs = jnp.where(left, tops[0], tops[1]) + jnp.log(norm)
        lse_ref[pl.ds(first_row, ROWS), :] = swap_halves(logs)

    def run(triangle):
        items = []
        for first_row in range(0, slots, ROWS):
            for half in range(2):
                items.append((first_row, first_row + ROWS if triangle else slots, triangle, half))
        waiting = [score(*item) for item in items[:AHEAD]]
        totals, tops = ([], [])
        for number, item in enumerate(items):
            if number + AHEAD < len(items):
                waiting.append(score(*items[number + AHEAD]))
            scores = waiting.pop(0)
            top = jnp.max(scores, axis=1, keepdims=True)
            tops.append(top)
            totals.append(
                jnp.dot(
                    low(jnp.exp(scores - top)),
                    value_refs[item[3]][pl.ds(0, item[1]), :],
                    preferred_element_type=jnp.float32,
                )
            )
            if item[3] == 1:
                finish(item[0], totals, tops)
                totals, tops = ([], [])

    @pl.when(causal == 0)
    def _():
        run(False)

    @pl.when(causal != 0)
    def _():
        run(True)


def fill_forward(length, keys_in, values, key_refs, value_refs):
    left = lanes_of(keys_in.shape[0]) < HS
    for ref, tile in zip(key_refs, key_tiles(keys_in, length, 0)):
        ref[...] = tile
    one = jnp.ones((), values.dtype)
    for ref, tile in zip(value_refs, half_tiles(values, one, one, left)):
        ref[...] = tile


def self_forward_kernel(scalars, packed_ref, mixed_ref, lse_ref, queries_ref, k0, k1, v0, v1):
    left = lanes_of(packed_ref.shape[0]) < HS
    queries, keys_in, values = pair_of(packed_ref[...], left)
    queries_ref[...] = queries
    fill_forward(scalars[0], keys_in, values, (k0, k1), (v0, v1))
    attend_forward(scalars[0], scalars[1], queries_ref, (k0, k1), (v0, v1), mixed_ref, lse_ref)


def cross_forward_kernel(
    scalars, query_ref, key_ref, value_ref, mixed_ref, lse_ref, k0, k1, v0, v1
):
    fill_forward(scalars[0], key_ref[...], value_ref[...], (k0, k1), (v0, v1))
    attend_forward(scalars[0], 0, query_ref, (k0, k1), (v0, v1), mixed_ref, lse_ref)


def attend_backward(
    causal, queries_ref, key_refs, plain_refs, value_refs, mixed_ref, grad_ref, lse_ref, outs
):
    dq_ref, key_acc, value_acc = outs
    slots = queries_ref.shape[0]
    lane = lanes_of(ROWS)
    left = lane < HS
    key_acc[...] = jnp.zeros_like(key_acc)
    value_acc[...] = jnp.zeros_like(value_acc)

    def extra(start, terms, one):
        filled = jnp.where(lane == start, one, 0.0)
        for number, term in enumerate(terms):
            filled = jnp.where(lane == start + 1 + number, -term, filled)
        return filled

    def parts(value, count):
        found = []
        for _ in range(count):
            found.append(wide(low(value)))
            value = value - found[-1]
        return found

    def prepare(first_row, key_count, triangle, half):
        rows = pl.ds(first_row, ROWS)
        keys = pl.ds(0, key_count)
        mine = left if half == 0 else jnp.logical_not(left)
        start = HS if half == 0 else 0
        queries = wide(queries_ref[rows, :]) * SCALE
        grads = wide(grad_ref[rows, :])
        product = grads * wide(mixed_ref[rows, :])
        delta = jnp.sum(jnp.where(mine, product, 0.0), axis=1, keepdims=True)
        log_parts = parts(lse_ref[rows, :], 3)
        query_aug = low(jnp.where(mine, queries, extra(start, log_parts, 1.0)))
        grad_aug = low(jnp.where(mine, grads, extra(start, parts(delta, 2), 0.0)))
        scores = lax.dot_general(
            key_refs[half][keys, :], query_aug, COL_DIMS, preferred_element_type=jnp.float32
        )
        grad_probs = lax.dot_general(
            value_refs[half][keys, :], grad_aug, COL_DIMS, preferred_element_type=jnp.float32
        )
        return (
            scores,
            grad_probs,
            low(jnp.where(mine, queries, 0.0)),
            low(jnp.where(mine, grads, 0.0)),
        )

    def run(triangle):
        items = []
        for first_row in range(0, slots, ROWS):
            for half in range(2):
                items.append((first_row, first_row + ROWS if triangle else slots, triangle, half))
        waiting = [prepare(*item) for item in items[:AHEAD]]
        query_total, key_total, value_total = (None, None, None)
        for number, (first_row, key_count, _, half) in enumerate(items):
            if number + AHEAD < len(items):
                waiting.append(prepare(*items[number + AHEAD]))
            scores, grad_probs, query_half, grad_half = waiting.pop(0)
            keys = pl.ds(0, key_count)
            probs = jnp.exp(scores)
            if triangle:
                key_pos = lax.broadcasted_iota(jnp.int32, (key_count, ROWS), 0)
                position = first_row + lax.broadcasted_iota(jnp.int32, (key_count, ROWS), 1)
                probs = jnp.where(key_pos <= position, probs, 0.0)
            grad_raw = low(probs * grad_probs)
            value_part = jnp.dot(low(probs), grad_half, preferred_element_type=jnp.float32)
            key_part = jnp.dot(grad_raw, query_half, preferred_element_type=jnp.float32)
            query_part = lax.dot_general(
                plain_refs[half][keys, :], grad_raw, ROW_DIMS, preferred_element_type=jnp.float32
            )
            if half == 0:
                query_total, key_total, value_total = (query_part, key_part, value_part)
                continue
            value_acc[keys, :] += value_total + value_part
            key_acc[keys, :] += key_total + key_part
            dq_ref[pl.ds(first_row, ROWS), :] = low(jnp.transpose(query_total + query_part))

    @pl.when(causal == 0)
    def _():
        run(False)

    @pl.when(causal != 0)
    def _():
        run(True)


def fill_backward(length, keys_in, values, key_refs, plain_refs, value_refs):
    lane = lanes_of(keys_in.shape[0])
    left = lane < HS
    for ref, tile in zip(key_refs, key_tiles(keys_in, length, 3)):
        ref[...] = tile
    zero = jnp.zeros((), jnp.float32)
    for ref, tile in zip(plain_refs, half_tiles(wide(keys_in) * SCALE, zero, zero, left)):
        ref[...] = low(tile)

    def ones(start):
        return jnp.where((lane > start) & (lane <= start + 2), 1.0, 0.0)

    for ref, tile in zip(value_refs, half_tiles(wide(values), ones(HS), ones(0), left)):
        ref[...] = low(tile)


def self_backward_kernel(
    scalars,
    packed_ref,
    mixed_ref,
    grad_ref,
    lse_ref,
    out_ref,
    queries_ref,
    dq_ref,
    key_acc,
    value_acc,
    k0,
    k1,
    p0,
    p1,
    v0,
    v1,
):
    slots = packed_ref.shape[0]
    left = lanes_of(slots) < HS
    queries, keys_in, values = pair_of(packed_ref[...], left)
    queries_ref[...] = queries
    fill_backward(scalars[0], keys_in, values, (k0, k1), (p0, p1), (v0, v1))
    attend_backward(
        scalars[1],
        queries_ref,
        (k0, k1),
        (p0, p1),
        (v0, v1),
        mixed_ref,
        grad_ref,
        lse_ref,
        (dq_ref, key_acc, value_acc),
    )
    grad_query = dq_ref[...]
    grad_key = low(swap_halves(key_acc[...]))
    grad_value = low(value_acc[...])
    out_ref[:, :LANES] = jnp.where(left, grad_query, grad_key)
    out_ref[:, LANES : 2 * LANES] = jnp.where(left, grad_value, grad_query)
    out_ref[:, 2 * LANES :] = jnp.where(left, grad_key, grad_value)


def cross_backward_kernel(
    scalars,
    query_ref,
    key_ref,
    value_ref,
    mixed_ref,
    grad_ref,
    lse_ref,
    dq_ref,
    dkv_ref,
    key_acc,
    value_acc,
    k0,
    k1,
    p0,
    p1,
    v0,
    v1,
):
    fill_backward(scalars[0], key_ref[...], value_ref[...], (k0, k1), (p0, p1), (v0, v1))
    attend_backward(
        0,
        query_ref,
        (k0, k1),
        (p0, p1),
        (v0, v1),
        mixed_ref,
        grad_ref,
        lse_ref,
        (dq_ref, key_acc, value_acc),
    )
    dkv_ref[:, :LANES] = low(key_acc[...])
    dkv_ref[:, LANES:] = low(value_acc[...])


def head_call(kernel, scalars, pairs, blocks, outs, scratch, products):
    slots = blocks[0][0].shape[0]

    def spec(width, shift, stride):
        return pl.BlockSpec((slots, width), lambda pair, *_: (0, stride * pair + shift))

    out_specs, out_shape = ([], [])
    for kind, width in outs:
        out_specs.append(spec(width, 0, 1))
        made = jnp.float32 if kind == "wide" else jnp.bfloat16
        out_shape.append(jax.ShapeDtypeStruct((slots, pairs * width), made))
    return pl.pallas_call(
        kernel,
        grid_spec=pltpu.PrefetchScalarGridSpec(
            num_scalar_prefetch=1,
            grid=(pairs,),
            in_specs=[spec(width, shift, stride) for _, width, shift, stride in blocks],
            out_specs=out_specs,
            scratch_shapes=[pltpu.VMEM((slots, LANES), kind) for kind in scratch],
        ),
        out_shape=out_shape,
        compiler_params=pltpu.CompilerParams(
            dimension_semantics=("arbitrary",), vmem_limit_bytes=48 * 1024 * 1024
        ),
        cost_estimate=pl.CostEstimate(
            flops=products * pairs * slots * slots * LANES * 16,
            bytes_accessed=2 * slots * pairs * sum(block[1] for block in blocks),
            transcendentals=2 * pairs * slots * slots,
        ),
    )(scalars, *[block[0] for block in blocks])


BF16 = jnp.bfloat16
F32 = jnp.float32


def self_attention(scalars, packed, first, pairs):
    return head_call(
        self_forward_kernel,
        scalars,
        pairs,
        [(packed, 3 * LANES, first, 1)],
        [("low", LANES), ("wide", LANES)],
        [BF16] * 5,
        2,
    )


def cross_attention(scalars, queries, key_values, first, pairs):
    return head_call(
        cross_forward_kernel,
        scalars,
        pairs,
        [
            (queries, LANES, 0, 1),
            (key_values, LANES, 2 * first, 2),
            (key_values, LANES, 2 * first + 1, 2),
        ],
        [("low", LANES), ("wide", LANES)],
        [BF16] * 4,
        2,
    )


def self_attention_back(scalars, packed, mixed, grads, lse, first, pairs):
    return head_call(
        self_backward_kernel,
        scalars,
        pairs,
        [
            (packed, 3 * LANES, first, 1),
            (mixed, LANES, first, 1),
            (grads, LANES, first, 1),
            (lse, LANES, first, 1),
        ],
        [("low", 3 * LANES)],
        [BF16, BF16, F32, F32] + [BF16] * 6,
        5,
    )[0]


def cross_attention_back(scalars, queries, key_values, mixed, grads, lse, first, pairs):
    return head_call(
        cross_backward_kernel,
        scalars,
        pairs,
        [
            (queries, LANES, 0, 1),
            (key_values, LANES, 2 * first, 2),
            (key_values, LANES, 2 * first + 1, 2),
            (mixed, LANES, 0, 1),
            (grads, LANES, 0, 1),
            (lse, LANES, 0, 1),
        ],
        [("low", LANES), ("low", 2 * LANES)],
        [F32, F32] + [BF16] * 6,
        5,
    )


def rows_nt(rows, weight_rows):
    return lax.dot_general(rows, weight_rows, COL_DIMS, preferred_element_type=jnp.float32)


def rows_nn(rows, weight_rows):
    return jnp.dot(rows, weight_rows, preferred_element_type=jnp.float32)


def rows_tn(left_rows, right_rows):
    return lax.dot_general(left_rows, right_rows, ROW_DIMS, preferred_element_type=jnp.float32)


def gelu_and_slope(values):
    square = values * values
    bend = jnp.tanh(GELU_C * values * (1.0 + 0.044715 * square))
    rise = GELU_C * (1.0 + 3 * 0.044715 * square)
    gate = 0.5 + 0.5 * bend
    return (values * gate, gate * (1.0 + values * (1.0 - bend) * rise))


def feed_kernel(
    alpha_ref,
    low_ref,
    wide_ref,
    in_ref,
    bias_ref,
    down_ref,
    down_shift_ref,
    gain_ref,
    shift_ref,
    hidden_ref,
    slope_ref,
    made_ref,
    norm_ref,
    factor_ref,
    acc,
):
    step = pl.program_id(0)
    slots = low_ref.shape[0]

    @pl.when(step == 0)
    def _():
        acc[...] = alpha_ref[0] * wide_ref[...] + down_shift_ref[...]

    starts = list(range(0, slots, FEED_ROWS))
    waiting = [rows_nt(low_ref[pl.ds(0, FEED_ROWS), :], in_ref[...])]
    for first in starts:
        rows = pl.ds(first, FEED_ROWS)
        if first != starts[-1]:
            waiting.append(rows_nt(low_ref[pl.ds(first + FEED_ROWS, FEED_ROWS), :], in_ref[...]))
        made, slope = gelu_and_slope(waiting.pop(0) + bias_ref[...])
        hidden = low(made)
        hidden_ref[rows, :] = hidden
        slope_ref[rows, :] = low(slope)
        acc[rows, :] += rows_nn(hidden, down_ref[...])

    @pl.when(step == pl.num_programs(0) - 1)
    def _():
        for first in range(0, slots, ROWS):
            rows = pl.ds(first, ROWS)
            made, normed, factor = layer_norm(acc[rows, :], gain_ref[...], shift_ref[...])
            made_ref[rows, :] = low(made)
            norm_ref[rows, :] = normed
            factor_ref[rows, :] = factor


def whole_spec(shape):
    return pl.BlockSpec(shape, lambda *_: (0,) * len(shape))


def feed_call(alpha, rows_low, rows_wide, in_rows, in_shift, down_rows, down_shift, gain, shift):
    slots, width = rows_low.shape
    hidden = in_rows.shape[0]
    block = min(BLOCK, hidden)
    square, row = (whole_spec((slots, width)), whole_spec((1, width)))
    weight = pl.BlockSpec((block, width), lambda step: (step, 0))
    column = pl.BlockSpec((slots, block), lambda step: (0, step))
    return pl.pallas_call(
        feed_kernel,
        grid=(hidden // block,),
        in_specs=[
            pl.BlockSpec(memory_space=pltpu.SMEM),
            square,
            square,
            weight,
            pl.BlockSpec((1, block), lambda step: (0, step)),
            weight,
            row,
            row,
            row,
        ],
        out_specs=[column, column, square, square, whole_spec((slots, 1))],
        out_shape=[
            jax.ShapeDtypeStruct((slots, hidden), BF16),
            jax.ShapeDtypeStruct((slots, hidden), BF16),
            jax.ShapeDtypeStruct((slots, width), BF16),
            jax.ShapeDtypeStruct((slots, width), F32),
            jax.ShapeDtypeStruct((slots, 1), F32),
        ],
        scratch_shapes=[pltpu.VMEM((slots, width), F32)],
        compiler_params=pltpu.CompilerParams(
            dimension_semantics=("arbitrary",), vmem_limit_bytes=56 * 1024 * 1024
        ),
        cost_estimate=pl.CostEstimate(
            flops=4 * slots * width * hidden,
            bytes_accessed=4 * hidden * (width + slots),
            transcendentals=slots * hidden,
        ),
    )(alpha, rows_low, rows_wide, in_rows, in_shift, down_rows, down_shift, gain, shift)


def feed_back_kernel(
    alpha_ref, low_ref, wide_ref, in_ref, down_ref, slope_ref, pre_ref, bias_ref, total_ref, acc
):
    step = pl.program_id(0)
    slots = low_ref.shape[0]

    @pl.when(step == 0)
    def _():
        acc[...] = alpha_ref[0] * wide_ref[...]

    sums = None
    starts = list(range(0, slots, FEED_ROWS))
    waiting = [rows_nt(low_ref[pl.ds(0, FEED_ROWS), :], down_ref[...])]
    for first in starts:
        rows = pl.ds(first, FEED_ROWS)
        if first != starts[-1]:
            waiting.append(rows_nt(low_ref[pl.ds(first + FEED_ROWS, FEED_ROWS), :], down_ref[...]))
        made = waiting.pop(0) * wide(slope_ref[rows, :])
        grad_pre = low(made)
        pre_ref[rows, :] = grad_pre
        part = jnp.sum(wide(grad_pre), axis=0, keepdims=True)
        sums = part if sums is None else sums + part
        acc[rows, :] += rows_nn(grad_pre, in_ref[...])
    bias_ref[...] = sums

    @pl.when(step == pl.num_programs(0) - 1)
    def _():
        total_ref[...] = acc[...]


def feed_back_call(alpha, grad_low, grad_wide, in_rows, down_rows, slopes):
    slots, width = grad_low.shape
    hidden = in_rows.shape[0]
    block = min(BLOCK, hidden)
    square = whole_spec((slots, width))
    weight = pl.BlockSpec((block, width), lambda step: (step, 0))
    column = pl.BlockSpec((slots, block), lambda step: (0, step))
    return pl.pallas_call(
        feed_back_kernel,
        grid=(hidden // block,),
        in_specs=[pl.BlockSpec(memory_space=pltpu.SMEM), square, square, weight, weight, column],
        out_specs=[column, pl.BlockSpec((1, block), lambda step: (0, step)), square],
        out_shape=[
            jax.ShapeDtypeStruct((slots, hidden), BF16),
            jax.ShapeDtypeStruct((1, hidden), F32),
            jax.ShapeDtypeStruct((slots, width), F32),
        ],
        scratch_shapes=[pltpu.VMEM((slots, width), F32)],
        compiler_params=pltpu.CompilerParams(
            dimension_semantics=("arbitrary",), vmem_limit_bytes=56 * 1024 * 1024
        ),
        cost_estimate=pl.CostEstimate(
            flops=4 * slots * width * hidden,
            bytes_accessed=4 * hidden * (width + slots),
            transcendentals=0,
        ),
    )(alpha, grad_low, grad_wide, in_rows, down_rows, slopes)


def norm_back_kernel(limit_ref, grad_ref, norm_ref, factor_ref, gain_ref, made_ref, low_ref, sums_ref):
    step = pl.program_id(0)
    rows = grad_ref.shape[0]
    position = step * rows + lax.broadcasted_iota(jnp.int32, (rows, 1), 0)
    gradient = jnp.where(position < limit_ref[0], wide(grad_ref[...]), 0.0)
    normed = norm_ref[...]
    made, gain_sum, shift_sum = norm_back(gradient, normed, factor_ref[...], gain_ref[...])
    made_ref[...] = made
    low_ref[...] = low(made)
    rows_made = jnp.concatenate(
        [
            gain_sum[None],
            shift_sum[None],
            jnp.sum(made, axis=0, keepdims=True),
            jnp.zeros((5, made.shape[1]), jnp.float32),
        ]
    )

    @pl.when(step == 0)
    def _():
        sums_ref[...] = rows_made

    @pl.when(step != 0)
    def _():
        sums_ref[...] += rows_made


def norm_back_call(limit, gradient, normed, factor, gain):
    slots, width = gradient.shape
    block = pl.BlockSpec((ROWS, width), lambda step, *_: (step, 0))
    return pl.pallas_call(
        norm_back_kernel,
        grid_spec=pltpu.PrefetchScalarGridSpec(
            num_scalar_prefetch=1,
            grid=(slots // ROWS,),
            in_specs=[
                block,
                block,
                pl.BlockSpec((ROWS, 1), lambda step, *_: (step, 0)),
                whole_spec((1, width)),
            ],
            out_specs=[block, block, whole_spec((8, width))],
        ),
        out_shape=[
            jax.ShapeDtypeStruct((slots, width), F32),
            jax.ShapeDtypeStruct((slots, width), BF16),
            jax.ShapeDtypeStruct((8, width), F32),
        ],
        compiler_params=pltpu.CompilerParams(
            dimension_semantics=("arbitrary",), vmem_limit_bytes=32 * 1024 * 1024
        ),
    )(limit, gradient, normed, factor, gain)


def mesh_place():
    return (
        lax.axis_index("dp"),
        lax.axis_index("tensor"),
        lax.axis_size("tensor"),
    )


def greet(unit, place, count):
    partners = [{"tensor": lax.rem(place + d, count)} for d in range(1, count)]
    partners.append({"dp": lax.rem(unit + 2, 4)})
    partners.append({"dp": unit + 1 - 2 * lax.rem(unit, 2)})
    barrier = pltpu.get_barrier_semaphore()
    for partner_id in partners:
        pl.semaphore_signal(barrier, inc=1, device_id=partner_id, device_id_type=MESH)
    pl.semaphore_wait(barrier, len(partners))
    return partners


def remote(source, target, send_sem, recv_sem, device_id):
    return pltpu.make_async_remote_copy(
        src_ref=source,
        dst_ref=target,
        send_sem=send_sem,
        recv_sem=recv_sem,
        device_id=device_id,
        device_id_type=MESH,
    )


def at_slot(ref, paired, half, slot):
    outer, inner = divmod(slot, 2)
    return ref.at[half, outer, :, inner] if paired else ref.at[half, outer, inner]


def gather_kernel(axes, *refs):
    groups = len(axes)
    blocks, own, across = (refs[0], refs[1 : 1 + groups], refs[1 + groups : 1 + 2 * groups])
    rest = refs[1 + 2 * groups :]
    rows, filled = (rest[0], rest[1 : 1 + groups])
    near, far = (0, 1)
    local_sem, block_send, block_recv, ring_send, ring_recv = rest[1 + groups : 6 + groups]
    side_send, side_recv, core_send, core_recv = rest[6 + groups :]
    unit, place, count = mesh_place()
    partners = greet(unit, place, count)
    right, side, core = (partners[0], partners[-2], partners[-1])
    started = []

    def begin(copy):
        copy.start()
        started.append(copy)
        return copy

    local = []

    def begin_local(source, target, index):
        copy = pltpu.make_async_copy(source, target, local_sem.at[index])
        copy.start()
        local.append(copy)

    def slot(half, group, index):
        return at_slot(filled[group], axes[group], half, index)

    def hop(group, step):
        source = own[group] if step == 1 else slot(near, group, step - 1)
        return begin(
            remote(
                source,
                slot(near, group, step),
                ring_send.at[group, step - 1],
                ring_recv.at[group, step - 1],
                right,
            )
        )

    def to_side(group, step):
        return begin(
            remote(
                slot(near, group, step),
                slot(near, group, count + step),
                side_send.at[group, step - 1],
                side_recv.at[group, step - 1],
                side,
            )
        )

    def to_core(group, index, source):
        return begin(
            remote(
                source,
                slot(far, group, index),
                core_send.at[group, index],
                core_recv.at[group, index],
                core,
            )
        )

    hops = {(0, 1): hop(0, 1)}
    block_copies = []
    for distance in range(1, count):
        block_copies.append(
            begin(
                remote(
                    blocks.at[lax.rem(place + distance, count)],
                    rows.at[place],
                    block_send.at[distance - 1],
                    block_recv.at[distance - 1],
                    partners[distance - 1],
                )
            )
        )
    for group in range(1, groups):
        hops[group, 1] = hop(group, 1)
    begin_local(blocks.at[place], rows.at[place], 0)
    cores, sides = ([], {})
    for group in range(groups):
        begin_local(own[group], slot(near, group, 0), 1 + 2 * group)
        begin_local(across[group], slot(near, group, count), 2 + 2 * group)
        cores.append(to_core(group, 0, own[group]))
        cores.append(to_core(group, count, across[group]))
    for step in range(1, count):
        for group in range(groups):
            hops[group, step].wait_recv()
            if step + 1 < count:
                hops[group, step + 1] = hop(group, step + 1)
            sides[group, step] = to_side(group, step)
            cores.append(to_core(group, step, slot(near, group, step)))
            earlier = (group, step - 1)
            if step > 1:
                sides[earlier].wait_recv()
                cores.append(to_core(group, count + step - 1, slot(near, group, count + step - 1)))
    for group in range(groups):
        last = count - 1
        sides[group, last].wait_recv()
        cores.append(to_core(group, count + last, slot(near, group, count + last)))
    for copy in block_copies:
        copy.wait_recv()
    for copy in cores:
        copy.wait_recv()
    for copy in local:
        copy.wait()
    for copy in started:
        copy.wait_send()


def gather_all(blocks, own, across, paired):
    count = lax.axis_size("tensor")
    groups = len(paired)
    anywhere = pl.BlockSpec(memory_space=pl.ANY)
    filled = []
    for array, in_pairs in zip(own, paired):
        if in_pairs:
            shape = (2, count, array.shape[0], 2) + array.shape[1:]
        else:
            shape = (2, count, 2) + array.shape
        filled.append(jax.ShapeDtypeStruct(shape, array.dtype))
    dma = pltpu.SemaphoreType.DMA
    made = pl.pallas_call(
        functools.partial(gather_kernel, paired),
        in_specs=[anywhere] * (1 + 2 * groups),
        out_specs=[anywhere] * (1 + groups),
        out_shape=[jax.ShapeDtypeStruct(blocks.shape, blocks.dtype)] + filled,
        scratch_shapes=[
            dma((1 + 2 * groups,)),
            dma((count - 1,)),
            dma((count - 1,)),
            dma((groups, count - 1)),
            dma((groups, count - 1)),
            dma((groups, count - 1)),
            dma((groups, count - 1)),
            dma((groups, 2 * count)),
            dma((groups, 2 * count)),
        ],
        compiler_params=pltpu.CompilerParams(collective_id=0, has_side_effects=True),
    )(blocks, *own, *across)
    return (made[0], made[1:])


def exchange_kernel(active, blocks, rows, local_sem, send_sem, recv_sem):
    @pl.when(lax.axis_index("section") == active)
    def _():
        place, count = (lax.axis_index("tensor"), lax.axis_size("tensor"))
        partners = [{"tensor": lax.rem(place + d, count)} for d in range(1, count)]
        barrier = pltpu.get_barrier_semaphore()
        for partner_id in partners:
            pl.semaphore_signal(barrier, inc=1, device_id=partner_id, device_id_type=MESH)
        pl.semaphore_wait(barrier, count - 1)
        own = pltpu.make_async_copy(blocks.at[place], rows.at[place], local_sem.at[0])
        own.start()
        copies = []
        for distance in range(1, count):
            copy = remote(
                blocks.at[lax.rem(place + distance, count)],
                rows.at[place],
                send_sem.at[distance - 1],
                recv_sem.at[distance - 1],
                partners[distance - 1],
            )
            copy.start()
            copies.append(copy)
        own.wait()
        for copy in copies:
            copy.wait()


def exchange_in(active, number, blocks):
    count = lax.axis_size("tensor")
    anywhere = pl.BlockSpec(memory_space=pl.ANY)
    return pl.pallas_call(
        functools.partial(exchange_kernel, active),
        in_specs=[anywhere],
        out_specs=anywhere,
        out_shape=jax.ShapeDtypeStruct(blocks.shape, blocks.dtype),
        scratch_shapes=[
            pltpu.SemaphoreType.DMA((1,)),
            pltpu.SemaphoreType.DMA((count - 1,)),
            pltpu.SemaphoreType.DMA((count - 1,)),
        ],
        compiler_params=pltpu.CompilerParams(collective_id=number, has_side_effects=True),
    )(blocks)


def reduce_kernel(paired, depths, *refs):
    groups = len(paired)
    blocks, small = refs[:2]
    made = refs[2 : 2 + groups]
    rest = refs[2 + groups :]
    rows, small_out, out = (rest[0], rest[1], rest[2 : 2 + groups])
    (
        near_buf,
        sums,
        side_in,
        ring_in,
        pair,
        other,
        small_core,
        small_side,
        small_far,
        near_sem,
        core_send,
        core_recv,
        side_send,
        side_recv,
        ring_send,
        ring_recv,
        pair_send,
        pair_recv,
        last_send,
        last_recv,
        out_sem,
        block_sem,
        block_send,
        block_recv,
        tiny_send,
        tiny_recv,
    ) = rest[2 + groups :]
    unit, place, count = mesh_place()
    partners = greet(unit, place, count)
    side, core = (partners[-2], partners[-1])
    units = (
        unit,
        lax.rem(unit + 2, 4),
        unit + 1 - 2 * lax.rem(unit, 2),
        lax.rem(unit + 3 - 2 * lax.rem(unit, 2), 4),
    )
    sends = []

    def begin(copy):
        copy.start()
        sends.append(copy)
        return copy

    chunks = []
    for group in range(groups):
        if not paired[group]:
            for first in range(0, depths[group], CHUNK):
                chunks.append((group, (pl.ds(first, CHUNK),)))
        else:
            for part in range(2):
                for first in range(0, depths[group], CHUNK):
                    chunks.append((group, (part, pl.ds(first, CHUNK))))

    def rows_of(chunk, half):
        group, place_in = chunk
        ref = made[group]
        if paired[group]:
            return ref.at[half, :, place_in[0], :, place_in[1]]
        return ref.at[half, :, :, place_in[0]]

    def result_of(chunk, owner):
        group, place_in = chunk
        if paired[group]:
            return out[group].at[owner, place_in[0], place_in[1]]
        return out[group].at[owner, place_in[0]]

    block_copies = []
    for distance in range(1, count):
        block_copies.append(
            begin(
                remote(
                    blocks.at[lax.rem(place + distance, count)],
                    rows.at[place],
                    block_send.at[distance - 1],
                    block_recv.at[distance - 1],
                    partners[distance - 1],
                )
            )
        )
    own_block = pltpu.make_async_copy(blocks.at[place], rows.at[place], block_sem.at[0])
    own_block.start()
    tiny = begin(remote(small, small_core, tiny_send.at[0], tiny_recv.at[0], core))
    state = {}
    outs = []

    def enter(index):
        chunk = chunks[index]
        copy = pltpu.make_async_copy(
            rows_of(chunk, 0), near_buf.at[index % 3], near_sem.at[index]
        )
        copy.start()
        state["near", index] = copy
        state["core", index] = begin(
            remote(
                rows_of(chunk, 1),
                sums.at[index],
                core_send.at[index],
                core_recv.at[index],
                core,
            )
        )

    def first_sum(index):
        state["near", index].wait()
        state["core", index].wait_recv()
        upper = pl.ds(count // 2, count // 2)
        total = wide(near_buf[index % 3, upper]) + wide(sums[index, upper])
        sums[index, upper] = total.astype(jnp.bfloat16)
        state["side", index] = begin(
            remote(
                sums.at[index, upper],
                side_in.at[index],
                side_send.at[index],
                side_recv.at[index],
                side,
            )
        )

    def second_sum(index):
        state["side", index].wait_recv()
        lower = pl.ds(0, count // 2)
        total = wide(near_buf[index % 3, lower]) + wide(sums[index, lower]) + wide(side_in[index])
        sums[index, lower] = total.astype(jnp.bfloat16)
        for distance in range(1, count):
            state["ring", index, distance] = begin(
                remote(
                    sums.at[index, distance // 2, distance % 2],
                    ring_in.at[index, distance - 1],
                    ring_send.at[index, distance - 1],
                    ring_recv.at[index, distance - 1],
                    partners[count - distance - 1],
                )
            )

    def third_sum(index):
        total = wide(sums[index, 0, 0])
        for distance in range(1, count):
            state["ring", index, distance].wait_recv()
            total = total + wide(ring_in[index, distance - 1])
        pair[index, 0] = total.astype(jnp.bfloat16)
        state["pair", index] = begin(
            remote(
                pair.at[index, 0],
                pair.at[index, 1],
                pair_send.at[index],
                pair_recv.at[index],
                side,
            )
        )

    def spread_pair(index):
        state["pair", index].wait_recv()
        state["last", index] = begin(
            remote(pair.at[index], other.at[index], last_send.at[index], last_recv.at[index], core)
        )

    def leave(index):
        state["last", index].wait_recv()
        chunk = chunks[index]
        found = (pair.at[index, 0], pair.at[index, 1], other.at[index, 0], other.at[index, 1])
        for bits in range(4):
            copy = pltpu.make_async_copy(
                found[bits], result_of(chunk, units[bits]), out_sem.at[index, bits]
            )
            copy.start()
            outs.append(copy)

    stages = (enter, first_sum, second_sum, third_sum, spread_pair, leave)
    for tick in range(len(chunks) + len(stages) - 1):
        for number, stage in enumerate(stages):
            if 0 <= tick - number < len(chunks):
                stage(tick - number)
        if tick == 2:
            tiny.wait_recv()
            small_core[...] += small[...]
            tiny = begin(remote(small_core, small_side, tiny_send.at[1], tiny_recv.at[1], side))
        if tick == 4:
            tiny.wait_recv()
            small_side[...] += small_core[...]
            tiny = [
                begin(
                    remote(
                        small_side,
                        small_far.at[distance - 1],
                        tiny_send.at[1 + distance],
                        tiny_recv.at[1 + distance],
                        partners[distance - 1],
                    )
                )
                for distance in range(1, count)
            ]
        if tick == 6:
            total = small_side[...]
            for distance in range(1, count):
                tiny[distance - 1].wait_recv()
                total = total + small_far[distance - 1]
            small_out[...] = total
    for copy in block_copies:
        copy.wait_recv()
    own_block.wait()
    for copy in outs:
        copy.wait()
    for copy in sends:
        copy.wait_send()


def reduce_all(blocks, small, made, paired):
    count = lax.axis_size("tensor")
    units = lax.axis_size("dp")
    groups = len(paired)
    anywhere = pl.BlockSpec(memory_space=pl.ANY)
    vmem = pl.BlockSpec(memory_space=pltpu.VMEM)
    width = blocks.shape[-1]
    depths = [array.shape[-2] for array in made]
    total = sum(depth * (2 if double else 1) for depth, double in zip(depths, paired)) // CHUNK
    results = []
    for array, double in zip(made, paired):
        shape = (units,) + ((2,) if double else ()) + array.shape[-2:]
        results.append(jax.ShapeDtypeStruct(shape, array.dtype))
    dma = pltpu.SemaphoreType.DMA
    bf16 = jnp.bfloat16
    found = pl.pallas_call(
        functools.partial(reduce_kernel, paired, depths),
        in_specs=[anywhere, vmem] + [anywhere] * groups,
        out_specs=[anywhere, vmem] + [anywhere] * groups,
        out_shape=[
            jax.ShapeDtypeStruct(blocks.shape, blocks.dtype),
            jax.ShapeDtypeStruct(small.shape, small.dtype),
        ]
        + results,
        scratch_shapes=[
            pltpu.VMEM((3, count, 2, CHUNK, width), bf16),
            pltpu.VMEM((total, count, 2, CHUNK, width), bf16),
            pltpu.VMEM((total, count // 2, 2, CHUNK, width), bf16),
            pltpu.VMEM((total, count - 1, CHUNK, width), bf16),
            pltpu.VMEM((total, 2, CHUNK, width), bf16),
            pltpu.VMEM((total, 2, CHUNK, width), bf16),
            pltpu.VMEM(small.shape, small.dtype),
            pltpu.VMEM(small.shape, small.dtype),
            pltpu.VMEM((count - 1,) + small.shape, small.dtype),
            dma((total,)),
            dma((total,)),
            dma((total,)),
            dma((total,)),
            dma((total,)),
            dma((total, count - 1)),
            dma((total, count - 1)),
            dma((total,)),
            dma((total,)),
            dma((total,)),
            dma((total,)),
            dma((total, 4)),
            dma((1,)),
            dma((count - 1,)),
            dma((count - 1,)),
            dma((count + 1,)),
            dma((count + 1,)),
        ],
        compiler_params=pltpu.CompilerParams(
            collective_id=1, has_side_effects=True, vmem_limit_bytes=56 * 1024 * 1024
        ),
    )(blocks, small, *made)
    return (found[0], found[1], found[2:])


def project_norm_kernel(parts, alpha_ref, *refs):
    lefts, weights = (refs[:parts], refs[parts : 2 * parts])
    wide_ref, gain_ref, shift_ref, made_ref, low_ref, norm_ref, factor_ref = refs[2 * parts :]
    total = alpha_ref[0] * wide(wide_ref[...])
    for left, weight in zip(lefts, weights):
        total = total + rows_nn(left[...], weight[...])
    made, normed, factor = layer_norm(total, gain_ref[...], shift_ref[...])
    made_ref[...] = made
    low_ref[...] = low(made)
    norm_ref[...] = normed
    factor_ref[...] = factor


def project_norm(alpha, lefts, weight_rows, rows_wide, gain, shift):
    slots, width = rows_wide.shape
    parts = len(lefts)
    depth = lefts[0].shape[1]

    def rows(columns):
        return pl.BlockSpec((ROWS, columns), lambda step: (step, 0))

    def part_spec(part):
        return pl.BlockSpec((depth, width), lambda step: (part, 0))

    return pl.pallas_call(
        functools.partial(project_norm_kernel, parts),
        grid=(slots // ROWS,),
        in_specs=[pl.BlockSpec(memory_space=pltpu.SMEM)]
        + [rows(depth)] * parts
        + [part_spec(part) for part in range(parts)]
        + [rows(width), whole_spec((1, width)), whole_spec((1, width))],
        out_specs=[rows(width), rows(width), rows(width), rows(1)],
        out_shape=[
            jax.ShapeDtypeStruct((slots, width), F32),
            jax.ShapeDtypeStruct((slots, width), BF16),
            jax.ShapeDtypeStruct((slots, width), F32),
            jax.ShapeDtypeStruct((slots, 1), F32),
        ],
        compiler_params=pltpu.CompilerParams(
            dimension_semantics=("arbitrary",), vmem_limit_bytes=32 * 1024 * 1024
        ),
        cost_estimate=pl.CostEstimate(
            flops=2 * slots * width * depth * parts,
            bytes_accessed=16 * slots * width,
            transcendentals=slots,
        ),
    )(alpha, *lefts, *([weight_rows] * parts), rows_wide, gain, shift)


def project_add_kernel(alpha_ref, left_ref, weight_ref, wide_ref, made_ref):
    made_ref[...] = low(
        alpha_ref[0] * wide(wide_ref[...]) + rows_nn(left_ref[...], weight_ref[...])
    )


def project_add(alpha, left, weight_rows, rows_wide):
    slots, width = rows_wide.shape
    depth = left.shape[1]

    def rows(columns):
        return pl.BlockSpec((ROWS, columns), lambda step: (step, 0))

    return pl.pallas_call(
        project_add_kernel,
        grid=(slots // ROWS,),
        in_specs=[
            pl.BlockSpec(memory_space=pltpu.SMEM),
            rows(depth),
            whole_spec((depth, width)),
            rows(width),
        ],
        out_specs=rows(width),
        out_shape=jax.ShapeDtypeStruct((slots, width), BF16),
        compiler_params=pltpu.CompilerParams(
            dimension_semantics=("arbitrary",), vmem_limit_bytes=40 * 1024 * 1024
        ),
        cost_estimate=pl.CostEstimate(
            flops=2 * slots * width * depth,
            bytes_accessed=6 * slots * width + 2 * depth * (slots + width),
            transcendentals=0,
        ),
    )(alpha, left, weight_rows, rows_wide)


def after(value, *earlier):
    return lax.optimization_barrier((value, earlier))[0]


def sequence_body(
    inputs,
    lengths,
    cotangent,
    qkv_weight,
    attn_out_weight,
    cross_weight,
    ffn_in_weight,
    ffn_in_bias,
    ffn_out_weight,
    ffn_out_bias,
    norm_gain,
    norm_bias,
):
    section = lax.axis_index("section")
    tensor_index = lax.axis_index("tensor")
    tensor_count = lax.axis_size("tensor")
    unit = lax.axis_index("dp")
    units = lax.axis_size("dp")
    decoder = section == 1
    alpha = jnp.where(decoder, ALPHA_DEC, ALPHA_ENC).astype(jnp.float32)
    alpha_row = alpha.reshape(1)
    batches, shard_rows, width = (inputs.shape[1], inputs.shape[2], inputs.shape[3])
    slots = batches * shard_rows
    gains = norm_gain[0].astype(jnp.float32)
    shifts = norm_bias[0].astype(jnp.float32)
    down_shift = ffn_out_bias.astype(jnp.float32)

    def unit_of(array, axis, bits):
        size = array.shape[axis] // units
        piece = lax.dynamic_slice_in_dim(array, (unit ^ bits) * size, size, axis)
        return piece.T if axis == 1 else piece

    bias_size = ffn_in_bias.shape[1] // units

    def units_of(bits):
        return (
            unit_of(qkv_weight[0], 1, bits),
            unit_of(attn_out_weight[0], 0, bits),
            unit_of(ffn_in_weight[0], 1, bits),
            unit_of(ffn_out_weight[0], 0, bits),
            unit_of(cross_weight[0], 1, bits).reshape(2, HS, width),
            jnp.broadcast_to(unit_of(ffn_in_bias[0], 0, bits)[None], (16, bias_size)),
        )

    x, filled = gather_all(
        inputs[0], units_of(0), units_of(2), (False, False, False, False, True, False)
    )
    x = x.reshape(slots, width)
    qkv_rows, out_rows, in_rows, down_rows, cross_rows = [
        array.reshape(-1, width) for array in filled[:5]
    ]
    in_shift = filled[5][:, :, :, 0].reshape(1, -1).astype(jnp.float32)
    cross_parts = cross_rows.reshape(-1, 2, LANES, width)
    half = width // 2

    source_len = lax.dynamic_index_in_dim(lengths[0, :, 0], tensor_index, 0, keepdims=False)
    target_len = lax.dynamic_index_in_dim(lengths[1, :, 0], tensor_index, 0, keepdims=False)
    own_len = jnp.where(decoder, target_len, source_len)
    self_scalars = jnp.stack([own_len, decoder.astype(jnp.int32)])
    cross_scalars = jnp.stack([source_len, jnp.zeros_like(source_len)])
    no_limit = jnp.full((1,), 1 << 20, jnp.int32)
    pairs = width // LANES
    sides = (0, 1)

    qkv = low(rows_nt(x, qkv_rows))
    mixed, lse_self = self_attention(self_scalars, qkv, 0, pairs)
    resid_a, a_low, norm_a, factor_a = project_norm(
        alpha_row, [mixed], out_rows, x, gains[0:1], shifts[0:1]
    )

    def zeros_like_of(branch):
        shapes = jax.eval_shape(branch)
        return lambda: jax.tree.map(lambda leaf: jnp.zeros(leaf.shape, leaf.dtype), shapes)

    def dec_query():
        first = cross_parts[:, 0].reshape(-1, width)
        return tuple(low(rows_nt(a_low, first[side * half : side * half + half])) for side in sides)

    query_sent = lax.cond(decoder, dec_query, zeros_like_of(dec_query))
    query_held = [lax.ppermute(piece, "section", [(1, 0)]) for piece in query_sent]
    cotangent_rows = exchange_in(1, 2, after(cotangent, query_held)).reshape(slots, width)

    def feed(rows_low, rows_wide):
        return feed_call(
            alpha_row,
            rows_low,
            rows_wide,
            in_rows,
            in_shift,
            down_rows,
            down_shift,
            gains[2:3],
            shifts[2:3],
        )

    def enc_feed():
        hidden, slopes, memory_low, norm_y, factor_y = feed(a_low, resid_a)
        key_values = low(rows_nt(memory_low, cross_rows))
        return (hidden, slopes, memory_low, norm_y, factor_y, key_values)

    hidden_e, slopes_e, memory_low, norm_e, factor_e, key_values = lax.cond(
        decoder, zeros_like_of(enc_feed), enc_feed
    )

    mixed_c, lse_c, mixed_held = ([], [], [])
    for side in sides:

        def enc_mix():
            return tuple(
                cross_attention(
                    cross_scalars, query_held[side], key_values, side * pairs // 2, pairs // 2
                )
            )

        mix_made, lse_made = lax.cond(decoder, zeros_like_of(enc_mix), enc_mix)
        mixed_c.append(mix_made)
        lse_c.append(lse_made)
        mixed_held.append(lax.ppermute(mix_made, "section", [(0, 1)]))

    def sharded(rows):
        return rows.reshape(batches, shard_rows, width)

    outputs_e = exchange_in(0, 3, after(sharded(memory_low), mixed_held))
    mixed_held = after(mixed_held, outputs_e)

    def dec_middle():
        cross_second = cross_parts[:, 1].reshape(-1, width)
        resid_c, c_low, norm_c, factor_c = project_norm(
            alpha_row, mixed_held, cross_second, resid_a, gains[1:2], shifts[1:2]
        )
        hidden, slopes, decoded_low, norm_y, factor_y = feed(c_low, resid_c)
        grad_y, grad_low, sums_y = norm_back_call(
            target_len.reshape(1), cotangent_rows, norm_y, factor_y, gains[2:3]
        )
        grad_pre, bias_sum, grad_c = feed_back_call(
            alpha_row, grad_low, grad_y, in_rows, down_rows, slopes
        )
        grad_mid, mid_low, sums_c = norm_back_call(
            no_limit, grad_c, norm_c, factor_c, gains[1:2]
        )
        grad_mixed_c = tuple(
            low(rows_nt(mid_low, cross_second[side * half : side * half + half]))
            for side in sides
        )
        return (
            decoded_low,
            hidden,
            c_low,
            grad_low,
            grad_pre,
            bias_sum,
            grad_mid,
            mid_low,
            grad_mixed_c,
            sums_y,
            sums_c,
        )

    (
        decoded_low,
        hidden_d,
        c_low,
        grad_low_d,
        grad_pre_d,
        bias_sum_d,
        grad_mid,
        mid_low,
        grad_mixed_c,
        sums_yd,
        sums_cd,
    ) = lax.cond(decoder, dec_middle, zeros_like_of(dec_middle))
    grad_mixed_held = [lax.ppermute(piece, "section", [(1, 0)]) for piece in grad_mixed_c]

    grad_query_held, grad_kv = ([], [])
    for side in sides:

        def enc_cross():
            return tuple(
                cross_attention_back(
                    cross_scalars,
                    query_held[side],
                    key_values,
                    mixed_c[side],
                    grad_mixed_held[side],
                    lse_c[side],
                    side * pairs // 2,
                    pairs // 2,
                )
            )

        query_made, kv_made = lax.cond(decoder, zeros_like_of(enc_cross), enc_cross)
        grad_kv.append(kv_made)
        grad_query_held.append(lax.ppermute(query_made, "section", [(0, 1)]))

    def enc_back():
        grad_memory = rows_nn(grad_kv[0], cross_rows[:width]) + rows_nn(
            grad_kv[1], cross_rows[width:]
        )
        grad_y, grad_low, sums_y = norm_back_call(
            no_limit, grad_memory, norm_e, factor_e, gains[2:3]
        )
        grad_pre, bias_sum, grad_a = feed_back_call(
            alpha_row, grad_low, grad_y, in_rows, down_rows, slopes_e
        )
        return (grad_low, grad_pre, bias_sum, grad_a, sums_y)

    grad_low_e, grad_pre_e, bias_sum_e, grad_a_e, sums_ye = lax.cond(
        decoder, zeros_like_of(enc_back), enc_back
    )

    outputs_d = exchange_in(1, 4, after(sharded(decoded_low), grad_mixed_held))
    grad_query_held = after(grad_query_held, outputs_d)
    outputs = jnp.where(decoder, outputs_d, outputs_e)

    grad_query_held = after(grad_query_held, grad_a_e)

    def enc_norm():
        made = [rows_tn(piece, memory_low) for piece in grad_kv]
        return tuple(norm_back_call(no_limit, grad_a_e, norm_a, factor_a, gains[0:1])) + (
            low(jnp.concatenate(made)),
        )

    def dec_norm():
        grad_query = jnp.concatenate(grad_query_held, axis=1)
        cross_first = cross_parts[:, 0].reshape(-1, width)
        grad_a = alpha * grad_mid + rows_nn(grad_query, cross_first)
        mixed_all = jnp.concatenate(mixed_held, axis=1)
        made = [rows_tn(grad_query, a_low), rows_tn(mixed_all, mid_low)]
        made = [piece.reshape(-1, 1, LANES, width) for piece in made]
        return tuple(norm_back_call(no_limit, grad_a, norm_a, factor_a, gains[0:1])) + (
            low(jnp.concatenate(made, axis=1)).reshape(-1, width),
        )

    grad_r, r_low, sums_a, cross_made = lax.cond(decoder, dec_norm, enc_norm)
    bias_sum = jnp.where(decoder, bias_sum_d, bias_sum_e)
    sums_y = jnp.where(decoder, sums_yd, sums_ye)

    def down_grads():
        return lax.cond(
            decoder,
            lambda: low(rows_tn(hidden_d, grad_low_d)),
            lambda: low(rows_tn(hidden_e, grad_low_e)),
        )

    def in_grads():
        return lax.cond(
            decoder,
            lambda: low(rows_tn(grad_pre_d, c_low)),
            lambda: low(rows_tn(grad_pre_e, a_low)),
        )

    grad_mixed = low(rows_nt(r_low, out_rows))
    grad_qkv = self_attention_back(self_scalars, qkv, mixed, grad_mixed, lse_self, 0, pairs)
    grad_x = project_add(alpha_row, grad_qkv, qkv_rows, grad_r)

    slot_bits = jnp.asarray([0, 2, 1, 3], jnp.int32)[:, None]
    slot_unit = unit ^ slot_bits
    slot_tensor = (tensor_index - lax.iota(jnp.int32, tensor_count)[None]) % tensor_count
    slot_index = (slot_tensor * units + slot_unit).reshape(-1)
    hot = (slot_index[None, :] == lax.iota(jnp.int32, slot_index.shape[0])[:, None]).astype(
        jnp.float32
    )
    shift_abs = jnp.dot(
        hot, bias_sum.reshape(-1, bias_size), precision=lax.Precision.HIGHEST
    ).reshape(-1, width)
    small = jnp.concatenate([sums_a[:2], sums_cd[:2], sums_y[:3], shift_abs])
    small = jnp.pad(small, ((0, -small.shape[0] % 8), (0, 0)))
    made = (
        low(rows_tn(grad_qkv, x)),
        low(rows_tn(mixed, r_low)),
        in_grads(),
        down_grads(),
        cross_made,
    )
    input_rows, small, grads = reduce_all(
        sharded(grad_x),
        small,
        [array.reshape(like.shape) for array, like in zip(made, filled)],
        (False, False, False, False, True),
    )
    input_grad = input_rows.astype(jnp.float32)
    qkv_grad, out_grad, in_grad, down_grad, cross_grad = [
        array.astype(jnp.float32) for array in grads
    ]
    in_shift_grad = lax.dynamic_index_in_dim(
        small[7:11].reshape(tensor_count, -1), tensor_index, 0, keepdims=False
    )

    def columns(ordered):
        return ordered.reshape(-1, width).T[None]

    return (
        outputs[None],
        input_grad[None],
        columns(qkv_grad),
        out_grad.reshape(1, -1, width),
        columns(cross_grad),
        columns(in_grad),
        in_shift_grad[None],
        down_grad.reshape(1, -1, width),
        small[6][None],
        small[jnp.asarray([0, 2, 4])][None],
        small[jnp.asarray([1, 3, 5])][None],
    )


def solution(mesh):
    placed = (
        P("section", None, ("dp", "tensor"), None),
        P(None, None, "dp"),
        P(None, ("dp", "tensor"), None),
        P("section", None, "tensor"),
        P("section", "tensor", None),
        P("section", None, "tensor"),
        P("section", None, "tensor"),
        P("section", "tensor"),
        P("section", "tensor", None),
        P("section", None),
        P("section", None, None),
        P("section", None, None),
    )
    returned = (
        P("section", None, ("dp", "tensor"), None),
        P("section", None, ("dp", "tensor"), None),
        P("section", None, "tensor"),
        P("section", "tensor", None),
        P("section", None, "tensor"),
        P("section", None, "tensor"),
        P("section", "tensor"),
        P("section", "tensor", None),
        P("section", None),
        P("section", None, None),
        P("section", None, None),
    )
    sizes = dict(mesh.shape)

    def whole(*arrays):
        batches, sequences = arrays[1].shape[1:]
        heads = arrays[3].shape[2] // (3 * HS)
        group = sizes["dp"] * sizes["tensor"]
        one_each = batches == sizes["tensor"] and sizes["dp"] == 4 and sequences == sizes["dp"] and heads % group == 0
        chosen = sequence_body if one_each else body
        return jax.shard_map(
            chosen, mesh=mesh, in_specs=placed, out_specs=returned, check_vma=False
        )(*arrays)

    return whole
```

```python
import functools

import jax
import jax.numpy as jnp
from jax import lax
from jax.experimental import pallas as pl
from jax.experimental.pallas import tpu as pltpu
from jax.sharding import PartitionSpec as P

HS = 64
QBLOCK = 512


ALPHA_ENC = 0.81 * (100.0**5) ** (1.0 / 16.0)
ALPHA_DEC = (3.0 * 100.0) ** 0.25
EPS = 1e-05
NEG = -1e30
ROW_DIMS = (((0,), (0,)), ((), ()))
COL_DIMS = (((1,), (1,)), ((), ()))
LANES = 2 * HS
ROWS = 256
CHUNK = 64
AHEAD = 1
FEED_ROWS = 512
BLOCK = 1024
MESH = pl.DeviceIdType.MESH
SCALE = HS ** (-0.5)
GELU_C = (2.0 / 3.141592653589793) ** 0.5


def from_behind(block, axis, distance):
    devices = range(lax.axis_size(axis))
    route = [(i - distance, i) for i in devices if i - distance in devices]
    return lax.ppermute(block, axis, route)


def layer_norm(values, gain_row, shift_row):
    centered = values - jnp.mean(values, axis=-1, keepdims=True)
    factor = lax.rsqrt(jnp.mean(centered * centered, axis=-1, keepdims=True) + EPS)
    normed = centered * factor
    return (normed * gain_row + shift_row, normed, factor)


def norm_back(gradient, normed, factor, gain_row):
    scaled = gradient * gain_row
    centred = (
        scaled
        - jnp.mean(scaled, axis=-1, keepdims=True)
        - normed * jnp.mean(scaled * normed, axis=-1, keepdims=True)
    )
    return (centred * factor, jnp.sum(gradient * normed, axis=0), jnp.sum(gradient, axis=0))


def visible(first_row, row_count, key_count, seq_lengths, causal):
    key_pos = lax.broadcasted_iota(jnp.int32, (1, row_count, key_count), 2)
    query_pos = first_row + lax.broadcasted_iota(jnp.int32, (1, row_count, key_count), 1)
    inside = key_pos < seq_lengths[:, None, None]
    return inside & ((key_pos <= query_pos) | jnp.logical_not(causal))


def attend(queries, keys_in, values, seq_lengths, causal):
    key_count = queries.shape[1]
    score_scale = queries.shape[3] ** (-0.5)
    row_block = min(QBLOCK, key_count)
    mixed_parts, lse_parts = ([], [])
    for first_row in range(0, key_count, row_block):
        allowed = visible(first_row, row_block, key_count, seq_lengths, causal)
        raw_scores = jnp.einsum(
            "bqhe,bkhe->bhqk",
            queries[:, first_row : first_row + row_block],
            keys_in,
            preferred_element_type=jnp.float32,
        )
        scores = jnp.where(allowed[:, None], raw_scores * score_scale, NEG)
        row_max = jnp.max(scores, axis=-1, keepdims=True)
        expo_vals = jnp.exp(scores - row_max)
        row_total = jnp.sum(expo_vals, axis=-1, keepdims=True)
        weights = (expo_vals / row_total).astype(jnp.bfloat16)
        mixed_block = jnp.einsum(
            "bhqk,bkhe->bqhe", weights, values, preferred_element_type=jnp.float32
        )
        mixed_parts.append(mixed_block.astype(jnp.bfloat16))
        lse_parts.append(row_max + jnp.log(row_total))
    return (jnp.concatenate(mixed_parts, axis=1), jnp.concatenate(lse_parts, axis=2))


def attend_back(grad_mixed, queries, keys_in, values, log_totals, seq_lengths, causal):
    key_count = queries.shape[1]
    score_scale = queries.shape[3] ** (-0.5)
    row_block = min(QBLOCK, key_count)
    query_parts = []
    grad_keys = jnp.zeros(keys_in.shape, jnp.float32)
    grad_values = jnp.zeros(values.shape, jnp.float32)
    for first_row in range(0, key_count, row_block):
        query_part = queries[:, first_row : first_row + row_block]
        grad_part = grad_mixed[:, first_row : first_row + row_block]
        allowed = visible(first_row, row_block, key_count, seq_lengths, causal)
        raw_scores = jnp.einsum(
            "bqhe,bkhe->bhqk", query_part, keys_in, preferred_element_type=jnp.float32
        )
        scores = jnp.where(allowed[:, None], raw_scores * score_scale, NEG)
        probs = jnp.exp(scores - log_totals[:, :, first_row : first_row + row_block])
        grad_probs = jnp.einsum(
            "bqhe,bkhe->bhqk", grad_part, values, preferred_element_type=jnp.float32
        )
        grad_scores = probs * (grad_probs - jnp.sum(probs * grad_probs, axis=-1, keepdims=True))
        grad_raw = (grad_scores * score_scale).astype(jnp.bfloat16)
        query_parts.append(
            jnp.einsum("bhqk,bkhe->bqhe", grad_raw, keys_in, preferred_element_type=jnp.float32)
        )
        grad_keys = grad_keys + jnp.einsum(
            "bhqk,bqhe->bkhe", grad_raw, query_part, preferred_element_type=jnp.float32
        )
        grad_values = grad_values + jnp.einsum(
            "bhqk,bqhe->bkhe",
            probs.astype(jnp.bfloat16),
            grad_part,
            preferred_element_type=jnp.float32,
        )
    return (jnp.concatenate(query_parts, axis=1), grad_keys, grad_values)


def ffn_forward(rows_in, in_proj, in_shift, down_proj):
    pre_act = jnp.dot(rows_in, in_proj, preferred_element_type=jnp.float32) + in_shift
    hidden = jax.nn.gelu(pre_act).astype(jnp.bfloat16)
    return (pre_act, jnp.dot(hidden, down_proj, preferred_element_type=jnp.float32))


def ffn_backward(grad_in, rows_in, pre_act, in_proj, down_proj):
    activated, slope_back = jax.vjp(jax.nn.gelu, pre_act)
    hidden = activated.astype(jnp.bfloat16)
    grad_down = lax.dot_general(hidden, grad_in, ROW_DIMS, preferred_element_type=jnp.float32)
    grad_hidden = lax.dot_general(grad_in, down_proj, COL_DIMS, preferred_element_type=jnp.float32)
    grad_pre = slope_back(grad_hidden)[0].astype(jnp.bfloat16)
    grad_shift = jnp.sum(grad_pre.astype(jnp.float32), axis=0)
    grad_inner = lax.dot_general(rows_in, grad_pre, ROW_DIMS, preferred_element_type=jnp.float32)
    grad_rows_out = lax.dot_general(grad_pre, in_proj, COL_DIMS, preferred_element_type=jnp.float32)
    return (grad_rows_out, grad_inner, grad_shift, grad_down)


def gather_rows(shard):
    return lax.all_gather(shard, "tensor", axis=0, tiled=True)


def sum_rows(partial_value):
    return lax.psum_scatter(partial_value, "tensor", scatter_dimension=0, tiled=True)


def ffn_input_rows(shard):
    return lax.all_gather(shard, "tensor", axis=0, tiled=True)


def ffn_sum_rows(partial_value):
    return lax.psum_scatter(
        partial_value.astype(jnp.bfloat16), "tensor", scatter_dimension=0, tiled=True
    ).astype(jnp.float32)


def grad_rows(shard):
    return lax.all_gather(shard, "tensor", axis=0, tiled=True)


def grad_sums(partial_value):
    return lax.psum_scatter(
        partial_value.astype(jnp.bfloat16), "tensor", scatter_dimension=0, tiled=True
    ).astype(jnp.float32)


def ffn_grad_rows(shard):
    return lax.all_gather(shard, "tensor", axis=0, tiled=True)


def ffn_grad_sums(partial_value):
    return lax.psum_scatter(
        partial_value.astype(jnp.bfloat16), "tensor", scatter_dimension=0, tiled=True
    ).astype(jnp.float32)


def body(
    inputs,
    lengths,
    cotangent,
    qkv_weight,
    attn_out_weight,
    cross_weight,
    ffn_in_weight,
    ffn_in_bias,
    ffn_out_weight,
    ffn_out_bias,
    norm_gain,
    norm_bias,
):
    tensor_count = lax.axis_size("tensor")
    section = lax.axis_index("section")
    tensor_index = lax.axis_index("tensor")
    decoder = section == 1
    alpha = jnp.where(decoder, ALPHA_DEC, ALPHA_ENC).astype(jnp.float32)
    batches, shard_rows, width = (inputs.shape[1], inputs.shape[2], inputs.shape[3])
    seq_count = lengths.shape[2]
    full_rows = shard_rows * tensor_count
    slots = full_rows // seq_count
    qkv_proj = qkv_weight[0]
    head_local = qkv_proj.shape[1] // (3 * HS)
    head_cols = head_local * HS
    out_proj = attn_out_weight[0]
    cross_proj = cross_weight[0]
    cross_split = cross_proj.reshape(width, head_local, 2, HS)
    first_cols = cross_split[:, :, 0].reshape(width, head_cols)
    second_cols = cross_split[:, :, 1].reshape(width, head_cols)
    in_proj = ffn_in_weight[0]
    in_shift = ffn_in_bias[0].astype(jnp.float32)
    down_proj = ffn_out_weight[0]
    hidden_width = in_proj.shape[1]
    down_shift = ffn_out_bias[0].astype(jnp.float32)
    gains = norm_gain[0].astype(jnp.float32)
    shifts = norm_bias[0].astype(jnp.float32)
    own_lengths = lax.dynamic_index_in_dim(lengths, section, 0, keepdims=False)
    source_lengths = lengths[0]
    row_index = tensor_index * shard_rows + lax.iota(jnp.int32, shard_rows)
    row_seq = row_index // slots
    row_pos = row_index % slots
    seq_ids = lax.iota(jnp.int32, seq_count)
    lse_shape = (seq_count, head_local, slots, 1)

    def zeros_float(shape):
        return jnp.zeros(shape, jnp.float32)

    def zeros_low(shape):
        return jnp.zeros(shape, jnp.bfloat16)

    def to_heads(flat_rows):
        return flat_rows.reshape(seq_count, slots, flat_rows.shape[1] // HS, HS)

    def to_rows(split_rows):
        return split_rows.reshape(full_rows, -1)

    def cross_forward(query_rows, kv_source, source_len):
        kv_split = kv_source.reshape(seq_count, slots, head_local, 2, HS)
        query_c = jnp.dot(query_rows, first_cols, preferred_element_type=jnp.float32).astype(
            jnp.bfloat16
        )
        mixed_c, lse_cross = attend(
            to_heads(query_c), kv_split[:, :, :, 0], kv_split[:, :, :, 1], source_len, False
        )
        mixed_c = to_rows(mixed_c)
        partial_value = lax.dot_general(
            mixed_c, second_cols, COL_DIMS, preferred_element_type=jnp.float32
        )
        return (query_c, mixed_c, lse_cross, partial_value)

    kv_held = zeros_low((full_rows, 2 * head_cols))
    kv_ticks, kept_ticks, out_ticks = ([], [], [])
    for tick_index in range(batches + 1):
        batch = jnp.clip(tick_index - section, 0, batches - 1)
        x_shard = lax.dynamic_index_in_dim(inputs[0], batch, 0, keepdims=False)
        own_len = lax.dynamic_index_in_dim(own_lengths, batch, 0, keepdims=False)
        source_len = lax.dynamic_index_in_dim(source_lengths, batch, 0, keepdims=False)
        x_full = gather_rows(x_shard)
        qkv = jnp.dot(x_full, qkv_proj, preferred_element_type=jnp.float32).astype(jnp.bfloat16)
        qkv_split = qkv.reshape(seq_count, slots, head_local, 3, HS)
        mixed, lse_self = attend(
            qkv_split[:, :, :, 0], qkv_split[:, :, :, 1], qkv_split[:, :, :, 2], own_len, decoder
        )
        mixed = to_rows(mixed)
        attn_sum = sum_rows(jnp.dot(mixed, out_proj, preferred_element_type=jnp.float32))
        resid_a, norm_a, factor_a = layer_norm(
            alpha * x_shard.astype(jnp.float32) + attn_sum, gains[0], shifts[0]
        )
        a_shard = resid_a.astype(jnp.bfloat16)
        a_full = gather_rows(a_shard)

        def enc_second():
            hidden_made, partial_value = ffn_forward(a_full, in_proj, in_shift, down_proj)
            return (
                hidden_made,
                zeros_low((full_rows, head_cols)),
                zeros_low((full_rows, head_cols)),
                zeros_float(lse_shape),
                partial_value,
            )

        def dec_second():
            query_c, mixed_c, lse_cross, partial_value = cross_forward(a_full, kv_held, source_len)
            return (
                zeros_float((full_rows, hidden_width)),
                query_c,
                mixed_c,
                lse_cross,
                partial_value,
            )

        hidden_enc, query_c, mixed_c, lse_cross, partial_value = lax.cond(
            decoder, dec_second, enc_second
        )
        second_sum = sum_rows(partial_value)
        resid_ye, norm_ye, factor_ye = layer_norm(
            alpha * resid_a + second_sum + down_shift, gains[2], shifts[2]
        )
        resid_c, norm_c, factor_c = layer_norm(alpha * resid_a + second_sum, gains[1], shifts[1])
        wide_rows = ffn_input_rows(jnp.where(decoder, resid_c, resid_ye).astype(jnp.bfloat16))

        def enc_third():
            kv_made = jnp.dot(wide_rows, cross_proj, preferred_element_type=jnp.float32).astype(
                jnp.bfloat16
            )
            return (
                kv_made,
                zeros_float((full_rows, hidden_width)),
                zeros_float((full_rows, width)),
            )

        def dec_third():
            hidden_made, partial_made = ffn_forward(wide_rows, in_proj, in_shift, down_proj)
            return (zeros_low((full_rows, 2 * head_cols)), hidden_made, partial_made)

        kv_out, hidden_dec, partial_third = lax.cond(decoder, dec_third, enc_third)
        third_sum = ffn_sum_rows(partial_third)
        resid_yd, norm_yd, factor_yd = layer_norm(
            alpha * resid_c + third_sum + down_shift, gains[2], shifts[2]
        )
        resid_y = jnp.where(decoder, resid_yd, resid_ye)
        norm_y = jnp.where(decoder, norm_yd, norm_ye)
        factor_y = jnp.where(decoder, factor_yd, factor_ye)
        hidden = jnp.where(decoder, hidden_dec, hidden_enc)
        ffn_rows = jnp.where(decoder, wide_rows, a_full)
        y_shard = resid_y.astype(jnp.bfloat16)
        kv_held = from_behind(kv_out, "section", 1)
        kv_ticks.append(kv_held)
        out_ticks.append(y_shard)
        kept_ticks.append(
            dict(
                x_rows=x_full,
                qkv=qkv,
                mixed=mixed,
                lse_self=lse_self,
                a_rows=a_full,
                kv_rows=wide_rows,
                ffn_rows=ffn_rows,
                hidden=hidden,
                query_c=query_c,
                mixed_c=mixed_c,
                lse_cross=lse_cross,
                norm_a=norm_a,
                factor_a=factor_a,
                norm_c=norm_c,
                factor_c=factor_c,
                norm_y=norm_y,
                factor_y=factor_y,
            )
        )
    kept_all = jax.tree.map(lambda *leaves: jnp.stack(leaves), *kept_ticks)
    kv_stack = jnp.stack(kv_ticks)
    outputs = lax.dynamic_slice_in_dim(jnp.stack(out_ticks), section, batches, 0)
    totals = dict(
        qkv=zeros_float(qkv_proj.shape),
        outer=zeros_float(out_proj.shape),
        cross=zeros_float(cross_proj.shape),
        inner=zeros_float(in_proj.shape),
        inner_shift=zeros_float(in_shift.shape),
        down=zeros_float(down_proj.shape),
        down_shift=zeros_float(down_shift.shape),
        gain=zeros_float(gains.shape),
        shift=zeros_float(shifts.shape),
    )
    zero_ffn = (
        zeros_float(in_proj.shape),
        zeros_float(in_shift.shape),
        zeros_float(down_proj.shape),
    )
    zero_cross = zeros_float((width, 2 * head_cols))
    dkv_held = zeros_low((full_rows, 2 * head_cols))
    grad_ticks = []
    for tick_index in range(batches + 1):
        batch_raw = batches - tick_index - section
        live = (batch_raw >= 0) & (batch_raw < batches)
        batch = jnp.clip(batch_raw, 0, batches - 1)
        kept = jax.tree.map(
            lambda leaf_value: lax.dynamic_index_in_dim(
                leaf_value, batch + section, 0, keepdims=False
            ),
            kept_all,
        )
        own_len = lax.dynamic_index_in_dim(own_lengths, batch, 0, keepdims=False)
        source_len = lax.dynamic_index_in_dim(source_lengths, batch, 0, keepdims=False)
        kv_now = lax.dynamic_index_in_dim(kv_stack, batch, 0, keepdims=False)
        kv_split = kv_now.reshape(seq_count, slots, head_local, 2, HS)
        own_rows = jnp.sum(
            jnp.where(row_seq[:, None] == seq_ids[None, :], own_len[None, :], 0), axis=1
        )
        grad_top = lax.dynamic_index_in_dim(cotangent, batch, 0, keepdims=False).astype(jnp.float32)
        grad_top = jnp.where((row_pos < own_rows)[:, None], grad_top, 0.0)
        grad_r3d, gain_yd, shift_yd = norm_back(
            grad_top, kept["norm_y"], kept["factor_y"], gains[2]
        )
        dkv_now = dkv_held

        def kv_back():
            partial_value = lax.dot_general(
                dkv_now, cross_proj, COL_DIMS, preferred_element_type=jnp.float32
            )
            grad_cross_enc = lax.dot_general(
                kept["kv_rows"], dkv_now, ROW_DIMS, preferred_element_type=jnp.float32
            )
            return (partial_value, grad_cross_enc)

        def cross_back(grad_full):
            grad_mixed_c = jnp.dot(
                grad_full, second_cols, preferred_element_type=jnp.float32
            ).astype(jnp.bfloat16)
            grad_second = lax.dot_general(
                grad_full, kept["mixed_c"], ROW_DIMS, preferred_element_type=jnp.float32
            )
            grad_qc, grad_kc, grad_vc = attend_back(
                to_heads(grad_mixed_c),
                to_heads(kept["query_c"]),
                kv_split[:, :, :, 0],
                kv_split[:, :, :, 1],
                kept["lse_cross"],
                source_len,
                False,
            )
            grad_qc = to_rows(grad_qc).astype(jnp.bfloat16)
            grad_first = lax.dot_general(
                kept["a_rows"], grad_qc, ROW_DIMS, preferred_element_type=jnp.float32
            )
            partial_value = lax.dot_general(
                grad_qc, first_cols, COL_DIMS, preferred_element_type=jnp.float32
            )
            grad_kv = (
                jnp.stack([grad_kc, grad_vc], axis=3)
                .astype(jnp.bfloat16)
                .reshape(full_rows, 2 * head_cols)
            )
            grad_cross_dec = jnp.stack(
                [
                    grad_first.reshape(width, head_local, HS),
                    grad_second.reshape(width, head_local, HS),
                ],
                axis=2,
            ).reshape(width, 2 * head_cols)
            return (partial_value, grad_cross_dec, grad_kv)

        first_full = grad_rows(jnp.where(decoder, grad_r3d, 0.0).astype(jnp.bfloat16))

        def enc_first():
            partial_value, grad_cross_enc = kv_back()
            return (partial_value, grad_cross_enc) + zero_ffn

        def dec_first():
            partial_value, inner_made, shift_made, down_made = ffn_backward(
                first_full, kept["ffn_rows"], kept["hidden"], in_proj, down_proj
            )
            return (partial_value, zero_cross, inner_made, shift_made, down_made)

        partial_one, cross_enc, inner_one, inner_shift_one, down_one = lax.cond(
            decoder, dec_first, enc_first
        )
        first_sum = grad_sums(partial_one)
        grad_r3e, gain_ye, shift_ye = norm_back(
            first_sum, kept["norm_y"], kept["factor_y"], gains[2]
        )
        grad_r2, gain_c, shift_c = norm_back(
            alpha * grad_r3d + first_sum, kept["norm_c"], kept["factor_c"], gains[1]
        )
        grad_r3 = jnp.where(decoder, grad_r3d, grad_r3e)
        gain_y = jnp.where(decoder, gain_yd, gain_ye)
        shift_y = jnp.where(decoder, shift_yd, shift_ye)
        middle_grad = jnp.where(decoder, grad_r2, grad_r3e)
        second_full = ffn_grad_rows(middle_grad.astype(jnp.bfloat16))

        def enc_second():
            partial_value, inner_made, shift_made, down_made = ffn_backward(
                second_full, kept["ffn_rows"], kept["hidden"], in_proj, down_proj
            )
            return (
                partial_value,
                inner_made,
                shift_made,
                down_made,
                zero_cross,
                zeros_low((full_rows, 2 * head_cols)),
            )

        def dec_second():
            partial_value, grad_cross_dec, grad_kv_made = cross_back(second_full)
            return (partial_value,) + zero_ffn + (grad_cross_dec, grad_kv_made)

        partial_two, inner_two, inner_shift_two, down_two, cross_dec, grad_kv = lax.cond(
            decoder, dec_second, enc_second
        )
        grad_a = alpha * middle_grad + ffn_grad_sums(partial_two)
        dkv_held = from_behind(grad_kv, "section", -1)
        grad_r1, gain_a, shift_a = norm_back(grad_a, kept["norm_a"], kept["factor_a"], gains[0])
        attn_full = grad_rows(grad_r1.astype(jnp.bfloat16))
        grad_mixed = lax.dot_general(
            attn_full, out_proj, COL_DIMS, preferred_element_type=jnp.float32
        ).astype(jnp.bfloat16)
        grad_outer = lax.dot_general(
            kept["mixed"], attn_full, ROW_DIMS, preferred_element_type=jnp.float32
        )
        qkv_split = kept["qkv"].reshape(seq_count, slots, head_local, 3, HS)
        grad_q, grad_k, grad_v = attend_back(
            to_heads(grad_mixed),
            qkv_split[:, :, :, 0],
            qkv_split[:, :, :, 1],
            qkv_split[:, :, :, 2],
            kept["lse_self"],
            own_len,
            decoder,
        )
        grad_qkv = (
            jnp.stack([grad_q, grad_k, grad_v], axis=3)
            .astype(jnp.bfloat16)
            .reshape(full_rows, 3 * head_cols)
        )
        grad_qkv_proj = lax.dot_general(
            kept["x_rows"], grad_qkv, ROW_DIMS, preferred_element_type=jnp.float32
        )
        grad_x = alpha * grad_r1 + grad_sums(
            lax.dot_general(grad_qkv, qkv_proj, COL_DIMS, preferred_element_type=jnp.float32)
        )
        grad_ticks.append(grad_x)
        gain_step = jnp.stack([gain_a, jnp.where(decoder, gain_c, 0.0), gain_y])
        shift_step = jnp.stack([shift_a, jnp.where(decoder, shift_c, 0.0), shift_y])
        steps = dict(
            qkv=grad_qkv_proj,
            outer=grad_outer,
            cross=cross_enc + cross_dec,
            inner=inner_one + inner_two,
            inner_shift=inner_shift_one + inner_shift_two,
            down=down_one + down_two,
            down_shift=jnp.sum(grad_r3, axis=0),
            gain=gain_step,
            shift=shift_step,
        )
        totals = {name: totals[name] + jnp.where(live, steps[name], 0.0) for name in totals}
    input_grad = lax.dynamic_slice_in_dim(jnp.stack(grad_ticks[::-1]), section, batches, 0)
    inner_total, inner_shift_total, down_total = (
        totals["inner"],
        totals["inner_shift"],
        totals["down"],
    )
    summed = (
        lax.psum(totals["qkv"].astype(jnp.bfloat16), "dp").astype(jnp.float32),
        lax.psum(totals["outer"].astype(jnp.bfloat16), "dp").astype(jnp.float32),
        lax.psum(totals["cross"].astype(jnp.bfloat16), "dp").astype(jnp.float32),
        lax.psum(inner_total.astype(jnp.bfloat16), "dp").astype(jnp.float32),
        lax.psum(inner_shift_total.astype(jnp.bfloat16), "dp").astype(jnp.float32),
        lax.psum(down_total.astype(jnp.bfloat16), "dp").astype(jnp.float32),
    )
    vectors = lax.psum((totals["gain"], totals["shift"], totals["down_shift"]), ("dp", "tensor"))
    return (
        outputs[None],
        input_grad[None],
        summed[0][None],
        summed[1][None],
        summed[2][None],
        summed[3][None],
        summed[4][None],
        summed[5][None],
        vectors[2][None],
        vectors[0][None],
        vectors[1][None],
    )


def lanes_of(rows):
    return lax.broadcasted_iota(jnp.int32, (rows, LANES), 1)


def swap_halves(tile):
    return pltpu.roll(tile, HS, 1)


def pair_of(packed, left):
    first, second, third = (packed[:, :LANES], packed[:, LANES : 2 * LANES], packed[:, 2 * LANES :])
    swap = lambda tile: jnp.concatenate([tile[:, HS:], tile[:, :HS]], axis=1)
    queries = jnp.where(left, first, second)
    keys_in = jnp.where(left, swap(first), swap(third))
    values = jnp.where(left, second, third)
    return (queries, keys_in, values)


def wide(value):
    return value.astype(jnp.float32)


def low(values):
    return values.astype(jnp.bfloat16)


def half_tiles(tile, fill_right, fill_left, left):
    return (jnp.where(left, tile, fill_right), jnp.where(left, fill_left, tile))


def key_tiles(keys_in, length, ones):
    slots = keys_in.shape[0]
    lane = lanes_of(slots)
    hidden = lax.broadcasted_iota(jnp.int32, (slots, LANES), 0) >= length
    left = lane < HS

    def fill(start):
        outside = jnp.where((lane == start) & hidden, NEG, 0.0)
        return jnp.where((lane > start) & (lane <= start + ones), 1.0, outside)

    first, second = half_tiles(wide(keys_in), fill(HS), fill(0), left)
    return (low(first), low(second))


def attend_forward(length, causal, queries_ref, key_refs, value_refs, mixed_ref, lse_ref):
    slots = queries_ref.shape[0]
    lane = lanes_of(ROWS)
    left = lane < HS

    def score(first_row, key_count, triangle, half):
        queries = wide(queries_ref[pl.ds(first_row, ROWS), :]) * SCALE
        start = HS if half == 0 else 0
        mine = left if half == 0 else jnp.logical_not(left)
        augmented = low(jnp.where(mine, queries, jnp.where(lane == start, 1.0, 0.0)))
        scores = lax.dot_general(
            augmented,
            key_refs[half][pl.ds(0, key_count), :],
            COL_DIMS,
            preferred_element_type=jnp.float32,
        )
        if triangle:
            column = lax.broadcasted_iota(jnp.int32, (ROWS, key_count), 1)
            row = first_row + lax.broadcasted_iota(jnp.int32, (ROWS, key_count), 0)
            scores = jnp.where(column <= row, scores, NEG)
        return scores

    def finish(first_row, totals, tops):
        norm = swap_halves(jnp.where(left, totals[1], totals[0]))
        mixed_ref[pl.ds(first_row, ROWS), :] = low(jnp.where(left, totals[0], totals[1]) / norm)
        logs = jnp.where(left, tops[0], tops[1]) + jnp.log(norm)
        lse_ref[pl.ds(first_row, ROWS), :] = swap_halves(logs)

    def run(triangle):
        items = []
        for first_row in range(0, slots, ROWS):
            for half in range(2):
                items.append((first_row, first_row + ROWS if triangle else slots, triangle, half))
        waiting = [score(*item) for item in items[:AHEAD]]
        totals, tops = ([], [])
        for number, item in enumerate(items):
            if number + AHEAD < len(items):
                waiting.append(score(*items[number + AHEAD]))
            scores = waiting.pop(0)
            top = jnp.max(scores, axis=1, keepdims=True)
            tops.append(top)
            totals.append(
                jnp.dot(
                    low(jnp.exp(scores - top)),
                    value_refs[item[3]][pl.ds(0, item[1]), :],
                    preferred_element_type=jnp.float32,
                )
            )
            if item[3] == 1:
                finish(item[0], totals, tops)
                totals, tops = ([], [])

    @pl.when(causal == 0)
    def _():
        run(False)

    @pl.when(causal != 0)
    def _():
        run(True)


def fill_forward(length, keys_in, values, key_refs, value_refs):
    left = lanes_of(keys_in.shape[0]) < HS
    for ref, tile in zip(key_refs, key_tiles(keys_in, length, 0)):
        ref[...] = tile
    one = jnp.ones((), values.dtype)
    for ref, tile in zip(value_refs, half_tiles(values, one, one, left)):
        ref[...] = tile


def self_forward_kernel(scalars, packed_ref, mixed_ref, lse_ref, queries_ref, k0, k1, v0, v1):
    left = lanes_of(packed_ref.shape[0]) < HS
    queries, keys_in, values = pair_of(packed_ref[...], left)
    queries_ref[...] = queries
    fill_forward(scalars[0], keys_in, values, (k0, k1), (v0, v1))
    attend_forward(scalars[0], scalars[1], queries_ref, (k0, k1), (v0, v1), mixed_ref, lse_ref)


def cross_forward_kernel(
    scalars, query_ref, key_ref, value_ref, mixed_ref, lse_ref, k0, k1, v0, v1
):
    fill_forward(scalars[0], key_ref[...], value_ref[...], (k0, k1), (v0, v1))
    attend_forward(scalars[0], 0, query_ref, (k0, k1), (v0, v1), mixed_ref, lse_ref)


def attend_backward(
    causal, queries_ref, key_refs, plain_refs, value_refs, mixed_ref, grad_ref, lse_ref, outs
):
    dq_ref, key_acc, value_acc = outs
    slots = queries_ref.shape[0]
    lane = lanes_of(ROWS)
    left = lane < HS
    key_acc[...] = jnp.zeros_like(key_acc)
    value_acc[...] = jnp.zeros_like(value_acc)

    def extra(start, terms, one):
        filled = jnp.where(lane == start, one, 0.0)
        for number, term in enumerate(terms):
            filled = jnp.where(lane == start + 1 + number, -term, filled)
        return filled

    def parts(value, count):
        found = []
        for _ in range(count):
            found.append(wide(low(value)))
            value = value - found[-1]
        return found

    def prepare(first_row, key_count, triangle, half):
        rows = pl.ds(first_row, ROWS)
        keys = pl.ds(0, key_count)
        mine = left if half == 0 else jnp.logical_not(left)
        start = HS if half == 0 else 0
        queries = wide(queries_ref[rows, :]) * SCALE
        grads = wide(grad_ref[rows, :])
        product = grads * wide(mixed_ref[rows, :])
        delta = jnp.sum(jnp.where(mine, product, 0.0), axis=1, keepdims=True)
        log_parts = parts(lse_ref[rows, :], 3)
        query_aug = low(jnp.where(mine, queries, extra(start, log_parts, 1.0)))
        grad_aug = low(jnp.where(mine, grads, extra(start, parts(delta, 2), 0.0)))
        scores = lax.dot_general(
            key_refs[half][keys, :], query_aug, COL_DIMS, preferred_element_type=jnp.float32
        )
        grad_probs = lax.dot_general(
            value_refs[half][keys, :], grad_aug, COL_DIMS, preferred_element_type=jnp.float32
        )
        return (
            scores,
            grad_probs,
            low(jnp.where(mine, queries, 0.0)),
            low(jnp.where(mine, grads, 0.0)),
        )

    def run(triangle):
        items = []
        for first_row in range(0, slots, ROWS):
            for half in range(2):
                items.append((first_row, first_row + ROWS if triangle else slots, triangle, half))
        waiting = [prepare(*item) for item in items[:AHEAD]]
        query_total, key_total, value_total = (None, None, None)
        for number, (first_row, key_count, _, half) in enumerate(items):
            if number + AHEAD < len(items):
                waiting.append(prepare(*items[number + AHEAD]))
            scores, grad_probs, query_half, grad_half = waiting.pop(0)
            keys = pl.ds(0, key_count)
            probs = jnp.exp(scores)
            if triangle:
                key_pos = lax.broadcasted_iota(jnp.int32, (key_count, ROWS), 0)
                position = first_row + lax.broadcasted_iota(jnp.int32, (key_count, ROWS), 1)
                probs = jnp.where(key_pos <= position, probs, 0.0)
            grad_raw = low(probs * grad_probs)
            value_part = jnp.dot(low(probs), grad_half, preferred_element_type=jnp.float32)
            key_part = jnp.dot(grad_raw, query_half, preferred_element_type=jnp.float32)
            query_part = lax.dot_general(
                plain_refs[half][keys, :], grad_raw, ROW_DIMS, preferred_element_type=jnp.float32
            )
            if half == 0:
                query_total, key_total, value_total = (query_part, key_part, value_part)
                continue
            value_acc[keys, :] += value_total + value_part
            key_acc[keys, :] += key_total + key_part
            dq_ref[pl.ds(first_row, ROWS), :] = low(jnp.transpose(query_total + query_part))

    @pl.when(causal == 0)
    def _():
        run(False)

    @pl.when(causal != 0)
    def _():
        run(True)


def fill_backward(length, keys_in, values, key_refs, plain_refs, value_refs):
    lane = lanes_of(keys_in.shape[0])
    left = lane < HS
    for ref, tile in zip(key_refs, key_tiles(keys_in, length, 3)):
        ref[...] = tile
    zero = jnp.zeros((), jnp.float32)
    for ref, tile in zip(plain_refs, half_tiles(wide(keys_in) * SCALE, zero, zero, left)):
        ref[...] = low(tile)

    def ones(start):
        return jnp.where((lane > start) & (lane <= start + 2), 1.0, 0.0)

    for ref, tile in zip(value_refs, half_tiles(wide(values), ones(HS), ones(0), left)):
        ref[...] = low(tile)


def self_backward_kernel(
    scalars,
    packed_ref,
    mixed_ref,
    grad_ref,
    lse_ref,
    out_ref,
    queries_ref,
    dq_ref,
    key_acc,
    value_acc,
    k0,
    k1,
    p0,
    p1,
    v0,
    v1,
):
    slots = packed_ref.shape[0]
    left = lanes_of(slots) < HS
    queries, keys_in, values = pair_of(packed_ref[...], left)
    queries_ref[...] = queries
    fill_backward(scalars[0], keys_in, values, (k0, k1), (p0, p1), (v0, v1))
    attend_backward(
        scalars[1],
        queries_ref,
        (k0, k1),
        (p0, p1),
        (v0, v1),
        mixed_ref,
        grad_ref,
        lse_ref,
        (dq_ref, key_acc, value_acc),
    )
    grad_query = dq_ref[...]
    grad_key = low(swap_halves(key_acc[...]))
    grad_value = low(value_acc[...])
    out_ref[:, :LANES] = jnp.where(left, grad_query, grad_key)
    out_ref[:, LANES : 2 * LANES] = jnp.where(left, grad_value, grad_query)
    out_ref[:, 2 * LANES :] = jnp.where(left, grad_key, grad_value)


def cross_backward_kernel(
    scalars,
    query_ref,
    key_ref,
    value_ref,
    mixed_ref,
    grad_ref,
    lse_ref,
    dq_ref,
    dkv_ref,
    key_acc,
    value_acc,
    k0,
    k1,
    p0,
    p1,
    v0,
    v1,
):
    fill_backward(scalars[0], key_ref[...], value_ref[...], (k0, k1), (p0, p1), (v0, v1))
    attend_backward(
        0,
        query_ref,
        (k0, k1),
        (p0, p1),
        (v0, v1),
        mixed_ref,
        grad_ref,
        lse_ref,
        (dq_ref, key_acc, value_acc),
    )
    dkv_ref[:, :LANES] = low(key_acc[...])
    dkv_ref[:, LANES:] = low(value_acc[...])


def head_call(kernel, scalars, pairs, blocks, outs, scratch, products):
    slots = blocks[0][0].shape[0]

    def spec(width, shift, stride):
        return pl.BlockSpec((slots, width), lambda pair, *_: (0, stride * pair + shift))

    out_specs, out_shape = ([], [])
    for kind, width in outs:
        out_specs.append(spec(width, 0, 1))
        made = jnp.float32 if kind == "wide" else jnp.bfloat16
        out_shape.append(jax.ShapeDtypeStruct((slots, pairs * width), made))
    return pl.pallas_call(
        kernel,
        grid_spec=pltpu.PrefetchScalarGridSpec(
            num_scalar_prefetch=1,
            grid=(pairs,),
            in_specs=[spec(width, shift, stride) for _, width, shift, stride in blocks],
            out_specs=out_specs,
            scratch_shapes=[pltpu.VMEM((slots, LANES), kind) for kind in scratch],
        ),
        out_shape=out_shape,
        compiler_params=pltpu.CompilerParams(
            dimension_semantics=("arbitrary",), vmem_limit_bytes=48 * 1024 * 1024
        ),
        cost_estimate=pl.CostEstimate(
            flops=products * pairs * slots * slots * LANES * 16,
            bytes_accessed=2 * slots * pairs * sum(block[1] for block in blocks),
            transcendentals=2 * pairs * slots * slots,
        ),
    )(scalars, *[block[0] for block in blocks])


BF16 = jnp.bfloat16
F32 = jnp.float32


def self_attention(scalars, packed, first, pairs):
    return head_call(
        self_forward_kernel,
        scalars,
        pairs,
        [(packed, 3 * LANES, first, 1)],
        [("low", LANES), ("wide", LANES)],
        [BF16] * 5,
        2,
    )


def cross_attention(scalars, queries, key_values, first, pairs):
    return head_call(
        cross_forward_kernel,
        scalars,
        pairs,
        [
            (queries, LANES, 0, 1),
            (key_values, LANES, 2 * first, 2),
            (key_values, LANES, 2 * first + 1, 2),
        ],
        [("low", LANES), ("wide", LANES)],
        [BF16] * 4,
        2,
    )


def self_attention_back(scalars, packed, mixed, grads, lse, first, pairs):
    return head_call(
        self_backward_kernel,
        scalars,
        pairs,
        [
            (packed, 3 * LANES, first, 1),
            (mixed, LANES, first, 1),
            (grads, LANES, first, 1),
            (lse, LANES, first, 1),
        ],
        [("low", 3 * LANES)],
        [BF16, BF16, F32, F32] + [BF16] * 6,
        5,
    )[0]


def cross_attention_back(scalars, queries, key_values, mixed, grads, lse, first, pairs):
    return head_call(
        cross_backward_kernel,
        scalars,
        pairs,
        [
            (queries, LANES, 0, 1),
            (key_values, LANES, 2 * first, 2),
            (key_values, LANES, 2 * first + 1, 2),
            (mixed, LANES, 0, 1),
            (grads, LANES, 0, 1),
            (lse, LANES, 0, 1),
        ],
        [("low", LANES), ("low", 2 * LANES)],
        [F32, F32] + [BF16] * 6,
        5,
    )


def rows_nt(rows, weight_rows):
    return lax.dot_general(rows, weight_rows, COL_DIMS, preferred_element_type=jnp.float32)


def rows_nn(rows, weight_rows):
    return jnp.dot(rows, weight_rows, preferred_element_type=jnp.float32)


def rows_tn(left_rows, right_rows):
    return lax.dot_general(left_rows, right_rows, ROW_DIMS, preferred_element_type=jnp.float32)


def gelu_and_slope(values):
    square = values * values
    bend = jnp.tanh(GELU_C * values * (1.0 + 0.044715 * square))
    rise = GELU_C * (1.0 + 3 * 0.044715 * square)
    gate = 0.5 + 0.5 * bend
    return (values * gate, gate * (1.0 + values * (1.0 - bend) * rise))


def feed_kernel(
    alpha_ref,
    low_ref,
    wide_ref,
    in_ref,
    bias_ref,
    down_ref,
    down_shift_ref,
    gain_ref,
    shift_ref,
    hidden_ref,
    slope_ref,
    made_ref,
    norm_ref,
    factor_ref,
    acc,
):
    step = pl.program_id(0)
    slots = low_ref.shape[0]

    @pl.when(step == 0)
    def _():
        acc[...] = alpha_ref[0] * wide_ref[...] + down_shift_ref[...]

    starts = list(range(0, slots, FEED_ROWS))
    waiting = [rows_nt(low_ref[pl.ds(0, FEED_ROWS), :], in_ref[...])]
    for first in starts:
        rows = pl.ds(first, FEED_ROWS)
        if first != starts[-1]:
            waiting.append(rows_nt(low_ref[pl.ds(first + FEED_ROWS, FEED_ROWS), :], in_ref[...]))
        made, slope = gelu_and_slope(waiting.pop(0) + bias_ref[...])
        hidden = low(made)
        hidden_ref[rows, :] = hidden
        slope_ref[rows, :] = low(slope)
        acc[rows, :] += rows_nn(hidden, down_ref[...])

    @pl.when(step == pl.num_programs(0) - 1)
    def _():
        for first in range(0, slots, ROWS):
            rows = pl.ds(first, ROWS)
            made, normed, factor = layer_norm(acc[rows, :], gain_ref[...], shift_ref[...])
            made_ref[rows, :] = low(made)
            norm_ref[rows, :] = normed
            factor_ref[rows, :] = factor


def whole_spec(shape):
    return pl.BlockSpec(shape, lambda *_: (0,) * len(shape))


def feed_call(alpha, rows_low, rows_wide, in_rows, in_shift, down_rows, down_shift, gain, shift):
    slots, width = rows_low.shape
    hidden = in_rows.shape[0]
    block = min(BLOCK, hidden)
    square, row = (whole_spec((slots, width)), whole_spec((1, width)))
    weight = pl.BlockSpec((block, width), lambda step: (step, 0))
    column = pl.BlockSpec((slots, block), lambda step: (0, step))
    return pl.pallas_call(
        feed_kernel,
        grid=(hidden // block,),
        in_specs=[
            pl.BlockSpec(memory_space=pltpu.SMEM),
            square,
            square,
            weight,
            pl.BlockSpec((1, block), lambda step: (0, step)),
            weight,
            row,
            row,
            row,
        ],
        out_specs=[column, column, square, square, whole_spec((slots, 1))],
        out_shape=[
            jax.ShapeDtypeStruct((slots, hidden), BF16),
            jax.ShapeDtypeStruct((slots, hidden), BF16),
            jax.ShapeDtypeStruct((slots, width), BF16),
            jax.ShapeDtypeStruct((slots, width), F32),
            jax.ShapeDtypeStruct((slots, 1), F32),
        ],
        scratch_shapes=[pltpu.VMEM((slots, width), F32)],
        compiler_params=pltpu.CompilerParams(
            dimension_semantics=("arbitrary",), vmem_limit_bytes=56 * 1024 * 1024
        ),
        cost_estimate=pl.CostEstimate(
            flops=4 * slots * width * hidden,
            bytes_accessed=4 * hidden * (width + slots),
            transcendentals=slots * hidden,
        ),
    )(alpha, rows_low, rows_wide, in_rows, in_shift, down_rows, down_shift, gain, shift)


def feed_back_kernel(
    alpha_ref, low_ref, wide_ref, in_ref, down_ref, slope_ref, pre_ref, bias_ref, total_ref, acc
):
    step = pl.program_id(0)
    slots = low_ref.shape[0]

    @pl.when(step == 0)
    def _():
        acc[...] = alpha_ref[0] * wide_ref[...]

    sums = None
    starts = list(range(0, slots, FEED_ROWS))
    waiting = [rows_nt(low_ref[pl.ds(0, FEED_ROWS), :], down_ref[...])]
    for first in starts:
        rows = pl.ds(first, FEED_ROWS)
        if first != starts[-1]:
            waiting.append(rows_nt(low_ref[pl.ds(first + FEED_ROWS, FEED_ROWS), :], down_ref[...]))
        made = waiting.pop(0) * wide(slope_ref[rows, :])
        grad_pre = low(made)
        pre_ref[rows, :] = grad_pre
        part = jnp.sum(wide(grad_pre), axis=0, keepdims=True)
        sums = part if sums is None else sums + part
        acc[rows, :] += rows_nn(grad_pre, in_ref[...])
    bias_ref[...] = sums

    @pl.when(step == pl.num_programs(0) - 1)
    def _():
        total_ref[...] = acc[...]


def feed_back_call(alpha, grad_low, grad_wide, in_rows, down_rows, slopes):
    slots, width = grad_low.shape
    hidden = in_rows.shape[0]
    block = min(BLOCK, hidden)
    square = whole_spec((slots, width))
    weight = pl.BlockSpec((block, width), lambda step: (step, 0))
    column = pl.BlockSpec((slots, block), lambda step: (0, step))
    return pl.pallas_call(
        feed_back_kernel,
        grid=(hidden // block,),
        in_specs=[pl.BlockSpec(memory_space=pltpu.SMEM), square, square, weight, weight, column],
        out_specs=[column, pl.BlockSpec((1, block), lambda step: (0, step)), square],
        out_shape=[
            jax.ShapeDtypeStruct((slots, hidden), BF16),
            jax.ShapeDtypeStruct((1, hidden), F32),
            jax.ShapeDtypeStruct((slots, width), F32),
        ],
        scratch_shapes=[pltpu.VMEM((slots, width), F32)],
        compiler_params=pltpu.CompilerParams(
            dimension_semantics=("arbitrary",), vmem_limit_bytes=56 * 1024 * 1024
        ),
        cost_estimate=pl.CostEstimate(
            flops=4 * slots * width * hidden,
            bytes_accessed=4 * hidden * (width + slots),
            transcendentals=0,
        ),
    )(alpha, grad_low, grad_wide, in_rows, down_rows, slopes)


def norm_back_kernel(limit_ref, grad_ref, norm_ref, factor_ref, gain_ref, made_ref, low_ref, sums_ref):
    step = pl.program_id(0)
    rows = grad_ref.shape[0]
    position = step * rows + lax.broadcasted_iota(jnp.int32, (rows, 1), 0)
    gradient = jnp.where(position < limit_ref[0], wide(grad_ref[...]), 0.0)
    normed = norm_ref[...]
    made, gain_sum, shift_sum = norm_back(gradient, normed, factor_ref[...], gain_ref[...])
    made_ref[...] = made
    low_ref[...] = low(made)
    rows_made = jnp.concatenate(
        [
            gain_sum[None],
            shift_sum[None],
            jnp.sum(made, axis=0, keepdims=True),
            jnp.zeros((5, made.shape[1]), jnp.float32),
        ]
    )

    @pl.when(step == 0)
    def _():
        sums_ref[...] = rows_made

    @pl.when(step != 0)
    def _():
        sums_ref[...] += rows_made


def norm_back_call(limit, gradient, normed, factor, gain):
    slots, width = gradient.shape
    block = pl.BlockSpec((ROWS, width), lambda step, *_: (step, 0))
    return pl.pallas_call(
        norm_back_kernel,
        grid_spec=pltpu.PrefetchScalarGridSpec(
            num_scalar_prefetch=1,
            grid=(slots // ROWS,),
            in_specs=[
                block,
                block,
                pl.BlockSpec((ROWS, 1), lambda step, *_: (step, 0)),
                whole_spec((1, width)),
            ],
            out_specs=[block, block, whole_spec((8, width))],
        ),
        out_shape=[
            jax.ShapeDtypeStruct((slots, width), F32),
            jax.ShapeDtypeStruct((slots, width), BF16),
            jax.ShapeDtypeStruct((8, width), F32),
        ],
        compiler_params=pltpu.CompilerParams(
            dimension_semantics=("arbitrary",), vmem_limit_bytes=32 * 1024 * 1024
        ),
    )(limit, gradient, normed, factor, gain)


def mesh_place():
    return (
        lax.axis_index("dp"),
        lax.axis_index("tensor"),
        lax.axis_size("tensor"),
    )


def greet(unit, place, count):
    partners = [{"tensor": lax.rem(place + d, count)} for d in range(1, count)]
    partners.append({"dp": lax.rem(unit + 2, 4)})
    partners.append({"dp": unit + 1 - 2 * lax.rem(unit, 2)})
    barrier = pltpu.get_barrier_semaphore()
    for partner_id in partners:
        pl.semaphore_signal(barrier, inc=1, device_id=partner_id, device_id_type=MESH)
    pl.semaphore_wait(barrier, len(partners))
    return partners


def remote(source, target, send_sem, recv_sem, device_id):
    return pltpu.make_async_remote_copy(
        src_ref=source,
        dst_ref=target,
        send_sem=send_sem,
        recv_sem=recv_sem,
        device_id=device_id,
        device_id_type=MESH,
    )


def at_slot(ref, paired, half, slot):
    outer, inner = divmod(slot, 2)
    return ref.at[half, outer, :, inner] if paired else ref.at[half, outer, inner]


def gather_kernel(axes, *refs):
    groups = len(axes)
    blocks, own, across = (refs[0], refs[1 : 1 + groups], refs[1 + groups : 1 + 2 * groups])
    rest = refs[1 + 2 * groups :]
    rows, filled = (rest[0], rest[1 : 1 + groups])
    near, far = (0, 1)
    local_sem, block_send, block_recv, ring_send, ring_recv = rest[1 + groups : 6 + groups]
    side_send, side_recv, core_send, core_recv = rest[6 + groups :]
    unit, place, count = mesh_place()
    partners = greet(unit, place, count)
    right, side, core = (partners[0], partners[-2], partners[-1])
    started = []

    def begin(copy):
        copy.start()
        started.append(copy)
        return copy

    local = []

    def begin_local(source, target, index):
        copy = pltpu.make_async_copy(source, target, local_sem.at[index])
        copy.start()
        local.append(copy)

    def slot(half, group, index):
        return at_slot(filled[group], axes[group], half, index)

    def hop(group, step):
        source = own[group] if step == 1 else slot(near, group, step - 1)
        return begin(
            remote(
                source,
                slot(near, group, step),
                ring_send.at[group, step - 1],
                ring_recv.at[group, step - 1],
                right,
            )
        )

    def to_side(group, step):
        return begin(
            remote(
                slot(near, group, step),
                slot(near, group, count + step),
                side_send.at[group, step - 1],
                side_recv.at[group, step - 1],
                side,
            )
        )

    def to_core(group, index, source):
        return begin(
            remote(
                source,
                slot(far, group, index),
                core_send.at[group, index],
                core_recv.at[group, index],
                core,
            )
        )

    hops = {(0, 1): hop(0, 1)}
    block_copies = []
    for distance in range(1, count):
        block_copies.append(
            begin(
                remote(
                    blocks.at[lax.rem(place + distance, count)],
                    rows.at[place],
                    block_send.at[distance - 1],
                    block_recv.at[distance - 1],
                    partners[distance - 1],
                )
            )
        )
    for group in range(1, groups):
        hops[group, 1] = hop(group, 1)
    begin_local(blocks.at[place], rows.at[place], 0)
    cores, sides = ([], {})
    for group in range(groups):
        begin_local(own[group], slot(near, group, 0), 1 + 2 * group)
        begin_local(across[group], slot(near, group, count), 2 + 2 * group)
        cores.append(to_core(group, 0, own[group]))
        cores.append(to_core(group, count, across[group]))
    for step in range(1, count):
        for group in range(groups):
            hops[group, step].wait_recv()
            if step + 1 < count:
                hops[group, step + 1] = hop(group, step + 1)
            sides[group, step] = to_side(group, step)
            cores.append(to_core(group, step, slot(near, group, step)))
            earlier = (group, step - 1)
            if step > 1:
                sides[earlier].wait_recv()
                cores.append(to_core(group, count + step - 1, slot(near, group, count + step - 1)))
    for group in range(groups):
        last = count - 1
        sides[group, last].wait_recv()
        cores.append(to_core(group, count + last, slot(near, group, count + last)))
    for copy in block_copies:
        copy.wait_recv()
    for copy in cores:
        copy.wait_recv()
    for copy in local:
        copy.wait()
    for copy in started:
        copy.wait_send()


def gather_all(blocks, own, across, paired):
    count = lax.axis_size("tensor")
    groups = len(paired)
    anywhere = pl.BlockSpec(memory_space=pl.ANY)
    filled = []
    for array, in_pairs in zip(own, paired):
        if in_pairs:
            shape = (2, count, array.shape[0], 2) + array.shape[1:]
        else:
            shape = (2, count, 2) + array.shape
        filled.append(jax.ShapeDtypeStruct(shape, array.dtype))
    dma = pltpu.SemaphoreType.DMA
    made = pl.pallas_call(
        functools.partial(gather_kernel, paired),
        in_specs=[anywhere] * (1 + 2 * groups),
        out_specs=[anywhere] * (1 + groups),
        out_shape=[jax.ShapeDtypeStruct(blocks.shape, blocks.dtype)] + filled,
        scratch_shapes=[
            dma((1 + 2 * groups,)),
            dma((count - 1,)),
            dma((count - 1,)),
            dma((groups, count - 1)),
            dma((groups, count - 1)),
            dma((groups, count - 1)),
            dma((groups, count - 1)),
            dma((groups, 2 * count)),
            dma((groups, 2 * count)),
        ],
        compiler_params=pltpu.CompilerParams(collective_id=0, has_side_effects=True),
    )(blocks, *own, *across)
    return (made[0], made[1:])


def exchange_kernel(active, blocks, rows, local_sem, send_sem, recv_sem):
    @pl.when(lax.axis_index("section") == active)
    def _():
        place, count = (lax.axis_index("tensor"), lax.axis_size("tensor"))
        partners = [{"tensor": lax.rem(place + d, count)} for d in range(1, count)]
        barrier = pltpu.get_barrier_semaphore()
        for partner_id in partners:
            pl.semaphore_signal(barrier, inc=1, device_id=partner_id, device_id_type=MESH)
        pl.semaphore_wait(barrier, count - 1)
        own = pltpu.make_async_copy(blocks.at[place], rows.at[place], local_sem.at[0])
        own.start()
        copies = []
        for distance in range(1, count):
            copy = remote(
                blocks.at[lax.rem(place + distance, count)],
                rows.at[place],
                send_sem.at[distance - 1],
                recv_sem.at[distance - 1],
                partners[distance - 1],
            )
            copy.start()
            copies.append(copy)
        own.wait()
        for copy in copies:
            copy.wait()


def exchange_in(active, number, blocks):
    count = lax.axis_size("tensor")
    anywhere = pl.BlockSpec(memory_space=pl.ANY)
    return pl.pallas_call(
        functools.partial(exchange_kernel, active),
        in_specs=[anywhere],
        out_specs=anywhere,
        out_shape=jax.ShapeDtypeStruct(blocks.shape, blocks.dtype),
        scratch_shapes=[
            pltpu.SemaphoreType.DMA((1,)),
            pltpu.SemaphoreType.DMA((count - 1,)),
            pltpu.SemaphoreType.DMA((count - 1,)),
        ],
        compiler_params=pltpu.CompilerParams(collective_id=number, has_side_effects=True),
    )(blocks)


def reduce_kernel(paired, depths, *refs):
    groups = len(paired)
    blocks, small = refs[:2]
    made = refs[2 : 2 + groups]
    rest = refs[2 + groups :]
    rows, small_out, out = (rest[0], rest[1], rest[2 : 2 + groups])
    (
        near_buf,
        sums,
        side_in,
        ring_in,
        pair,
        other,
        small_core,
        small_side,
        small_far,
        near_sem,
        core_send,
        core_recv,
        side_send,
        side_recv,
        ring_send,
        ring_recv,
        pair_send,
        pair_recv,
        last_send,
        last_recv,
        out_sem,
        block_sem,
        block_send,
        block_recv,
        tiny_send,
        tiny_recv,
    ) = rest[2 + groups :]
    unit, place, count = mesh_place()
    partners = greet(unit, place, count)
    side, core = (partners[-2], partners[-1])
    units = (
        unit,
        lax.rem(unit + 2, 4),
        unit + 1 - 2 * lax.rem(unit, 2),
        lax.rem(unit + 3 - 2 * lax.rem(unit, 2), 4),
    )
    sends = []

    def begin(copy):
        copy.start()
        sends.append(copy)
        return copy

    chunks = []
    for group in range(groups):
        if not paired[group]:
            for first in range(0, depths[group], CHUNK):
                chunks.append((group, (pl.ds(first, CHUNK),)))
        else:
            for part in range(2):
                for first in range(0, depths[group], CHUNK):
                    chunks.append((group, (part, pl.ds(first, CHUNK))))

    def rows_of(chunk, half):
        group, place_in = chunk
        ref = made[group]
        if paired[group]:
            return ref.at[half, :, place_in[0], :, place_in[1]]
        return ref.at[half, :, :, place_in[0]]

    def result_of(chunk, owner):
        group, place_in = chunk
        if paired[group]:
            return out[group].at[owner, place_in[0], place_in[1]]
        return out[group].at[owner, place_in[0]]

    block_copies = []
    for distance in range(1, count):
        block_copies.append(
            begin(
                remote(
                    blocks.at[lax.rem(place + distance, count)],
                    rows.at[place],
                    block_send.at[distance - 1],
                    block_recv.at[distance - 1],
                    partners[distance - 1],
                )
            )
        )
    own_block = pltpu.make_async_copy(blocks.at[place], rows.at[place], block_sem.at[0])
    own_block.start()
    tiny = begin(remote(small, small_core, tiny_send.at[0], tiny_recv.at[0], core))
    state = {}
    outs = []

    def enter(index):
        chunk = chunks[index]
        copy = pltpu.make_async_copy(
            rows_of(chunk, 0), near_buf.at[index % 3], near_sem.at[index]
        )
        copy.start()
        state["near", index] = copy
        state["core", index] = begin(
            remote(
                rows_of(chunk, 1),
                sums.at[index],
                core_send.at[index],
                core_recv.at[index],
                core,
            )
        )

    def first_sum(index):
        state["near", index].wait()
        state["core", index].wait_recv()
        upper = pl.ds(count // 2, count // 2)
        total = wide(near_buf[index % 3, upper]) + wide(sums[index, upper])
        sums[index, upper] = total.astype(jnp.bfloat16)
        state["side", index] = begin(
            remote(
                sums.at[index, upper],
                side_in.at[index],
                side_send.at[index],
                side_recv.at[index],
                side,
            )
        )

    def second_sum(index):
        state["side", index].wait_recv()
        lower = pl.ds(0, count // 2)
        total = wide(near_buf[index % 3, lower]) + wide(sums[index, lower]) + wide(side_in[index])
        sums[index, lower] = total.astype(jnp.bfloat16)
        for distance in range(1, count):
            state["ring", index, distance] = begin(
                remote(
                    sums.at[index, distance // 2, distance % 2],
                    ring_in.at[index, distance - 1],
                    ring_send.at[index, distance - 1],
                    ring_recv.at[index, distance - 1],
                    partners[count - distance - 1],
                )
            )

    def third_sum(index):
        total = wide(sums[index, 0, 0])
        for distance in range(1, count):
            state["ring", index, distance].wait_recv()
            total = total + wide(ring_in[index, distance - 1])
        pair[index, 0] = total.astype(jnp.bfloat16)
        state["pair", index] = begin(
            remote(
                pair.at[index, 0],
                pair.at[index, 1],
                pair_send.at[index],
                pair_recv.at[index],
                side,
            )
        )

    def spread_pair(index):
        state["pair", index].wait_recv()
        state["last", index] = begin(
            remote(pair.at[index], other.at[index], last_send.at[index], last_recv.at[index], core)
        )

    def leave(index):
        state["last", index].wait_recv()
        chunk = chunks[index]
        found = (pair.at[index, 0], pair.at[index, 1], other.at[index, 0], other.at[index, 1])
        for bits in range(4):
            copy = pltpu.make_async_copy(
                found[bits], result_of(chunk, units[bits]), out_sem.at[index, bits]
            )
            copy.start()
            outs.append(copy)

    stages = (enter, first_sum, second_sum, third_sum, spread_pair, leave)
    for tick in range(len(chunks) + len(stages) - 1):
        for number, stage in enumerate(stages):
            if 0 <= tick - number < len(chunks):
                stage(tick - number)
        if tick == 2:
            tiny.wait_recv()
            small_core[...] += small[...]
            tiny = begin(remote(small_core, small_side, tiny_send.at[1], tiny_recv.at[1], side))
        if tick == 4:
            tiny.wait_recv()
            small_side[...] += small_core[...]
            tiny = [
                begin(
                    remote(
                        small_side,
                        small_far.at[distance - 1],
                        tiny_send.at[1 + distance],
                        tiny_recv.at[1 + distance],
                        partners[distance - 1],
                    )
                )
                for distance in range(1, count)
            ]
        if tick == 6:
            total = small_side[...]
            for distance in range(1, count):
                tiny[distance - 1].wait_recv()
                total = total + small_far[distance - 1]
            small_out[...] = total
    for copy in block_copies:
        copy.wait_recv()
    own_block.wait()
    for copy in outs:
        copy.wait()
    for copy in sends:
        copy.wait_send()


def reduce_all(blocks, small, made, paired):
    count = lax.axis_size("tensor")
    units = lax.axis_size("dp")
    groups = len(paired)
    anywhere = pl.BlockSpec(memory_space=pl.ANY)
    vmem = pl.BlockSpec(memory_space=pltpu.VMEM)
    width = blocks.shape[-1]
    depths = [array.shape[-2] for array in made]
    total = sum(depth * (2 if double else 1) for depth, double in zip(depths, paired)) // CHUNK
    results = []
    for array, double in zip(made, paired):
        shape = (units,) + ((2,) if double else ()) + array.shape[-2:]
        results.append(jax.ShapeDtypeStruct(shape, array.dtype))
    dma = pltpu.SemaphoreType.DMA
    bf16 = jnp.bfloat16
    found = pl.pallas_call(
        functools.partial(reduce_kernel, paired, depths),
        in_specs=[anywhere, vmem] + [anywhere] * groups,
        out_specs=[anywhere, vmem] + [anywhere] * groups,
        out_shape=[
            jax.ShapeDtypeStruct(blocks.shape, blocks.dtype),
            jax.ShapeDtypeStruct(small.shape, small.dtype),
        ]
        + results,
        scratch_shapes=[
            pltpu.VMEM((3, count, 2, CHUNK, width), bf16),
            pltpu.VMEM((total, count, 2, CHUNK, width), bf16),
            pltpu.VMEM((total, count // 2, 2, CHUNK, width), bf16),
            pltpu.VMEM((total, count - 1, CHUNK, width), bf16),
            pltpu.VMEM((total, 2, CHUNK, width), bf16),
            pltpu.VMEM((total, 2, CHUNK, width), bf16),
            pltpu.VMEM(small.shape, small.dtype),
            pltpu.VMEM(small.shape, small.dtype),
            pltpu.VMEM((count - 1,) + small.shape, small.dtype),
            dma((total,)),
            dma((total,)),
            dma((total,)),
            dma((total,)),
            dma((total,)),
            dma((total, count - 1)),
            dma((total, count - 1)),
            dma((total,)),
            dma((total,)),
            dma((total,)),
            dma((total,)),
            dma((total, 4)),
            dma((1,)),
            dma((count - 1,)),
            dma((count - 1,)),
            dma((count + 1,)),
            dma((count + 1,)),
        ],
        compiler_params=pltpu.CompilerParams(
            collective_id=1, has_side_effects=True, vmem_limit_bytes=56 * 1024 * 1024
        ),
    )(blocks, small, *made)
    return (found[0], found[1], found[2:])


def project_norm_kernel(parts, alpha_ref, *refs):
    lefts, weights = (refs[:parts], refs[parts : 2 * parts])
    wide_ref, gain_ref, shift_ref, made_ref, low_ref, norm_ref, factor_ref = refs[2 * parts :]
    total = alpha_ref[0] * wide(wide_ref[...])
    for left, weight in zip(lefts, weights):
        total = total + rows_nn(left[...], weight[...])
    made, normed, factor = layer_norm(total, gain_ref[...], shift_ref[...])
    made_ref[...] = made
    low_ref[...] = low(made)
    norm_ref[...] = normed
    factor_ref[...] = factor


def project_norm(alpha, lefts, weight_rows, rows_wide, gain, shift):
    slots, width = rows_wide.shape
    parts = len(lefts)
    depth = lefts[0].shape[1]

    def rows(columns):
        return pl.BlockSpec((ROWS, columns), lambda step: (step, 0))

    def part_spec(part):
        return pl.BlockSpec((depth, width), lambda step: (part, 0))

    return pl.pallas_call(
        functools.partial(project_norm_kernel, parts),
        grid=(slots // ROWS,),
        in_specs=[pl.BlockSpec(memory_space=pltpu.SMEM)]
        + [rows(depth)] * parts
        + [part_spec(part) for part in range(parts)]
        + [rows(width), whole_spec((1, width)), whole_spec((1, width))],
        out_specs=[rows(width), rows(width), rows(width), rows(1)],
        out_shape=[
            jax.ShapeDtypeStruct((slots, width), F32),
            jax.ShapeDtypeStruct((slots, width), BF16),
            jax.ShapeDtypeStruct((slots, width), F32),
            jax.ShapeDtypeStruct((slots, 1), F32),
        ],
        compiler_params=pltpu.CompilerParams(
            dimension_semantics=("arbitrary",), vmem_limit_bytes=32 * 1024 * 1024
        ),
        cost_estimate=pl.CostEstimate(
            flops=2 * slots * width * depth * parts,
            bytes_accessed=16 * slots * width,
            transcendentals=slots,
        ),
    )(alpha, *lefts, *([weight_rows] * parts), rows_wide, gain, shift)


def project_add_kernel(alpha_ref, left_ref, weight_ref, wide_ref, made_ref):
    made_ref[...] = low(
        alpha_ref[0] * wide(wide_ref[...]) + rows_nn(left_ref[...], weight_ref[...])
    )


def project_add(alpha, left, weight_rows, rows_wide):
    slots, width = rows_wide.shape
    depth = left.shape[1]

    def rows(columns):
        return pl.BlockSpec((ROWS, columns), lambda step: (step, 0))

    return pl.pallas_call(
        project_add_kernel,
        grid=(slots // ROWS,),
        in_specs=[
            pl.BlockSpec(memory_space=pltpu.SMEM),
            rows(depth),
            whole_spec((depth, width)),
            rows(width),
        ],
        out_specs=rows(width),
        out_shape=jax.ShapeDtypeStruct((slots, width), BF16),
        compiler_params=pltpu.CompilerParams(
            dimension_semantics=("arbitrary",), vmem_limit_bytes=40 * 1024 * 1024
        ),
        cost_estimate=pl.CostEstimate(
            flops=2 * slots * width * depth,
            bytes_accessed=6 * slots * width + 2 * depth * (slots + width),
            transcendentals=0,
        ),
    )(alpha, left, weight_rows, rows_wide)


def finish_kernel(*refs):
    half = (len(refs) - 5) // 2
    small_ref, gain_ref, shift_ref, down_ref, in_ref = (refs[half],) + refs[2 * half + 1 :]
    rows_in_all = lax.axis_size("tensor")

    @pl.when(pl.program_id(0) == 0)
    def _():
        gain_ref[...] = small_ref[0:3]
        shift_ref[...] = small_ref[3:6]
        down_ref[...] = small_ref[6:7]
        candidates = small_ref[7 : 7 + rows_in_all]
        row = lax.broadcasted_iota(jnp.int32, candidates.shape, 0)
        mine = jnp.where(row == lax.axis_index("tensor"), candidates, 0.0)
        in_ref[...] = jnp.sum(mine, axis=0, keepdims=True)

    for source, made in zip(refs[:half], refs[half + 1 : 2 * half + 1]):
        value = wide(source[...])
        if source.shape != made.shape:
            value = jnp.transpose(value)
        made[...] = value


def finish(arrays, turned, small):
    steps = 4
    width = small.shape[1]
    in_specs, out_specs, out_shape = ([], [], [])
    for array, turn in zip(arrays, turned):
        rows, width = array.shape
        if turn:
            in_specs.append(pl.BlockSpec((rows, width // steps), lambda step: (0, step)))
            out_specs.append(pl.BlockSpec((width // steps, rows), lambda step: (step, 0)))
            out_shape.append(jax.ShapeDtypeStruct((width, rows), F32))
        else:
            spec = pl.BlockSpec((rows // steps, width), lambda step: (step, 0))
            in_specs.append(spec)
            out_specs.append(spec)
            out_shape.append(jax.ShapeDtypeStruct((rows, width), F32))
    for rows in (3, 3, 1, 1):
        out_specs.append(whole_spec((rows, width)))
        out_shape.append(jax.ShapeDtypeStruct((rows, width), F32))
    return pl.pallas_call(
        finish_kernel,
        grid=(steps,),
        in_specs=in_specs + [whole_spec(small.shape)],
        out_specs=out_specs,
        out_shape=out_shape,
        compiler_params=pltpu.CompilerParams(
            dimension_semantics=("arbitrary",), vmem_limit_bytes=48 * 1024 * 1024
        ),
    )(*arrays, small)


def after(value, *earlier):
    return lax.optimization_barrier((value, earlier))[0]


def sequence_body(
    inputs,
    lengths,
    cotangent,
    qkv_weight,
    attn_out_weight,
    cross_weight,
    ffn_in_weight,
    ffn_in_bias,
    ffn_out_weight,
    ffn_out_bias,
    norm_gain,
    norm_bias,
):
    section = lax.axis_index("section")
    tensor_index = lax.axis_index("tensor")
    tensor_count = lax.axis_size("tensor")
    unit = lax.axis_index("dp")
    units = lax.axis_size("dp")
    decoder = section == 1
    alpha = jnp.where(decoder, ALPHA_DEC, ALPHA_ENC).astype(jnp.float32)
    alpha_row = alpha.reshape(1)
    batches, shard_rows, width = (inputs.shape[1], inputs.shape[2], inputs.shape[3])
    slots = batches * shard_rows
    gains = norm_gain[0].astype(jnp.float32)
    shifts = norm_bias[0].astype(jnp.float32)
    down_shift = ffn_out_bias.astype(jnp.float32)

    def unit_of(array, axis, bits):
        size = array.shape[axis] // units
        piece = lax.dynamic_slice_in_dim(array, (unit ^ bits) * size, size, axis)
        return piece.T if axis == 1 else piece

    bias_size = ffn_in_bias.shape[1] // units

    def units_of(bits):
        return (
            unit_of(qkv_weight[0], 1, bits),
            unit_of(attn_out_weight[0], 0, bits),
            unit_of(ffn_in_weight[0], 1, bits),
            unit_of(ffn_out_weight[0], 0, bits),
            unit_of(cross_weight[0], 1, bits).reshape(2, HS, width),
            jnp.broadcast_to(unit_of(ffn_in_bias[0], 0, bits)[None], (16, bias_size)),
        )

    x, filled = gather_all(
        inputs[0], units_of(0), units_of(2), (False, False, False, False, True, False)
    )
    x = x.reshape(slots, width)
    qkv_rows, out_rows, in_rows, down_rows, cross_rows = [
        array.reshape(-1, width) for array in filled[:5]
    ]
    in_shift = filled[5][:, :, :, 0].reshape(1, -1).astype(jnp.float32)
    cross_parts = cross_rows.reshape(-1, 2, LANES, width)
    half = width // 2

    source_len = lax.dynamic_index_in_dim(lengths[0, :, 0], tensor_index, 0, keepdims=False)
    target_len = lax.dynamic_index_in_dim(lengths[1, :, 0], tensor_index, 0, keepdims=False)
    own_len = jnp.where(decoder, target_len, source_len)
    self_scalars = jnp.stack([own_len, decoder.astype(jnp.int32)])
    cross_scalars = jnp.stack([source_len, jnp.zeros_like(source_len)])
    no_limit = jnp.full((1,), 1 << 20, jnp.int32)
    pairs = width // LANES
    sides = (0, 1)

    qkv = low(rows_nt(x, qkv_rows))
    mixed, lse_self = self_attention(self_scalars, qkv, 0, pairs)
    resid_a, a_low, norm_a, factor_a = project_norm(
        alpha_row, [mixed], out_rows, x, gains[0:1], shifts[0:1]
    )

    def zeros_like_of(branch):
        shapes = jax.eval_shape(branch)
        return lambda: jax.tree.map(lambda leaf: jnp.zeros(leaf.shape, leaf.dtype), shapes)

    def dec_query():
        first = cross_parts[:, 0].reshape(-1, width)
        return tuple(low(rows_nt(a_low, first[side * half : side * half + half])) for side in sides)

    query_sent = lax.cond(decoder, dec_query, zeros_like_of(dec_query))
    query_held = [lax.ppermute(piece, "section", [(1, 0)]) for piece in query_sent]
    cotangent_rows = exchange_in(1, 2, after(cotangent, query_held)).reshape(slots, width)

    def feed(rows_low, rows_wide):
        return feed_call(
            alpha_row,
            rows_low,
            rows_wide,
            in_rows,
            in_shift,
            down_rows,
            down_shift,
            gains[2:3],
            shifts[2:3],
        )

    def enc_feed():
        hidden, slopes, memory_low, norm_y, factor_y = feed(a_low, resid_a)
        key_values = low(rows_nt(memory_low, cross_rows))
        return (hidden, slopes, memory_low, norm_y, factor_y, key_values)

    hidden_e, slopes_e, memory_low, norm_e, factor_e, key_values = lax.cond(
        decoder, zeros_like_of(enc_feed), enc_feed
    )

    mixed_c, lse_c, mixed_held = ([], [], [])
    for side in sides:

        def enc_mix():
            return tuple(
                cross_attention(
                    cross_scalars, query_held[side], key_values, side * pairs // 2, pairs // 2
                )
            )

        mix_made, lse_made = lax.cond(decoder, zeros_like_of(enc_mix), enc_mix)
        mixed_c.append(mix_made)
        lse_c.append(lse_made)
        mixed_held.append(lax.ppermute(mix_made, "section", [(0, 1)]))

    def sharded(rows):
        return rows.reshape(batches, shard_rows, width)

    outputs_e = exchange_in(0, 3, after(sharded(memory_low), mixed_held))
    mixed_held = after(mixed_held, outputs_e)

    def dec_middle():
        cross_second = cross_parts[:, 1].reshape(-1, width)
        resid_c, c_low, norm_c, factor_c = project_norm(
            alpha_row, mixed_held, cross_second, resid_a, gains[1:2], shifts[1:2]
        )
        hidden, slopes, decoded_low, norm_y, factor_y = feed(c_low, resid_c)
        grad_y, grad_low, sums_y = norm_back_call(
            target_len.reshape(1), cotangent_rows, norm_y, factor_y, gains[2:3]
        )
        grad_pre, bias_sum, grad_c = feed_back_call(
            alpha_row, grad_low, grad_y, in_rows, down_rows, slopes
        )
        grad_mid, mid_low, sums_c = norm_back_call(
            no_limit, grad_c, norm_c, factor_c, gains[1:2]
        )
        grad_mixed_c = tuple(
            low(rows_nt(mid_low, cross_second[side * half : side * half + half]))
            for side in sides
        )
        return (
            decoded_low,
            hidden,
            c_low,
            grad_low,
            grad_pre,
            bias_sum,
            grad_mid,
            mid_low,
            grad_mixed_c,
            sums_y,
            sums_c,
        )

    (
        decoded_low,
        hidden_d,
        c_low,
        grad_low_d,
        grad_pre_d,
        bias_sum_d,
        grad_mid,
        mid_low,
        grad_mixed_c,
        sums_yd,
        sums_cd,
    ) = lax.cond(decoder, dec_middle, zeros_like_of(dec_middle))
    grad_mixed_held = [lax.ppermute(piece, "section", [(1, 0)]) for piece in grad_mixed_c]

    grad_query_held, grad_kv = ([], [])
    for side in sides:

        def enc_cross():
            return tuple(
                cross_attention_back(
                    cross_scalars,
                    query_held[side],
                    key_values,
                    mixed_c[side],
                    grad_mixed_held[side],
                    lse_c[side],
                    side * pairs // 2,
                    pairs // 2,
                )
            )

        query_made, kv_made = lax.cond(decoder, zeros_like_of(enc_cross), enc_cross)
        grad_kv.append(kv_made)
        grad_query_held.append(lax.ppermute(query_made, "section", [(0, 1)]))

    def enc_back():
        grad_memory = rows_nn(grad_kv[0], cross_rows[:width]) + rows_nn(
            grad_kv[1], cross_rows[width:]
        )
        grad_y, grad_low, sums_y = norm_back_call(
            no_limit, grad_memory, norm_e, factor_e, gains[2:3]
        )
        grad_pre, bias_sum, grad_a = feed_back_call(
            alpha_row, grad_low, grad_y, in_rows, down_rows, slopes_e
        )
        return (grad_low, grad_pre, bias_sum, grad_a, sums_y)

    grad_low_e, grad_pre_e, bias_sum_e, grad_a_e, sums_ye = lax.cond(
        decoder, zeros_like_of(enc_back), enc_back
    )

    outputs_d = exchange_in(1, 4, after(sharded(decoded_low), grad_mixed_held))
    grad_query_held = after(grad_query_held, outputs_d)
    outputs = jnp.where(decoder, outputs_d, outputs_e)

    grad_query_held = after(grad_query_held, grad_a_e)

    def enc_norm():
        made = [rows_tn(piece, memory_low) for piece in grad_kv]
        return tuple(norm_back_call(no_limit, grad_a_e, norm_a, factor_a, gains[0:1])) + (
            low(jnp.concatenate(made)),
        )

    def dec_norm():
        grad_query = jnp.concatenate(grad_query_held, axis=1)
        cross_first = cross_parts[:, 0].reshape(-1, width)
        grad_a = alpha * grad_mid + rows_nn(grad_query, cross_first)
        mixed_all = jnp.concatenate(mixed_held, axis=1)
        made = [rows_tn(grad_query, a_low), rows_tn(mixed_all, mid_low)]
        made = [piece.reshape(-1, 1, LANES, width) for piece in made]
        return tuple(norm_back_call(no_limit, grad_a, norm_a, factor_a, gains[0:1])) + (
            low(jnp.concatenate(made, axis=1)).reshape(-1, width),
        )

    grad_r, r_low, sums_a, cross_made = lax.cond(decoder, dec_norm, enc_norm)
    bias_sum = jnp.where(decoder, bias_sum_d, bias_sum_e)
    sums_y = jnp.where(decoder, sums_yd, sums_ye)

    def down_grads():
        return lax.cond(
            decoder,
            lambda: low(rows_tn(hidden_d, grad_low_d)),
            lambda: low(rows_tn(hidden_e, grad_low_e)),
        )

    def in_grads():
        return lax.cond(
            decoder,
            lambda: low(rows_tn(grad_pre_d, c_low)),
            lambda: low(rows_tn(grad_pre_e, a_low)),
        )

    grad_mixed = low(rows_nt(r_low, out_rows))
    grad_qkv = self_attention_back(self_scalars, qkv, mixed, grad_mixed, lse_self, 0, pairs)
    grad_x = project_add(alpha_row, grad_qkv, qkv_rows, grad_r)

    slot_bits = jnp.asarray([0, 2, 1, 3], jnp.int32)[:, None]
    slot_unit = unit ^ slot_bits
    slot_tensor = (tensor_index - lax.iota(jnp.int32, tensor_count)[None]) % tensor_count
    slot_index = (slot_tensor * units + slot_unit).reshape(-1)
    hot = (slot_index[None, :] == lax.iota(jnp.int32, slot_index.shape[0])[:, None]).astype(
        jnp.float32
    )
    shift_abs = jnp.dot(
        hot, bias_sum.reshape(-1, bias_size), precision=lax.Precision.HIGHEST
    ).reshape(-1, width)
    small = jnp.concatenate(
        [
            sums_a[0:1],
            sums_cd[0:1],
            sums_y[0:1],
            sums_a[1:2],
            sums_cd[1:2],
            sums_y[1:3],
            shift_abs,
        ]
    )
    small = jnp.pad(small, ((0, -small.shape[0] % 8), (0, 0)))
    made = (
        low(rows_tn(grad_qkv, x)),
        low(rows_tn(mixed, r_low)),
        in_grads(),
        down_grads(),
        cross_made,
    )
    input_rows, small, grads = reduce_all(
        sharded(grad_x),
        small,
        [array.reshape(like.shape) for array, like in zip(made, filled)],
        (False, False, False, False, True),
    )
    finished = finish(
        [array.reshape(-1, width) for array in list(grads) + [input_rows]],
        (True, False, True, False, True, False),
        small,
    )
    qkv_grad, out_grad, in_grad, down_grad, cross_grad, input_grad = finished[:6]
    gain_grad, shift_grad, down_shift_grad, in_shift_grad = finished[6:]

    return (
        outputs[None],
        sharded(input_grad)[None],
        qkv_grad[None],
        out_grad[None],
        cross_grad[None],
        in_grad[None],
        in_shift_grad,
        down_grad[None],
        down_shift_grad,
        gain_grad[None],
        shift_grad[None],
    )


def solution(mesh):
    placed = (
        P("section", None, ("dp", "tensor"), None),
        P(None, None, "dp"),
        P(None, ("dp", "tensor"), None),
        P("section", None, "tensor"),
        P("section", "tensor", None),
        P("section", None, "tensor"),
        P("section", None, "tensor"),
        P("section", "tensor"),
        P("section", "tensor", None),
        P("section", None),
        P("section", None, None),
        P("section", None, None),
    )
    returned = (
        P("section", None, ("dp", "tensor"), None),
        P("section", None, ("dp", "tensor"), None),
        P("section", None, "tensor"),
        P("section", "tensor", None),
        P("section", None, "tensor"),
        P("section", None, "tensor"),
        P("section", "tensor"),
        P("section", "tensor", None),
        P("section", None),
        P("section", None, None),
        P("section", None, None),
    )
    sizes = dict(mesh.shape)

    def whole(*arrays):
        batches, sequences = arrays[1].shape[1:]
        heads = arrays[3].shape[2] // (3 * HS)
        group = sizes["dp"] * sizes["tensor"]
        one_each = batches == sizes["tensor"] and sizes["dp"] == 4 and sequences == sizes["dp"] and heads % group == 0
        chosen = sequence_body if one_each else body
        return jax.shard_map(
            chosen, mesh=mesh, in_specs=placed, out_specs=returned, check_vma=False
        )(*arrays)

    return whole
```
